256 devices in a mesh: lon: 16 (over z, core), lat: 8 (over x_hi, y), lev: 2 (over x_lo).
Axes of the slice: x: 4 (x_hi: 2, x_lo: 2; x = x_hi * 2 + x_lo), y: 4, z: 8, core: 2. Of those that a mesh axis runs over, the one named last changes fastest.
Arguments:
- inputs: float32 [4, 48, 192, 192], P('lev', 'lat', 'lon'), may hold values from -6 to 6
- cotangent: float32 [4, 48, 192, 192], P('lev', 'lat', 'lon'), may hold values from -6 to 6
- qkv_weight: float32 [2, 192, 576], replicated, may hold values from -0.4375 to 0.4375
- proj_weight: float32 [2, 192, 192], replicated, may hold values from -0.4375 to 0.4375
- up_weight: float32 [2, 192, 768], replicated, may hold values from -0.4375 to 0.4375
- down_weight: float32 [2, 768, 192], replicated, may hold values from -0.21875 to 0.21875
- bias_table: float32 [2, 2, 8, 6, 3312], P(None, 'lev', 'lat'), may hold values from -4 to 302
- lat_mask: int32 [48], replicated, may hold values 0 or 1
Outputs:
- grad_input: float32 [4, 48, 192, 192], P('lev', 'lat', 'lon')
- grad_qkv: float32 [2, 192, 576], P(None, 'lon')
- grad_proj: float32 [2, 192, 192], P(None, 'lon')
- grad_up: float32 [2, 192, 768], P(None, 'lon')
- grad_down: float32 [2, 768, 192], P(None, 'lon')
- grad_table: float32 [2, 2, 8, 6, 3312], P(None, 'lev', 'lat', None, 'lon')
The draws below stay inside these ranges and needn't reach their ends.
Inputs may be any that keep to these rules, and one draw needn't show every extreme that they name: `lat_mask`: 1 marks a latitude row holding data, 0 a padding row.
All inputs are finite; a program needn't handle non-finite values.
Results may differ from the reference program's by a relative error of at most 0.0003.
Values sent between devices are 32-bit elements; how exact they have to be, the bound alone decides.
No kernel may reach another device: no remote copies, remote signals or barrier semaphores. Data moves between devices by JAX's collectives and lax.ppermute only.
A program may use at most 128 MiB of HBM per device.

```python
import jax
import jax.numpy as jnp
from jax import lax

C = 192
HEADS = 6
HID = 768
WLEV = 2
WLAT = 6
WLON = 12
POS = 3312
NLEV = 4
NLAT = 48
NLON = 192
NLEVW = 2
NLATW = 8


def draw_bias_table(key, part):
    key = jax.random.fold_in(key, 7)
    noise_key = jax.random.fold_in(key, 0)
    full_shape = (2, NLEVW, NLATW, HEADS, WLEV, WLEV, WLAT, WLAT, 2 * WLON - 1)
    earth_table = jnp.clip(jax.random.normal(noise_key, full_shape, jnp.float32), -4.0, 4.0)
    return earth_table.reshape(2, NLEVW, NLATW, HEADS, POS)


def place_ends(drawn, own_key, smallest, high):
    index_at = [jax.random.randint(jax.random.fold_in(own_key, axis), (), 0, length) for axis, length in enumerate(drawn.shape)]
    widest = drawn.shape.index(max(drawn.shape))
    next_to = index_at[:widest] + [(index_at[widest] + 1) % drawn.shape[widest]] + index_at[widest + 1:]
    return drawn.at[tuple(index_at)].set(smallest).at[tuple(next_to)].set(high)


def block_levels(rng, shape, cuts, low, top_value):
    loudness, own = 1.0, jax.random.fold_in(rng, 6)
    for position, shards_of in cuts:
        steps = jnp.exp(jax.random.uniform(jax.random.fold_in(own, position), (shards_of,), jnp.float32, low / len(cuts), top_value / len(cuts)))
        loudness = loudness * jnp.repeat(steps, shape[position] // shards_of).reshape([-1 if axis == position else 1 for axis in range(len(shape))])
    return loudness


def centred(own_key, dims, scale, bound, cuts=(), held_as=jnp.bfloat16):
    values = scale * jax.random.normal(own_key, dims, jnp.float32)
    if cuts:
        values = values * block_levels(own_key, dims, cuts, -0.22, 0.18)
    return jnp.clip(values, -bound, bound).astype(held_as)


def setup_inputs(seed: int = 0) -> dict:
    seeds = jax.random.split(jax.random.key(seed), 9)
    inputs = centred(seeds[0], (NLEV, NLAT, NLON, C), 1.0, 6.0, ((0, 2), (1, 8), (2, 16)), jnp.float32)
    cotangent = centred(seeds[1], (NLEV, NLAT, NLON, C), 1.0, 6.0, ((0, 2), (1, 8), (2, 16)), jnp.float32)
    qkv_weight = centred(seeds[2], (2, C, 3 * C), C ** -0.5, 0.4375, (), jnp.float32)
    proj_weight = centred(seeds[3], (2, C, C), C ** -0.5, 0.4375, (), jnp.float32)
    up_weight = centred(seeds[4], (2, C, HID), C ** -0.5, 0.4375, (), jnp.float32)
    down_weight = centred(seeds[5], (2, HID, C), HID ** -0.5, 0.21875, (), jnp.float32)
    bias_table = draw_bias_table(jax.random.fold_in(seeds[8], 71), 0)
    lat_mask = place_ends((jax.random.randint(seeds[7], (NLAT,), 0, 16) < 15).astype(jnp.int32), jax.random.fold_in(seeds[7], 1), 0, 1)
    return {"inputs": inputs, "cotangent": cotangent, "qkv_weight": qkv_weight, "proj_weight": proj_weight, "up_weight": up_weight, "down_weight": down_weight, "bias_table": bias_table, "lat_mask": lat_mask}


NEGATIVE = -10000.0
HIGHEST = lax.Precision.HIGHEST

def to_windows(token_grid):
    levels, lat_rows, columns = token_grid.shape[:3]
    trailing = token_grid.shape[3:]
    split_grid = token_grid.reshape((levels // WLEV, WLEV, lat_rows // WLAT, WLAT, columns // WLON, WLON) + trailing)
    axes_order = (0, 2, 4, 1, 3, 5) + tuple(range(6, 6 + len(trailing)))
    return split_grid.transpose(axes_order).reshape((levels // WLEV, lat_rows // WLAT, columns // WLON, WLEV * WLAT * WLON) + trailing)

def from_windows(windows, levels, lat_rows, columns):
    trailing = windows.shape[4:]
    split_win = windows.reshape((levels // WLEV, lat_rows // WLAT, columns // WLON, WLEV, WLAT, WLON) + trailing)
    axes_order = (0, 3, 1, 4, 2, 5) + tuple(range(6, 6 + len(trailing)))
    return split_win.transpose(axes_order).reshape((levels, lat_rows, columns) + trailing)

def layer_norm(values):
    row_mean = lax.optimization_barrier(jnp.mean(values, axis=-1, keepdims=True))
    centered = values - row_mean
    row_var = lax.optimization_barrier(jnp.mean(centered * centered, axis=-1, keepdims=True))
    return centered * lax.rsqrt(row_var + 1e-05)

def earth_bias(earth_table):
    lev_windows, lat_windows = earth_table.shape[:2]
    lon_span = 2 * WLON - 1
    shaped = earth_table.reshape(lev_windows, lat_windows, HEADS, WLEV, WLEV, WLAT, WLAT, lon_span)
    offsets = jnp.arange(WLON)[None, :] - jnp.arange(WLON)[:, None] + WLON - 1
    one_hot = (offsets[:, :, None] == jnp.arange(lon_span)[None, None, :]).astype(jnp.float32)
    earth_terms = jnp.einsum('abhlmpqr,xyr->abhlpxmqy', shaped, one_hot, precision=HIGHEST)
    tokens_win = WLEV * WLAT * WLON
    return earth_terms.reshape(lev_windows, lat_windows, HEADS, tokens_win, tokens_win)

def frame_masks(valid_rows, level_region, row_region, levels, columns):
    lat_rows = valid_rows.shape[0]
    valid_grid = jnp.broadcast_to(valid_rows[None, :, None], (levels, lat_rows, columns))
    key_bias = to_windows(NEGATIVE * (1.0 - valid_grid)).astype(jnp.float32)
    region = level_region[:, None] * 2 + row_region[None, :]
    region = to_windows(jnp.broadcast_to(region[:, :, None], (levels, lat_rows, columns)))
    pair_bias = jnp.where(region[..., :, None] == region[..., None, :], 0.0, NEGATIVE).astype(jnp.float32)
    return (key_bias, pair_bias)

def window_block(token_grid, qkv_weight, proj_weight, up_weight, down_weight, earth_table, key_bias, pair_bias):
    levels, lat_rows, columns, channels = token_grid.shape
    head_size = channels // HEADS
    normed = to_windows(layer_norm(token_grid))
    packed = jnp.einsum('abcnd,de->abcne', normed, qkv_weight, precision=HIGHEST)
    packed = packed.reshape(packed.shape[:4] + (3, HEADS, head_size))
    queries = packed[..., 0, :, :]
    key_heads = packed[..., 1, :, :]
    values = packed[..., 2, :, :]
    scores = jnp.einsum('abcnhe,abcmhe->abchnm', queries, key_heads, precision=HIGHEST) * head_size ** (-0.5)
    scores = scores + earth_bias(earth_table)[:, :, None] + key_bias[:, :, :, None, None, :] + pair_bias[:, :, :, None]
    attention = jax.nn.softmax(scores, axis=-1)
    attended = jnp.einsum('abchnm,abcmhe->abcnhe', attention, values, precision=HIGHEST)
    attended = attended.reshape(attended.shape[:4] + (channels,))
    projected = jnp.einsum('abcnd,de->abcne', attended, proj_weight, precision=HIGHEST)
    middle = token_grid + from_windows(projected, levels, lat_rows, columns)
    hidden = jax.nn.gelu(jnp.einsum('lrcd,de->lrce', layer_norm(middle), up_weight, precision=HIGHEST), approximate=False)
    return middle + jnp.einsum('lrce,ed->lrcd', hidden, down_weight, precision=HIGHEST)

def reference(inputs, cotangent, qkv_weight, proj_weight, up_weight, down_weight, bias_table, lat_mask):
    valid_rows = lat_mask.astype(jnp.float32)
    shift_lev, shift_lat, shift_lon = (WLEV // 2, WLAT // 2, WLON // 2)
    plain_key, plain_pair = frame_masks(valid_rows, jnp.zeros((NLEV,), jnp.int32), jnp.zeros((NLAT,), jnp.int32), NLEV, WLON)
    level_region = (jnp.arange(NLEV) >= NLEV - shift_lev).astype(jnp.int32)
    row_region = (jnp.arange(NLAT) >= NLAT - shift_lat).astype(jnp.int32)
    shift_key, shift_pair = frame_masks(jnp.roll(valid_rows, -shift_lat), level_region, row_region, NLEV, WLON)
    params_first = (qkv_weight[0], proj_weight[0], up_weight[0], down_weight[0], bias_table[0])
    params_second = (qkv_weight[1], proj_weight[1], up_weight[1], down_weight[1], bias_table[1])

    def columns_of(token_grid):
        return token_grid.reshape(NLEV, NLAT, NLON // WLON, WLON, token_grid.shape[-1]).transpose(2, 0, 1, 3, 4)

    def grid_of(stacked):
        return stacked.transpose(1, 2, 0, 3, 4).reshape(NLEV, NLAT, NLON, stacked.shape[-1])

    def forward_first(column):
        return window_block(column, *params_first, plain_key, plain_pair)

    def backward_with(params, key_bias, pair_bias):

        def column_grads(column_pair):

            def apply_block(token_grid, *weights):
                return window_block(token_grid, *weights, key_bias, pair_bias)
            _, pullback = jax.vjp(apply_block, column_pair[0], *params)
            return pullback(column_pair[1])
        return column_grads
    first_out = grid_of(lax.map(forward_first, columns_of(inputs)))
    shifts = (-shift_lev, -shift_lat, -shift_lon)
    framed = jnp.roll(first_out, shifts, axis=(0, 1, 2))
    framed_cot = jnp.roll(cotangent, shifts, axis=(0, 1, 2))
    grads_second = lax.map(backward_with(params_second, shift_key, shift_pair), (columns_of(framed), columns_of(framed_cot)))
    back_grad = jnp.roll(grid_of(grads_second[0]), (shift_lev, shift_lat, shift_lon), axis=(0, 1, 2))
    grads_first = lax.map(backward_with(params_first, plain_key, plain_pair), (columns_of(inputs), columns_of(back_grad)))
    grad_scale = (NLEV * NLAT * NLON) ** (-0.5)
    grad_input = grid_of(grads_first[0])
    grad_qkv = jnp.stack([lax.optimization_barrier(jnp.sum(grads_first[1], axis=0)), lax.optimization_barrier(jnp.sum(grads_second[1], axis=0))]) * grad_scale
    grad_proj = jnp.stack([lax.optimization_barrier(jnp.sum(grads_first[2], axis=0)), lax.optimization_barrier(jnp.sum(grads_second[2], axis=0))]) * grad_scale
    grad_up = jnp.stack([lax.optimization_barrier(jnp.sum(grads_first[3], axis=0)), lax.optimization_barrier(jnp.sum(grads_second[3], axis=0))]) * grad_scale
    grad_down = jnp.stack([lax.optimization_barrier(jnp.sum(grads_first[4], axis=0)), lax.optimization_barrier(jnp.sum(grads_second[4], axis=0))]) * grad_scale
    grad_table = jnp.stack([lax.optimization_barrier(jnp.sum(grads_first[5], axis=0)), lax.optimization_barrier(jnp.sum(grads_second[5], axis=0))])
    return (grad_input, grad_qkv, grad_proj, grad_up, grad_down, grad_table)
```

```python
import jax
import jax.numpy as jnp
import numpy as np
from jax import lax
from jax.experimental import pallas as pl
from jax.experimental.pallas import tpu as pltpu
from jax.sharding import PartitionSpec as P

F32 = jnp.float32
BF16 = jnp.bfloat16

HEADS = 6
HEAD = 32
CH = 192
HID = 768
LEVS = 2
ROWS = 6
COLS = 12
CELLS = LEVS * ROWS
TOK = CELLS * COLS
STACK = HEADS * TOK
SPAN = 2 * COLS - 1
POS = 3312
CHUNK = ROWS * SPAN
UPLANES = 384
NEGATIVE = -10000.0
SCALE = HEAD ** (-0.5)

NZ = 8
SHARE = 12
GROUPS = 3
GROWS = NZ * GROUPS * SHARE
TROWS = 24
BUF = GROWS + TROWS
TSHARE = POS // 16
PLANE = 16
UNIT = 27

NN = ((1,), (0,))
NT = ((1,), (1,))
TN = ((0,), (0,))


def params(mib=28):
    return pltpu.CompilerParams(vmem_limit_bytes=mib * 1024 * 1024)


def halves(v):
    top = v.astype(BF16)
    return top, (v - top.astype(F32)).astype(BF16)


def thirds(v):
    top = v.astype(BF16)
    rest = v - top.astype(F32)
    mid = rest.astype(BF16)
    return top, mid, (rest - mid.astype(F32)).astype(BF16)


def dot(a, b, dims):
    return lax.dot_general(a, b, (dims, ((), ())), preferred_element_type=F32)


def dot3(a, b, dims):
    return dot(a[0], b[0], dims) + (dot(a[0], b[1], dims) + dot(a[1], b[0], dims))


def exact_dot(v, one_hot, dims):
    a, b, c = thirds(v)
    return (dot(a, one_hot, dims) + dot(b, one_hot, dims)) + dot(c, one_hot, dims)


def norm(v):
    centered = v - jnp.mean(v, axis=-1, keepdims=True)
    inv = lax.rsqrt(jnp.mean(centered * centered, axis=-1, keepdims=True) + 1e-05)
    return centered * inv, inv


def norm_back(d, normed, inv):
    return inv * (
        d
        - jnp.mean(d, axis=-1, keepdims=True)
        - normed * jnp.mean(d * normed, axis=-1, keepdims=True)
    )


ERF_TOP = (
    0.00022905065861350646,
    0.0034082910107109506,
    0.050955695062380861,
    0.18520832239976145,
    1.128379143519084,
)
ERF_LOW = (
    -1.1791602954361697e-7,
    0.000023547966471313185,
    0.0010179625278914885,
    0.014070470171167667,
    0.11098505178285362,
    0.49746925110067538,
    1.0,
)


def erf(v):
    v = jnp.clip(v, -3.832506856900711, 3.832506856900711)
    sq = v * v
    top = jnp.full_like(v, ERF_TOP[0])
    for term in ERF_TOP[1:]:
        top = top * sq + term
    low = jnp.full_like(v, ERF_LOW[0])
    for term in ERF_LOW[1:]:
        low = low * sq + term
    return v * top / low


def half_cdf(pre):
    return 0.5 + 0.5 * erf(pre * (0.5**0.5))


def head_rows(dtype):
    lane = lax.broadcasted_iota(jnp.int32, (1, CH), 1)
    return [
        jnp.where((lane >= h * HEAD) & (lane < (h + 1) * HEAD), 1.0, 0.0).astype(dtype)
        for h in range(HEADS)
    ]


def stack_heads(pair):
    rows = head_rows(BF16)
    return tuple(jnp.concatenate([part * rows[h] for h in range(HEADS)], axis=0) for part in pair)


def merge_heads(stacked):
    rows = head_rows(F32)
    total = stacked[0:TOK] * rows[0]
    for h in range(1, HEADS):
        total = total + stacked[h * TOK : (h + 1) * TOK] * rows[h]
    return total


def place_matrix():
    mat = np.zeros((UPLANES, UPLANES), np.float32)
    for kl in range(LEVS):
        for kr in range(ROWS):
            for p in range(SPAN):
                mat[kl * CHUNK + kr * SPAN + p, p * CELLS + kl * ROWS + kr] = 1.0
    return jnp.asarray(mat, BF16)


def chunk_start(ql, kl, qr):
    return ((ql * LEVS + kl) * ROWS + qr) * CHUNK


def expand_bias(table_ref, place_ref, flat_ref, up_ref, bias_ref):
    flat_ref[...] = jnp.zeros_like(flat_ref)
    flat_ref[0:HEADS, 0:POS] = table_ref[...].reshape(HEADS, POS)
    lane = lax.broadcasted_iota(jnp.int32, (8, UPLANES), 1)
    for ql in range(LEVS):
        for qr in range(ROWS):
            g = ql * ROWS + qr
            row = jnp.zeros((8, UPLANES), F32)
            for kl in range(LEVS):
                start = chunk_start(ql, kl, qr)
                base = start // 128 * 128
                window = flat_ref[:, base : base + UPLANES]
                turn = (kl * CHUNK - (start - base)) % UPLANES
                if turn:
                    window = pltpu.roll(window, turn, 1)
                row = jnp.where((lane >= kl * CHUNK) & (lane < (kl + 1) * CHUNK), window, row)
            up_ref[g * 8 : (g + 1) * 8, :] = row
    ups = exact_dot(up_ref[...], place_ref[...], NN)
    for h in range(HEADS):
        rows = jnp.concatenate([ups[g * 8 + h : g * 8 + h + 1] for g in range(CELLS)], axis=0)
        for qc in range(COLS):
            turn = (-(COLS - 1 - qc) * CELLS) % UPLANES
            moved = pltpu.roll(rows, turn, 1) if turn else rows
            bias_ref[h * TOK + qc * CELLS : h * TOK + (qc + 1) * CELLS, :] = moved[:, 0:TOK]


def collect_table(dscore_ref, place_ref, up_ref, flat_ref):
    up_ref[...] = jnp.zeros_like(up_ref)
    for h in range(HEADS):
        total = jnp.zeros((CELLS, UPLANES), F32)
        for qc in range(COLS):
            block = dscore_ref[h * TOK + qc * CELLS : h * TOK + (qc + 1) * CELLS, :]
            block = jnp.concatenate([block, jnp.zeros((CELLS, UPLANES - TOK), F32)], axis=1)
            turn = (COLS - 1 - qc) * CELLS
            total = total + (pltpu.roll(block, turn, 1) if turn else block)
        for g in range(CELLS):
            up_ref[g * 8 + h : g * 8 + h + 1, :] = total[g : g + 1]
    raw = exact_dot(up_ref[...], place_ref[...], NT)
    flat_ref[...] = jnp.zeros_like(flat_ref)
    lane = lax.broadcasted_iota(jnp.int32, (8, UPLANES), 1)
    for ql in range(LEVS):
        for qr in range(ROWS):
            g = ql * ROWS + qr
            row = raw[g * 8 : (g + 1) * 8]
            for kl in range(LEVS):
                start = chunk_start(ql, kl, qr)
                base = start // 128 * 128
                shift = start - base
                turn = (shift - kl * CHUNK) % UPLANES
                moved = pltpu.roll(row, turn, 1) if turn else row
                keep = (lane >= shift) & (lane < shift + CHUNK)
                window = flat_ref[:, base : base + UPLANES]
                flat_ref[:, base : base + UPLANES] = jnp.where(keep, moved, window)


def window_masks(mask_ref, second):
    lev = lax.axis_index("lev")
    lat = lax.axis_index("lat")
    last_lev = lev == lax.axis_size("lev") - 1
    last_lat = lat == lax.axis_size("lat") - 1
    key_col = lax.broadcasted_iota(jnp.int32, (1, TOK), 1)
    key_row = lax.rem(key_col, ROWS)
    key_bias = jnp.zeros((1, TOK), F32)
    count = ROWS * lax.axis_size("lat")
    for r in range(ROWS):
        place = lat * ROWS + r
        if second:
            place = lax.rem(place + ROWS // 2, count)
        value = NEGATIVE * (1.0 - mask_ref[place].astype(F32))
        key_bias = jnp.where(key_row == r, value, key_bias)
    if not second:
        return key_bias, None

    def label(tokens):
        level = jnp.where(lax.rem(tokens, CELLS) >= ROWS, 2, 0)
        row = jnp.where(lax.rem(tokens, ROWS) >= ROWS // 2, 1, 0)
        return level * last_lev.astype(jnp.int32) + row * last_lat.astype(jnp.int32)

    query = label(lax.broadcasted_iota(jnp.int32, (TOK, 1), 0))
    pair = jnp.where(query == label(key_col), 0.0, NEGATIVE).astype(F32)
    return key_bias, pair


def add_masks(scores, key_bias, pair):
    scores = scores + key_bias
    if pair is None:
        return scores
    return jnp.concatenate([scores[h * TOK : (h + 1) * TOK] + pair for h in range(HEADS)], axis=0)


def scaled_parts(qkv):
    return qkv[:, 0:CH] * SCALE, qkv[:, CH : 2 * CH], qkv[:, 2 * CH : 3 * CH]


def forward_attention(x, wq, bias, key_bias, pair):
    normed, inv = norm(x)
    qkv = dot3(halves(normed), halves(wq), NN)
    q, k, v = scaled_parts(qkv)
    scores = dot3(stack_heads(halves(q)), halves(k), NT) + bias
    scores = add_masks(scores, key_bias, pair)
    grown = jnp.exp(scores - jnp.max(scores, axis=-1, keepdims=True))
    weights = grown * (1.0 / jnp.sum(grown, axis=-1, keepdims=True))
    attended = merge_heads(dot3(halves(weights), halves(v), NN))
    return normed, inv, qkv, weights, attended


OCTANT = 24


def octants():
    for j in range(2):
        for k in range(2):
            for rr in range(ROWS // 2):
                yield j, k, rr


def spread_octants(scratch, out_ref, slot, lev):
    for j, k, rr in octants():
        start = k * (COLS // 2) * CELLS + lev * ROWS + j * (ROWS // 2) + rr
        rows = slice(rr * 8, rr * 8 + COLS // 2)
        from_rows = pl.ds(start, COLS // 2, stride=CELLS)
        out_ref[j, k, slot, rows, 0:128] = scratch[0, from_rows, :]
        out_ref[j, k, slot, rows, 128:CH] = scratch[1, from_rows, :][:, 0 : CH - 128]


def store_wide(scratch, rows, value):
    scratch[0, rows, :] = value[:, 0:128]
    scratch[1, rows, :] = jnp.concatenate(
        [value[:, 128:CH], jnp.zeros((value.shape[0], 256 - CH), F32)], axis=1
    )


def load_wide(scratch):
    return jnp.concatenate([scratch[0], scratch[1][:, 0 : CH - 128]], axis=1)


def load_window(x_ref, scratch):
    for lev in range(LEVS):
        for r in range(ROWS):
            store_wide(scratch, pl.ds(lev * ROWS + r, COLS, stride=CELLS), x_ref[lev, r])
    return load_wide(scratch)


def save_window(value, scratch, out_ref):
    store_wide(scratch, slice(0, TOK), value)
    for lev in range(LEVS):
        for r in range(ROWS):
            rows = pl.ds(lev * ROWS + r, COLS, stride=CELLS)
            out_ref[lev, r, :, 0:128] = scratch[0, rows, :]
            out_ref[lev, r, :, 128:CH] = scratch[1, rows, :][:, 0 : CH - 128]


def gather_octant(scratch, lev, j, k, piece):
    for rr in range(ROWS // 2):
        start = k * (COLS // 2) * CELLS + lev * ROWS + j * (ROWS // 2) + rr
        store_wide(
            scratch,
            pl.ds(start, COLS // 2, stride=CELLS),
            piece[rr * 8 : rr * 8 + COLS // 2],
        )


def first_forward(
    mask_ref, x_ref, cot_ref, wq_ref, wp_ref, wu_ref, wd_ref, table_ref, place_ref,
    keep_ref, send_ref, qkv_ref, weights_ref, attended_ref, mid_ref, pre_ref,
    grid_ref, flat_ref, up_ref, bias_ref,
):
    expand_bias(table_ref, place_ref, flat_ref, up_ref, bias_ref)
    for j, k, rr in octants():
        rows = pl.ds(rr * 8, COLS // 2)
        r = j * (ROWS // 2) + rr
        cols = slice(k * (COLS // 2), (k + 1) * (COLS // 2))
        send_ref[j, k, 1, rows, :] = cot_ref[0, r, cols, :]
        keep_ref[j, k, 1, rows, :] = cot_ref[1, r, cols, :]
    x = load_window(x_ref, grid_ref)
    key_bias, _ = window_masks(mask_ref, False)
    _, _, qkv, weights, attended = forward_attention(x, wq_ref[...], bias_ref[...], key_bias, None)
    qkv_ref[...] = qkv
    weights_ref[...] = weights
    attended_ref[...] = attended
    mid = x + dot3(halves(attended), halves(wp_ref[...]), NN)
    mid_ref[...] = mid
    normed, _ = norm(mid)
    pre = dot3(halves(normed), halves(wu_ref[...]), NN)
    pre_ref[...] = pre
    hidden = pre * half_cdf(pre)
    out = mid + dot3(halves(hidden), halves(wd_ref[...]), NN)
    store_wide(grid_ref, slice(0, TOK), out)
    spread_octants(grid_ref, send_ref, 0, 0)
    spread_octants(grid_ref, keep_ref, 0, 1)


def mlp_backward(g, pre, cdf, normed, inv, wu, wd):
    gp = halves(g)
    slope = cdf + pre * jnp.exp(-0.5 * pre * pre) * ((2.0 * np.pi) ** (-0.5))
    dpre = dot3(gp, halves(wd), NT) * slope
    dnormed = dot3(halves(dpre), halves(wu), NT)
    return dpre, g + norm_back(dnormed, normed, inv)


def attention_backward(dmid, qkv, weights, wp):
    q, k, v = scaled_parts(qkv)
    dattended = dot3(halves(dmid), halves(wp), NT)
    dstack = stack_heads(halves(dattended))
    dweights = dot3(dstack, halves(v), NT)
    inner = jnp.sum(dweights * weights, axis=-1, keepdims=True)
    dscores = weights * (dweights - inner)
    ds = halves(dscores)
    dq = merge_heads(dot3(ds, halves(k), NN)) * SCALE
    dk = dot3(ds, stack_heads(halves(q)), TN)
    dv = dot3(halves(weights), dstack, TN)
    return dscores, jnp.concatenate([dq, dk, dv], axis=1)


def pack_gradients(keep_ref, send_ref, wide_ref, dqkv, dproj, dup, ddown, flat_ref):
    core = lax.rem(lax.axis_index("lon"), 2)
    wide_ref[0, :, 0 : 3 * CH] = dqkv
    wide_ref[0, :, 3 * CH : 4 * CH] = dproj
    wide_ref[1] = dup
    for share in range(2 * NZ):
        rows = [
            ddown[share * 48 + m * SHARE : share * 48 + (m + 1) * SHARE] for m in range(HID // CH)
        ]
        wide_ref[2, share * SHARE : (share + 1) * SHARE, :] = jnp.concatenate(rows, axis=1)
    even = core == 0
    for z in range(NZ):
        for group in range(GROUPS):
            first = wide_ref[group, 2 * SHARE * z : 2 * SHARE * z + SHARE, :]
            second = wide_ref[group, 2 * SHARE * z + SHARE : 2 * SHARE * (z + 1), :]
            rows = slice((z * GROUPS + group) * SHARE, (z * GROUPS + group + 1) * SHARE)
            keep_ref[rows, :] = jnp.where(even, first, second)
            send_ref[rows, :] = jnp.where(even, second, first)
    for ref in (keep_ref, send_ref):
        ref[GROWS:BUF, :] = jnp.zeros((TROWS, HID), F32)
    for z in range(NZ):
        first = table_share(flat_ref, 2 * z)
        second = table_share(flat_ref, 2 * z + 1)
        rows = slice(GROWS + z // 3 * 8, GROWS + z // 3 * 8 + 8)
        lanes = slice(z % 3 * 256, z % 3 * 256 + 256)
        keep_ref[rows, lanes] = jnp.where(even, first, second)
        send_ref[rows, lanes] = jnp.where(even, second, first)


def table_share(flat_ref, share):
    start = share * TSHARE
    base = start // 128 * 128
    window = flat_ref[:, base : base + UPLANES]
    if start - base:
        window = pltpu.roll(window, UPLANES - (start - base), 1)
    return window[:, 0:256]


def second_pass(
    mask_ref, keep_ref, send_ref, across_ref, around_ref, wq_ref, wp_ref, wu_ref, wd_ref, bias_ref,
    back_keep_ref, back_send_ref, dscores_ref, normed_ref, attended_ref, hnormed_ref, hidden_ref,
    g_ref, dpre_ref, dmid_ref, dqkv_ref,
    grid_ref, cot_ref,
):
    for slot, scratch in ((0, grid_ref), (1, cot_ref)):
        for lev, source in ((0, keep_ref), (1, send_ref)):
            gather_octant(scratch, lev, 0, 0, source[1, 1, slot])
            gather_octant(scratch, lev, 1, 0, across_ref[lev, 1, slot])
            gather_octant(scratch, lev, 0, 1, around_ref[lev, 0, slot])
            gather_octant(scratch, lev, 1, 1, around_ref[lev, 1, slot])
    x = load_wide(grid_ref)
    g = load_wide(cot_ref)
    key_bias, pair = window_masks(mask_ref, True)
    normed, inv, qkv, weights, attended = forward_attention(
        x, wq_ref[...], bias_ref[...], key_bias, pair
    )
    normed_ref[...] = normed
    attended_ref[...] = attended
    mid = x + dot3(halves(attended), halves(wp_ref[...]), NN)
    hnormed, hinv = norm(mid)
    hnormed_ref[...] = hnormed
    pre = dot3(halves(hnormed), halves(wu_ref[...]), NN)
    cdf = half_cdf(pre)
    hidden_ref[...] = pre * cdf
    g_ref[...] = g
    dpre, dmid = mlp_backward(g, pre, cdf, hnormed, hinv, wu_ref[...], wd_ref[...])
    dpre_ref[...] = dpre
    dmid_ref[...] = dmid
    dscores, dqkv = attention_backward(dmid, qkv, weights, wp_ref[...])
    dscores_ref[...] = dscores
    dqkv_ref[...] = dqkv
    dx = dmid + norm_back(dot3(halves(dqkv), halves(wq_ref[...]), NT), normed, inv)
    store_wide(grid_ref, slice(0, TOK), dx)
    spread_octants(grid_ref, back_keep_ref, 0, 0)
    spread_octants(grid_ref, back_send_ref, 0, 1)


def second_gradients(
    dscores_ref, normed_ref, attended_ref, hnormed_ref, hidden_ref, g_ref, dpre_ref, dmid_ref,
    dqkv_ref, place_ref,
    keep_ref, send_ref,
    flat_ref, up_ref, wide_ref,
):
    collect_table(dscores_ref, place_ref, up_ref, flat_ref)
    pack_gradients(
        keep_ref, send_ref, wide_ref,
        dot3(halves(normed_ref[...]), halves(dqkv_ref[...]), TN),
        dot3(halves(attended_ref[...]), halves(dmid_ref[...]), TN),
        dot3(halves(hnormed_ref[...]), halves(dpre_ref[...]), TN),
        dot3(halves(hidden_ref[...]), halves(g_ref[...]), TN),
        flat_ref,
    )


def first_backward(
    x_ref, keep_ref, send_ref, across_ref, around_ref, wq_ref, wp_ref, wu_ref, wd_ref, qkv_ref,
    weights_ref, attended_ref, mid_ref, pre_ref, place_ref,
    grad_ref, gkeep_ref, gsend_ref,
    grid_ref, flat_ref, up_ref, wide_ref, dscores_ref,
):
    for lev, source in ((1, keep_ref), (0, send_ref)):
        gather_octant(grid_ref, lev, 1, 1, source[0, 0, 0])
        gather_octant(grid_ref, lev, 0, 1, across_ref[1 - lev, 0, 0])
        gather_octant(grid_ref, lev, 1, 0, around_ref[1 - lev, 0, 0])
        gather_octant(grid_ref, lev, 0, 0, around_ref[1 - lev, 1, 0])
    g = load_wide(grid_ref)
    pre = pre_ref[...]
    cdf = half_cdf(pre)
    hnormed, hinv = norm(mid_ref[...])
    dpre, dmid = mlp_backward(g, pre, cdf, hnormed, hinv, wu_ref[...], wd_ref[...])
    dup = dot3(halves(hnormed), halves(dpre), TN)
    ddown = dot3(halves(pre * cdf), halves(g), TN)
    dproj = dot3(halves(attended_ref[...]), halves(dmid), TN)
    dscores, dqkv = attention_backward(dmid, qkv_ref[...], weights_ref[...], wp_ref[...])
    dscores_ref[...] = dscores
    x = load_window(x_ref, grid_ref)
    normed, inv = norm(x)
    dx = dmid + norm_back(dot3(halves(dqkv), halves(wq_ref[...]), NT), normed, inv)
    save_window(dx, grid_ref, grad_ref)
    collect_table(dscores_ref, place_ref, up_ref, flat_ref)
    pack_gradients(
        gkeep_ref, gsend_ref, wide_ref,
        dot3(halves(normed), halves(dqkv), TN), dproj, dup, ddown, flat_ref,
    )


def spread_bias(table_ref, place_ref, bias_ref, flat_ref, up_ref):
    expand_bias(table_ref, place_ref, flat_ref, up_ref, bias_ref)


def pair_sum(k0_ref, r0_ref, k1_ref, r1_ref, plane_ref, table_ref, sum_ref):
    sum_ref[0] = k0_ref[...] + r0_ref[...]
    sum_ref[1] = k1_ref[...] + r1_ref[...]
    for z in range(NZ):
        for tile in range(36):
            block, group, lane = tile // 18, tile // 6 % 3, tile % 6
            start = z * GROUPS * SHARE + group * SHARE
            lanes = slice(lane * 128, lane * 128 + 128)
            if tile < 32:
                to = z * UNIT + tile % 2 * SHARE
                plane_ref[tile // 2, to : to + SHARE, :] = sum_ref[block, start : start + SHARE, lanes]
            else:
                to = z * UNIT + 24
                for quarter in range(4):
                    part = slice(start + quarter * 3, start + quarter * 3 + 3)
                    plane_ref[(tile - 32) * 4 + quarter, to : to + 3, :] = sum_ref[block, part, lanes]
        for block in range(2):
            for half in range(2):
                rows = slice(GROWS + z // 3 * 8, GROWS + z // 3 * 8 + 8)
                lanes = slice(z % 3 * 256 + half * 128, z % 3 * 256 + half * 128 + 128)
                to = (block * 2 + half) * 8
                table_ref[z, to : to + 8, :] = sum_ref[block, rows, lanes]


def plane_sum(got_ref, table_ref, out_ref, sum_ref):
    total = got_ref[0]
    for p in range(1, PLANE):
        total = total + got_ref[p]
    sum_ref[...] = total
    for z in range(NZ):
        out_ref[z, 0:UNIT, :] = sum_ref[z * UNIT : (z + 1) * UNIT, :]
        out_ref[z, UNIT:32, :] = jnp.zeros((32 - UNIT, 128), F32)
    out_ref[:, 32:64, :] = table_ref[...]


def lon_sum(got_ref, out_ref, table_ref, sum_ref):
    total = got_ref[0]
    for z in range(1, NZ):
        total = total + got_ref[z]
    sum_ref[...] = total
    for p in range(PLANE):
        out_ref[p] = sum_ref[0:32, :]
    for block in range(2):
        rows = 32 + block * 16
        table_ref[block, :, 0:128] = sum_ref[rows : rows + HEADS, :]
        table_ref[block, :, 128:TSHARE] = sum_ref[rows + 8 : rows + 8 + HEADS, 0 : TSHARE - 128]


def unpack(scale, got_ref, qkv_ref, proj_ref, up_ref, down_ref, wide_ref):
    for tile in range(36):
        block, group, lane = tile // 18, tile // 6 % 3, tile % 6
        lanes = slice(lane * 128, lane * 128 + 128)
        if tile < 32:
            to = tile % 2 * SHARE
            wide_ref[block, group, 0:SHARE, lanes] = got_ref[tile // 2, to : to + SHARE, :] * scale
        else:
            for quarter in range(4):
                wide_ref[block, group, quarter * 3 : quarter * 3 + 3, lanes] = (
                    got_ref[(tile - 32) * 4 + quarter, 24:27, :] * scale
                )
    for block in range(2):
        qkv_ref[block] = wide_ref[block, 0, 0:SHARE, 0 : 3 * CH]
        proj_ref[block] = wide_ref[block, 0, 0:SHARE, 3 * CH : 4 * CH]
        up_ref[block] = wide_ref[block, 1, 0:SHARE, :]
        for m in range(HID // CH):
            down_ref[block, m * SHARE : (m + 1) * SHARE, :] = wide_ref[
                block, 2, 0:SHARE, m * CH : (m + 1) * CH
            ]


def struct(*shape):
    return jax.ShapeDtypeStruct(shape, F32)


def vmem(*shape):
    return pltpu.VMEM(shape, F32)


def whole(*shape):
    return pl.BlockSpec(shape, lambda i: (0,) * len(shape))


def part_of(block, *shape):
    return pl.BlockSpec((None,) + shape, lambda i: (block,) + (0,) * len(shape))


def weight_specs(block):
    return [
        part_of(block, CH, 3 * CH),
        part_of(block, CH, CH),
        part_of(block, CH, HID),
        part_of(block, HID, CH),
    ]


def table_spec(block):
    return pl.BlockSpec((None, 1, 1, HEADS, POS), lambda i: (block, 0, 0, 0, 0))


def call(body, in_specs, outs, scratch, cost=0, mib=28):
    return pl.pallas_call(
        body,
        grid=(1,),
        in_specs=in_specs,
        out_specs=[whole(*o.shape) for o in outs],
        out_shape=outs,
        scratch_shapes=scratch,
        compiler_params=params(mib),
        cost_estimate=pl.CostEstimate(flops=cost, bytes_accessed=4 * 2**20, transcendentals=0),
    )


SMEM = pl.BlockSpec(memory_space=pltpu.SMEM)
FLAT = 3456


def shifted(block, axis, distance):
    devices = range(lax.axis_size(axis))
    route = [((i - distance) % len(devices), i) for i in devices]
    return lax.ppermute(block, axis, route)


def exchange(keep, send, step, side):
    stay = 1 - side
    moved = shifted(send, "lev", step)
    across = shifted(jnp.stack([keep[side], moved[side]]), "lat", step)
    around = shifted(
        jnp.stack(
            [
                jnp.stack([keep[stay, side], across[0, side]]),
                jnp.stack([moved[stay, side], across[1, side]]),
            ]
        ),
        "lon",
        step,
    )
    return moved, across, around


def swap_cores(v):
    return lax.ppermute(v, "lon", [(i, i ^ 1) for i in range(lax.axis_size("lon"))])


def local(inputs, cotangent, qkv_weight, proj_weight, up_weight, down_weight, bias_table, lat_mask):
    place = place_matrix()
    weights = (qkv_weight, proj_weight, up_weight, down_weight)
    grid_spec = whole(LEVS, ROWS, COLS, CH)
    wide_scratch = [vmem(8, FLAT), vmem(8 * CELLS, UPLANES)]
    half = (2, 2, 2, OCTANT, CH)
    keep, send, qkv, attention, attended, mid, pre = call(
        first_forward,
        [SMEM, grid_spec, grid_spec] + weight_specs(0) + [table_spec(0), whole(UPLANES, UPLANES)],
        [
            struct(*half),
            struct(*half),
            struct(TOK, 3 * CH),
            struct(STACK, TOK),
            struct(TOK, CH),
            struct(TOK, CH),
            struct(TOK, HID),
        ],
        [vmem(2, TOK, 128)] + wide_scratch + [vmem(STACK, TOK)],
        cost=500_000_000,
    )(lat_mask, inputs, cotangent, *weights, bias_table, place)
    (bias_second,) = call(
        spread_bias,
        [table_spec(1), whole(UPLANES, UPLANES)],
        [struct(STACK, TOK)],
        wide_scratch,
        cost=200_000_000,
    )(bias_table, place)
    moved, across, around = exchange(keep, send, -1, 0)
    side = (2, 2, 2, OCTANT, CH)
    back_half = (2, 2, 1, OCTANT, CH)
    factors = [
        struct(STACK, TOK),
        struct(TOK, CH),
        struct(TOK, CH),
        struct(TOK, CH),
        struct(TOK, HID),
        struct(TOK, CH),
        struct(TOK, HID),
        struct(TOK, CH),
        struct(TOK, 3 * CH),
    ]
    back_keep, back_send, *saved = call(
        second_pass,
        [SMEM, whole(*half), whole(*half), whole(*side), whole(2, 2, 2, OCTANT, CH)]
        + weight_specs(1)
        + [whole(STACK, TOK)],
        [struct(*back_half), struct(*back_half)] + factors,
        [vmem(2, TOK, 128), vmem(2, TOK, 128)],
        cost=1_000_000_000,
    )(lat_mask, keep, moved, across, around, *weights, bias_second)
    keep2, send2 = call(
        second_gradients,
        [whole(*f.shape) for f in factors] + [whole(UPLANES, UPLANES)],
        [struct(BUF, HID), struct(BUF, HID)],
        wide_scratch + [vmem(GROUPS, CH, HID)],
        cost=500_000_000,
    )(*saved, place)
    back_moved, back_across, back_around = exchange(back_keep, back_send, 1, 1)
    got2 = swap_cores(send2)
    grad_input, keep1, send1 = call(
        first_backward,
        [
            grid_spec,
            whole(*back_half),
            whole(*back_half),
            whole(2, 2, 1, OCTANT, CH),
            whole(2, 2, 1, OCTANT, CH),
        ]
        + weight_specs(0)
        + [
            whole(TOK, 3 * CH),
            whole(STACK, TOK),
            whole(TOK, CH),
            whole(TOK, CH),
            whole(TOK, HID),
            whole(UPLANES, UPLANES),
        ],
        [struct(LEVS, ROWS, COLS, CH), struct(BUF, HID), struct(BUF, HID)],
        [vmem(2, TOK, 128)] + wide_scratch + [vmem(GROUPS, CH, HID), vmem(STACK, TOK)],
        cost=1_000_000_000,
    )(
        inputs, back_keep, back_moved, back_across, back_around, *weights,
        qkv, attention, attended, mid, pre, place,
    )
    got1 = swap_cores(send1)
    for_plane, table_part = call(
        pair_sum,
        [whole(BUF, HID)] * 4,
        [struct(PLANE, NZ * UNIT, 128), struct(NZ, 32, 128)],
        [vmem(2, BUF, HID)],
    )(keep1, got1, keep2, got2)
    plane_got = lax.all_to_all(for_plane, ("lat", "lev"), 0, 0, tiled=True)
    (for_lon,) = call(
        plane_sum,
        [whole(PLANE, NZ * UNIT, 128), whole(NZ, 32, 128)],
        [struct(NZ, 64, 128)],
        [vmem(NZ * UNIT, 128)],
    )(plane_got, table_part)
    core_groups = [[z * 2 + c for z in range(NZ)] for c in range(2)]
    lon_got = lax.all_to_all(
        for_lon, "lon", 0, 0, axis_index_groups=core_groups, tiled=True
    )
    copies, grad_table = call(
        lon_sum,
        [whole(NZ, 64, 128)],
        [struct(PLANE, 32, 128), struct(2, HEADS, TSHARE)],
        [vmem(64, 128)],
    )(lon_got)
    shares = lax.all_to_all(copies, ("lat", "lev"), 0, 0, tiled=True)
    tokens = TOK * lax.axis_size("lon") * lax.axis_size("lat") * lax.axis_size("lev")
    grad_qkv, grad_proj, grad_up, grad_down = call(
        lambda *refs: unpack(float(tokens) ** (-0.5), *refs),
        [whole(PLANE, 32, 128)],
        [
            struct(2, SHARE, 3 * CH),
            struct(2, SHARE, CH),
            struct(2, SHARE, HID),
            struct(2, 48, CH),
        ],
        [vmem(2, GROUPS, 16, HID)],
    )(shares)
    return (
        grad_input,
        grad_qkv,
        grad_proj,
        grad_up,
        grad_down,
        grad_table.reshape(2, 1, 1, HEADS, TSHARE),
    )


def solution(mesh):
    in_specs = (
        P("lev", "lat", "lon", None),
        P("lev", "lat", "lon", None),
        P(),
        P(),
        P(),
        P(),
        P(None, "lev", "lat", None, None),
        P(),
    )
    out_specs = (
        P("lev", "lat", "lon", None),
        P(None, "lon", None),
        P(None, "lon", None),
        P(None, "lon", None),
        P(None, "lon", None),
        P(None, "lev", "lat", None, "lon"),
    )
    return jax.shard_map(local, mesh=mesh, in_specs=in_specs, out_specs=out_specs, check_vma=False)
```

```python
import jax
import jax.numpy as jnp
import numpy as np
from jax import lax
from jax.experimental import pallas as pl
from jax.experimental.pallas import tpu as pltpu
from jax.sharding import PartitionSpec as P

F32 = jnp.float32
BF16 = jnp.bfloat16

HEADS = 6
HEAD = 32
CH = 192
HID = 768
LEVS = 2
ROWS = 6
COLS = 12
CELLS = LEVS * ROWS
TOK = CELLS * COLS
STACK = HEADS * TOK
SPAN = 2 * COLS - 1
POS = 3312
CHUNK = ROWS * SPAN
UPLANES = 384
NEGATIVE = -10000.0
SCALE = HEAD ** (-0.5)

NZ = 8
SHARE = 12
GROUPS = 3
GROWS = NZ * GROUPS * SHARE
TROWS = 24
BUF = GROWS + TROWS
TSHARE = POS // 16
PLANE = 16
UNIT = 27

NN = ((1,), (0,))
NT = ((1,), (1,))
TN = ((0,), (0,))


def params(mib=28):
    return pltpu.CompilerParams(vmem_limit_bytes=mib * 1024 * 1024)


def halves(v):
    top = v.astype(BF16)
    return top, (v - top.astype(F32)).astype(BF16)


def thirds(v):
    top = v.astype(BF16)
    rest = v - top.astype(F32)
    mid = rest.astype(BF16)
    return top, mid, (rest - mid.astype(F32)).astype(BF16)


def dot(a, b, dims):
    return lax.dot_general(a, b, (dims, ((), ())), preferred_element_type=F32)


def dot3(a, b, dims):
    return dot(a[0], b[0], dims) + (dot(a[0], b[1], dims) + dot(a[1], b[0], dims))


def exact_dot(v, one_hot, dims):
    a, b, c = thirds(v)
    return (dot(a, one_hot, dims) + dot(b, one_hot, dims)) + dot(c, one_hot, dims)


def norm(v):
    centered = v - jnp.mean(v, axis=-1, keepdims=True)
    inv = lax.rsqrt(jnp.mean(centered * centered, axis=-1, keepdims=True) + 1e-05)
    return centered * inv, inv


def norm_back(d, normed, inv):
    return inv * (
        d
        - jnp.mean(d, axis=-1, keepdims=True)
        - normed * jnp.mean(d * normed, axis=-1, keepdims=True)
    )


ERF_TOP = (
    0.00022905065861350646,
    0.0034082910107109506,
    0.050955695062380861,
    0.18520832239976145,
    1.128379143519084,
)
ERF_LOW = (
    -1.1791602954361697e-7,
    0.000023547966471313185,
    0.0010179625278914885,
    0.014070470171167667,
    0.11098505178285362,
    0.49746925110067538,
    1.0,
)


def erf(v):
    v = jnp.clip(v, -3.832506856900711, 3.832506856900711)
    sq = v * v
    top = jnp.full_like(v, ERF_TOP[0])
    for term in ERF_TOP[1:]:
        top = top * sq + term
    low = jnp.full_like(v, ERF_LOW[0])
    for term in ERF_LOW[1:]:
        low = low * sq + term
    return v * top / low


def half_cdf(pre):
    return 0.5 + 0.5 * erf(pre * (0.5**0.5))


def head_rows(dtype):
    lane = lax.broadcasted_iota(jnp.int32, (1, CH), 1)
    return [
        jnp.where((lane >= h * HEAD) & (lane < (h + 1) * HEAD), 1.0, 0.0).astype(dtype)
        for h in range(HEADS)
    ]


def stack_heads(pair):
    rows = head_rows(BF16)
    return tuple(jnp.concatenate([part * rows[h] for h in range(HEADS)], axis=0) for part in pair)


def merge_heads(stacked):
    rows = head_rows(F32)
    total = stacked[0:TOK] * rows[0]
    for h in range(1, HEADS):
        total = total + stacked[h * TOK : (h + 1) * TOK] * rows[h]
    return total


def place_matrix():
    mat = np.zeros((UPLANES, UPLANES), np.float32)
    for kl in range(LEVS):
        for kr in range(ROWS):
            for p in range(SPAN):
                mat[kl * CHUNK + kr * SPAN + p, p * CELLS + kr * LEVS + kl] = 1.0
    return jnp.asarray(mat, BF16)


def chunk_start(ql, kl, qr):
    return ((ql * LEVS + kl) * ROWS + qr) * CHUNK


def expand_bias(table_ref, place_ref, flat_ref, up_ref, bias_ref):
    flat_ref[...] = jnp.zeros_like(flat_ref)
    for h in range(HEADS):
        flat_ref[h : h + 1, 0:POS] = table_ref[0, h]
    lane = lax.broadcasted_iota(jnp.int32, (8, UPLANES), 1)
    for ql in range(LEVS):
        for qr in range(ROWS):
            g = qr * LEVS + ql
            row = jnp.zeros((8, UPLANES), F32)
            for kl in range(LEVS):
                start = chunk_start(ql, kl, qr)
                base = start // 128 * 128
                window = flat_ref[:, base : base + UPLANES]
                turn = (kl * CHUNK - (start - base)) % UPLANES
                if turn:
                    window = pltpu.roll(window, turn, 1)
                row = jnp.where((lane >= kl * CHUNK) & (lane < (kl + 1) * CHUNK), window, row)
            up_ref[g * 8 : (g + 1) * 8, :] = row
    ups = exact_dot(up_ref[...], place_ref[...], NN)
    for h in range(HEADS):
        rows = jnp.concatenate([ups[g * 8 + h : g * 8 + h + 1] for g in range(CELLS)], axis=0)
        for qc in range(COLS):
            turn = (-(COLS - 1 - qc) * CELLS) % UPLANES
            moved = pltpu.roll(rows, turn, 1) if turn else rows
            bias_ref[h * TOK + qc * CELLS : h * TOK + (qc + 1) * CELLS, :] = moved[:, 0:TOK]


def collect_table(dscore_ref, place_ref, up_ref, flat_ref):
    up_ref[...] = jnp.zeros_like(up_ref)
    for h in range(HEADS):
        total = jnp.zeros((CELLS, UPLANES), F32)
        for qc in range(COLS):
            block = dscore_ref[h * TOK + qc * CELLS : h * TOK + (qc + 1) * CELLS, :]
            block = jnp.concatenate([block, jnp.zeros((CELLS, UPLANES - TOK), F32)], axis=1)
            turn = (COLS - 1 - qc) * CELLS
            total = total + (pltpu.roll(block, turn, 1) if turn else block)
        for g in range(CELLS):
            up_ref[g * 8 + h : g * 8 + h + 1, :] = total[g : g + 1]
    raw = exact_dot(up_ref[...], place_ref[...], NT)
    flat_ref[...] = jnp.zeros_like(flat_ref)
    lane = lax.broadcasted_iota(jnp.int32, (8, UPLANES), 1)
    for ql in range(LEVS):
        for qr in range(ROWS):
            g = qr * LEVS + ql
            row = raw[g * 8 : (g + 1) * 8]
            for kl in range(LEVS):
                start = chunk_start(ql, kl, qr)
                base = start // 128 * 128
                shift = start - base
                turn = (shift - kl * CHUNK) % UPLANES
                moved = pltpu.roll(row, turn, 1) if turn else row
                keep = (lane >= shift) & (lane < shift + CHUNK)
                window = flat_ref[:, base : base + UPLANES]
                flat_ref[:, base : base + UPLANES] = jnp.where(keep, moved, window)


def window_masks(mask_ref, second):
    lev = lax.axis_index("lev")
    lat = lax.axis_index("lat")
    last_lev = lev == lax.axis_size("lev") - 1
    last_lat = lat == lax.axis_size("lat") - 1
    key_col = lax.broadcasted_iota(jnp.int32, (1, TOK), 1)
    key_row = lax.div(lax.rem(key_col, CELLS), LEVS)
    key_bias = jnp.zeros((1, TOK), F32)
    count = ROWS * lax.axis_size("lat")
    for r in range(ROWS):
        place = lat * ROWS + r
        if second:
            place = lax.rem(place + ROWS // 2, count)
        value = NEGATIVE * (1.0 - mask_ref[place].astype(F32))
        key_bias = jnp.where(key_row == r, value, key_bias)
    if not second:
        return key_bias, None

    def label(tokens):
        level = jnp.where(lax.rem(tokens, LEVS) >= LEVS // 2, 2, 0)
        row = jnp.where(lax.rem(tokens, CELLS) >= CELLS // 2, 1, 0)
        return level * last_lev.astype(jnp.int32) + row * last_lat.astype(jnp.int32)

    query = label(lax.broadcasted_iota(jnp.int32, (TOK, 1), 0))
    pair = jnp.where(query == label(key_col), 0.0, NEGATIVE).astype(F32)
    return key_bias, pair


def add_masks(scores, key_bias, pair):
    scores = scores + key_bias
    if pair is None:
        return scores
    return jnp.concatenate([scores[h * TOK : (h + 1) * TOK] + pair for h in range(HEADS)], axis=0)


def scaled_parts(qkv):
    return qkv[:, 0:CH] * SCALE, qkv[:, CH : 2 * CH], qkv[:, 2 * CH : 3 * CH]


def forward_attention(x, wq, bias, key_bias, pair):
    normed, inv = norm(x)
    qkv = dot3(halves(normed), halves(wq), NN)
    q, k, v = scaled_parts(qkv)
    scores = dot3(stack_heads(halves(q)), halves(k), NT) + bias
    scores = add_masks(scores, key_bias, pair)
    grown = jnp.exp(scores - jnp.max(scores, axis=-1, keepdims=True))
    weights = grown * (1.0 / jnp.sum(grown, axis=-1, keepdims=True))
    attended = merge_heads(dot3(halves(weights), halves(v), NN))
    return normed, inv, qkv, weights, attended


SIDE = COLS // 2
MAIN = ROWS // 2 * SIDE
WIDE = 56
THIN = 32
REST = CH - 128


MOVES = ((0, 0), (1, 0), (0, 1), (1, 1))


def six_rows(lev, j, k):
    for rr in range(ROWS // 2):
        yield rr, k * SIDE * CELLS + (j * (ROWS // 2) + rr) * LEVS + lev


def spread_pair(grid, out_refs):
    for (dlev, dj), out_ref in zip(MOVES, out_refs):
        for k in range(2):
            for rr, start in six_rows(1 - dlev, 1 - dj, k):
                rows = pl.ds(start, SIDE, stride=CELLS)
                for part, to in ((0, 0), (2, MAIN), (1, 2 * MAIN)):
                    out_ref[k, to + rr * SIDE : to + (rr + 1) * SIDE, :] = grid[part, rows, :]


def gather_pair(grid, own_refs, around_ref):
    for piece, (dlev, dj) in enumerate(MOVES):
        for k in range(2):
            ref, slot = (own_refs[piece], 1) if k == 0 else (around_ref, piece)
            for rr, start in six_rows(dlev, dj, k):
                rows = pl.ds(start, SIDE, stride=CELLS)
                for part, at in ((0, 0), (2, MAIN), (1, 2 * MAIN)):
                    grid[part, rows, :] = ref[slot, at + rr * SIDE : at + (rr + 1) * SIDE, :]


def spread_one(grid, out_refs):
    low = lax.broadcasted_iota(jnp.int32, (SIDE // 2, 128), 1) < REST
    for (dlev, dj), out_ref in zip(MOVES, out_refs):
        for k in range(2):
            for rr, start in six_rows(dlev, dj, k):
                rows = pl.ds(start, SIDE, stride=CELLS)
                out_ref[k, rr * SIDE : (rr + 1) * SIDE, :] = grid[0, rows, :]
                one = grid[1, pl.ds(start, SIDE // 2, stride=CELLS), :]
                two = grid[1, pl.ds(start + SIDE // 2 * CELLS, SIDE // 2, stride=CELLS), :]
                to = MAIN + rr * (SIDE // 2)
                out_ref[k, to : to + SIDE // 2, :] = jnp.where(low, one, pltpu.roll(two, REST, 1))


def gather_one(grid, own_refs, around_ref):
    for piece, (dlev, dj) in enumerate(MOVES):
        for k in range(2):
            ref, slot = (own_refs[piece], 0) if k == 1 else (around_ref, piece)
            for rr, start in six_rows(1 - dlev, 1 - dj, k):
                rows = pl.ds(start, SIDE, stride=CELLS)
                grid[0, rows, :] = ref[slot, rr * SIDE : (rr + 1) * SIDE, :]
                at = MAIN + rr * (SIDE // 2)
                both = ref[slot, at : at + SIDE // 2, :]
                grid[1, pl.ds(start, SIDE // 2, stride=CELLS), :] = both
                rows = pl.ds(start + SIDE // 2 * CELLS, SIDE // 2, stride=CELLS)
                grid[1, rows, :] = pltpu.roll(both, REST, 1)


def load_first(grid):
    return jnp.concatenate([grid[0], grid[1][:, 0:REST]], axis=1)


def load_second(grid):
    return jnp.concatenate([grid[2], grid[1][:, REST:128]], axis=1)


def store_first(grid, value):
    grid[0] = value[:, 0:128]
    grid[1, :, 0:REST] = value[:, 128:CH]


def load_window(x_ref, grid, second=False):
    head, at = (2, REST) if second else (0, 0)
    for r in range(ROWS):
        for c in range(COLS):
            rows = slice(c * CELLS + r * LEVS, c * CELLS + (r + 1) * LEVS)
            cell = x_ref[r, c]
            grid[head, rows, :] = cell[:, 0:128]
            grid[1, rows, at : at + REST] = cell[:, 128:CH]


def save_window(grid, out_ref):
    for r in range(ROWS):
        for c in range(COLS):
            rows = slice(c * CELLS + r * LEVS, c * CELLS + (r + 1) * LEVS)
            out_ref[r, c, :, 0:128] = grid[0, rows, :]
            out_ref[r, c, :, 128:CH] = grid[1, rows, 0:REST]


def first_forward(
    mask_ref, x_hbm, cot_hbm, wq_hbm, wp_hbm, wu_hbm, wd_hbm, table_hbm, place_hbm,
    own_ref, lev_ref, lat_ref, both_ref, qkv_hbm, weights_hbm, attended_hbm, mid_hbm, pre_hbm,
    x_ref, cot_ref, wq_ref, wp_ref, wu_ref, wd_ref, table_ref, place_ref,
    grid_ref, flat_ref, up_ref, bias_ref, qkv_ref, weights_ref, attended_ref, mid_ref, pre_ref, sems,
    out_sems,
):
    pairs = (
        (table_hbm.at[0], table_ref),
        (place_hbm, place_ref),
        (x_hbm, x_ref),
        (wq_hbm.at[0], wq_ref),
        (cot_hbm, cot_ref),
        (wp_hbm.at[0], wp_ref),
        (wu_hbm.at[0], wu_ref),
        (wd_hbm.at[0], wd_ref),
    )
    copies = [pltpu.make_async_copy(*pair, sems.at[i]) for i, pair in enumerate(pairs)]
    for copy in copies:
        copy.start()
    copies[0].wait()
    copies[1].wait()
    expand_bias(table_ref, place_ref, flat_ref, up_ref, bias_ref)
    copies[2].wait()
    load_window(x_ref, grid_ref)
    x = load_first(grid_ref)
    copies[3].wait()
    key_bias, _ = window_masks(mask_ref, False)
    _, _, qkv, weights, attended = forward_attention(x, wq_ref[...], bias_ref[...], key_bias, None)
    saved = []

    def save(value, ref, to):
        ref[...] = value
        saved.append(pltpu.make_async_copy(ref, to, out_sems.at[len(saved)]))
        saved[-1].start()

    save(qkv, qkv_ref, qkv_hbm)
    save(weights, weights_ref, weights_hbm)
    save(attended, attended_ref, attended_hbm)
    for copy in copies[4:]:
        copy.wait()
    mid = x + dot3(halves(attended), halves(wp_ref[...]), NN)
    save(mid, mid_ref, mid_hbm)
    normed, _ = norm(mid)
    pre = dot3(halves(normed), halves(wu_ref[...]), NN)
    save(pre, pre_ref, pre_hbm)
    hidden = pre * half_cdf(pre)
    load_window(cot_ref, grid_ref, True)
    store_first(grid_ref, mid + dot3(halves(hidden), halves(wd_ref[...]), NT))
    for copy in saved:
        copy.wait()
    spread_pair(grid_ref, (own_ref, lev_ref, lat_ref, both_ref))


def mlp_backward(g, pre, cdf, normed, inv, wu, wd):
    gp = halves(g)
    slope = cdf + pre * jnp.exp(-0.5 * pre * pre) * ((2.0 * np.pi) ** (-0.5))
    dpre = dot3(gp, halves(wd), NN) * slope
    dnormed = dot3(halves(dpre), halves(wu), NT)
    return dpre, g + norm_back(dnormed, normed, inv)


def attention_backward(dmid, qkv, weights, wp):
    q, k, v = scaled_parts(qkv)
    dattended = dot3(halves(dmid), halves(wp), NT)
    dstack = stack_heads(halves(dattended))
    dweights = dot3(dstack, halves(v), NT)
    inner = jnp.sum(dweights * weights, axis=-1, keepdims=True)
    dscores = weights * (dweights - inner)
    ds = halves(dscores)
    dq = merge_heads(dot3(ds, halves(k), NN)) * SCALE
    dk = dot3(ds, stack_heads(halves(q)), TN)
    dv = dot3(halves(weights), dstack, TN)
    return dscores, jnp.concatenate([dq, dk, dv], axis=1)


def pack_gradients(keep_ref, send_ref, wide_ref, dqkv, dproj, dup, ddown, flat_ref):
    core = lax.rem(lax.axis_index("lon"), 2)
    wide_ref[0, :, 0 : 3 * CH] = dqkv
    wide_ref[0, :, 3 * CH : 4 * CH] = dproj
    wide_ref[1] = dup
    for share in range(2 * NZ):
        rows = [
            ddown[share * 48 + m * SHARE : share * 48 + (m + 1) * SHARE] for m in range(HID // CH)
        ]
        wide_ref[2, share * SHARE : (share + 1) * SHARE, :] = jnp.concatenate(rows, axis=1)
    even = core == 0
    for z in range(NZ):
        for group in range(GROUPS):
            first = wide_ref[group, 2 * SHARE * z : 2 * SHARE * z + SHARE, :]
            second = wide_ref[group, 2 * SHARE * z + SHARE : 2 * SHARE * (z + 1), :]
            rows = slice((z * GROUPS + group) * SHARE, (z * GROUPS + group + 1) * SHARE)
            keep_ref[rows, :] = jnp.where(even, first, second)
            send_ref[rows, :] = jnp.where(even, second, first)
    for ref in (keep_ref, send_ref):
        ref[GROWS:BUF, :] = jnp.zeros((TROWS, HID), F32)
    for z in range(NZ):
        first = table_share(flat_ref, 2 * z)
        second = table_share(flat_ref, 2 * z + 1)
        rows = slice(GROWS + z // 3 * 8, GROWS + z // 3 * 8 + 8)
        lanes = slice(z % 3 * 256, z % 3 * 256 + 256)
        keep_ref[rows, lanes] = jnp.where(even, first, second)
        send_ref[rows, lanes] = jnp.where(even, second, first)


def table_share(flat_ref, share):
    start = share * TSHARE
    base = start // 128 * 128
    window = flat_ref[:, base : base + UPLANES]
    if start - base:
        window = pltpu.roll(window, UPLANES - (start - base), 1)
    return window[:, 0:256]


def second_pass(
    mask_ref, own_ref, lev_ref, lat_ref, both_ref, around_ref, wq_ref, wp_ref, wu_ref, wd_ref, bias_ref,
    back_own_ref, back_lev_ref, back_lat_ref, back_both_ref, dscores_ref, normed_ref, attended_ref, hnormed_ref, hidden_ref,
    g_ref, dpre_ref, dmid_ref, dqkv_ref,
    grid_ref,
):
    gather_pair(grid_ref, (own_ref, lev_ref, lat_ref, both_ref), around_ref)
    x = load_first(grid_ref)
    g = load_second(grid_ref)
    key_bias, pair = window_masks(mask_ref, True)
    normed, inv, qkv, weights, attended = forward_attention(
        x, wq_ref[...], bias_ref[...], key_bias, pair
    )
    normed_ref[...] = normed
    attended_ref[...] = attended
    mid = x + dot3(halves(attended), halves(wp_ref[...]), NN)
    hnormed, hinv = norm(mid)
    hnormed_ref[...] = hnormed
    pre = dot3(halves(hnormed), halves(wu_ref[...]), NN)
    cdf = half_cdf(pre)
    hidden_ref[...] = pre * cdf
    g_ref[...] = g
    dpre, dmid = mlp_backward(g, pre, cdf, hnormed, hinv, wu_ref[...], wd_ref[...])
    dpre_ref[...] = dpre
    dmid_ref[...] = dmid
    dscores, dqkv = attention_backward(dmid, qkv, weights, wp_ref[...])
    dscores_ref[...] = dscores
    dqkv_ref[...] = dqkv
    dx = dmid + norm_back(dot3(halves(dqkv), halves(wq_ref[...]), NT), normed, inv)
    store_first(grid_ref, dx)
    spread_one(grid_ref, (back_own_ref, back_lev_ref, back_lat_ref, back_both_ref))


def second_gradients(
    dscores_ref, normed_ref, attended_ref, hnormed_ref, hidden_ref, g_ref, dpre_ref, dmid_ref,
    dqkv_ref, place_ref,
    keep_ref, send_ref,
    flat_ref, up_ref, wide_ref,
):
    collect_table(dscores_ref, place_ref, up_ref, flat_ref)
    pack_gradients(
        keep_ref, send_ref, wide_ref,
        dot3(halves(normed_ref[...]), halves(dqkv_ref[...]), TN),
        dot3(halves(attended_ref[...]), halves(dmid_ref[...]), TN),
        dot3(halves(hnormed_ref[...]), halves(dpre_ref[...]), TN),
        dot3(halves(hidden_ref[...]), halves(g_ref[...]), TN),
        flat_ref,
    )


def first_backward(
    x_ref, own_ref, lev_ref, lat_ref, both_ref, around_ref, wp_ref, wu_ref, wd_ref, qkv_ref,
    weights_ref, attended_ref, mid_ref, pre_ref, place_ref,
    dmid_ref, dqkv_ref, gkeep_ref, gsend_ref,
    grid_ref, flat_ref, up_ref, wide_ref, dscores_ref,
):
    gather_one(grid_ref, (own_ref, lev_ref, lat_ref, both_ref), around_ref)
    g = load_first(grid_ref)
    pre = pre_ref[...]
    cdf = half_cdf(pre)
    hnormed, hinv = norm(mid_ref[...])
    dpre, dmid = mlp_backward(g, pre, cdf, hnormed, hinv, wu_ref[...], wd_ref[...])
    dup = dot3(halves(hnormed), halves(dpre), TN)
    ddown = dot3(halves(pre * cdf), halves(g), TN)
    dproj = dot3(halves(attended_ref[...]), halves(dmid), TN)
    dscores, dqkv = attention_backward(dmid, qkv_ref[...], weights_ref[...], wp_ref[...])
    dscores_ref[...] = dscores
    dmid_ref[...] = dmid
    dqkv_ref[...] = dqkv
    load_window(x_ref, grid_ref)
    normed, _ = norm(load_first(grid_ref))
    collect_table(dscores_ref, place_ref, up_ref, flat_ref)
    pack_gradients(
        gkeep_ref, gsend_ref, wide_ref,
        dot3(halves(normed), halves(dqkv), TN), dproj, dup, ddown, flat_ref,
    )


def input_gradient(x_ref, wq_ref, dmid_ref, dqkv_ref, grad_ref, grid_ref):
    load_window(x_ref, grid_ref)
    normed, inv = norm(load_first(grid_ref))
    dnormed = dot3(halves(dqkv_ref[...]), halves(wq_ref[...]), NT)
    store_first(grid_ref, dmid_ref[...] + norm_back(dnormed, normed, inv))
    save_window(grid_ref, grad_ref)


def spread_bias(table_ref, place_ref, bias_ref, flat_ref, up_ref):
    expand_bias(table_ref, place_ref, flat_ref, up_ref, bias_ref)


def pair_sum(k0_ref, r0_ref, k1_ref, r1_ref, plane_ref, table_ref, sum_ref):
    sum_ref[0] = k0_ref[...] + r0_ref[...]
    sum_ref[1] = k1_ref[...] + r1_ref[...]
    for z in range(NZ):
        for tile in range(36):
            block, group, lane = tile // 18, tile // 6 % 3, tile % 6
            start = z * GROUPS * SHARE + group * SHARE
            lanes = slice(lane * 128, lane * 128 + 128)
            if tile < 32:
                to = z * UNIT + tile % 2 * SHARE
                plane_ref[tile // 2, to : to + SHARE, :] = sum_ref[block, start : start + SHARE, lanes]
            else:
                to = z * UNIT + 24
                for quarter in range(4):
                    part = slice(start + quarter * 3, start + quarter * 3 + 3)
                    plane_ref[(tile - 32) * 4 + quarter, to : to + 3, :] = sum_ref[block, part, lanes]
        for block in range(2):
            for half in range(2):
                rows = slice(GROWS + z // 3 * 8, GROWS + z // 3 * 8 + 8)
                lanes = slice(z % 3 * 256 + half * 128, z % 3 * 256 + half * 128 + 128)
                to = (block * 2 + half) * HEADS
                table_ref[z, to : to + HEADS, :] = sum_ref[block, rows, lanes][0:HEADS]


def plane_sum(got_ref, table_ref, out_ref, sum_ref):
    total = got_ref[0]
    for p in range(1, PLANE):
        total = total + got_ref[p]
    sum_ref[...] = total
    for z in range(NZ):
        out_ref[z, 0:UNIT, :] = sum_ref[z * UNIT : (z + 1) * UNIT, :]
        out_ref[z, UNIT:32, :] = jnp.zeros((32 - UNIT, 128), F32)
    out_ref[:, 32:56, :] = table_ref[...]


def lon_sum(got_ref, out_ref, table_ref, sum_ref):
    total = got_ref[0]
    for z in range(1, NZ):
        total = total + got_ref[z]
    sum_ref[...] = total
    for p in range(PLANE):
        out_ref[p] = sum_ref[0:32, :]
    for block in range(2):
        for h in range(HEADS):
            row = 32 + block * 2 * HEADS + h
            table_ref[block, 0, h, :, 0:128] = sum_ref[row : row + 1, :]
            table_ref[block, 0, h, :, 128:TSHARE] = sum_ref[row + HEADS : row + HEADS + 1, 0 : TSHARE - 128]


def unpack(scale, got_ref, qkv_ref, proj_ref, up_ref, down_ref, wide_ref):
    for tile in range(36):
        block, group, lane = tile // 18, tile // 6 % 3, tile % 6
        lanes = slice(lane * 128, lane * 128 + 128)
        if tile < 32:
            to = tile % 2 * SHARE
            wide_ref[block, group, 0:SHARE, lanes] = got_ref[tile // 2, to : to + SHARE, :] * scale
        else:
            for quarter in range(4):
                wide_ref[block, group, quarter * 3 : quarter * 3 + 3, lanes] = (
                    got_ref[(tile - 32) * 4 + quarter, 24:27, :] * scale
                )
    for block in range(2):
        for row in range(SHARE):
            at = slice(row, row + 1)
            qkv_ref[row, block : block + 1, :] = wide_ref[block, 0, at, 0 : 3 * CH]
            proj_ref[row, block : block + 1, :] = wide_ref[block, 0, at, 3 * CH : 4 * CH]
            up_ref[row, block : block + 1, :] = wide_ref[block, 1, at, :]
        for m in range(HID // CH):
            down_ref[block, m * SHARE : (m + 1) * SHARE, :] = wide_ref[
                block, 2, 0:SHARE, m * CH : (m + 1) * CH
            ]


def struct(*shape):
    return jax.ShapeDtypeStruct(shape, F32)


def vmem(*shape):
    return pltpu.VMEM(shape, F32)


def whole(*shape):
    return pl.BlockSpec(shape, lambda i: (0,) * len(shape))


def part_of(block, *shape):
    return pl.BlockSpec((None,) + shape, lambda i: (block,) + (0,) * len(shape))


def weight_specs(block):
    return [
        part_of(block, CH, 3 * CH),
        part_of(block, CH, CH),
        part_of(block, CH, HID),
        part_of(block, CH, HID),
    ]


def table_spec(block):
    return part_of(block, 1, HEADS, 1, POS)


def call(body, in_specs, outs, scratch, cost=0, mib=28, far=0):
    near = [whole(*o.shape) for o in outs[: len(outs) - far]]
    return pl.pallas_call(
        body,
        grid=(1,),
        in_specs=in_specs,
        out_specs=near + [HBM] * far,
        out_shape=outs,
        scratch_shapes=scratch,
        compiler_params=params(mib),
        cost_estimate=pl.CostEstimate(flops=cost, bytes_accessed=4 * 2**20, transcendentals=0),
    )


SMEM = pl.BlockSpec(memory_space=pltpu.SMEM)
HBM = pl.BlockSpec(memory_space=pltpu.HBM)
FLAT = 3456


def shifted(block, axis, distance):
    devices = range(lax.axis_size(axis))
    route = [((i - distance) % len(devices), i) for i in devices]
    return lax.ppermute(block, axis, route)


def shifted_plane(block, levels, rows):
    size = lax.axis_size("lev")
    count = lax.axis_size("lat")
    route = [
        (lat * size + lev, (lat + rows) % count * size + (lev + levels) % size)
        for lat in range(count)
        for lev in range(size)
    ]
    return lax.ppermute(block, ("lat", "lev"), route)


def exchange(pieces, step, side):
    held = [pieces[0]] + [
        shifted_plane(piece, step * dlev, step * dlat)
        for piece, (dlev, dlat) in zip(pieces[1:], MOVES[1:])
    ]
    return held + [shifted(jnp.stack([piece[side] for piece in held]), "lon", step)]


def swap_cores(v):
    return lax.ppermute(v, "lon", [(i, i ^ 1) for i in range(lax.axis_size("lon"))])


def local(inputs, cotangent, qkv_weight, proj_weight, up_weight, down_weight, bias_table, lat_mask):
    place = place_matrix()
    x = inputs.transpose(1, 2, 0, 3)
    cot = cotangent.transpose(1, 2, 0, 3)
    table = bias_table.transpose(0, 1, 3, 2, 4)
    weights = (qkv_weight, proj_weight, up_weight, down_weight.transpose(0, 2, 1))
    grid_spec = whole(ROWS, COLS, LEVS, CH)
    wide_scratch = [vmem(8, FLAT), vmem(8 * CELLS, UPLANES)]
    half = (2, WIDE, 128)
    *pieces, qkv, attention, attended, mid, pre = call(
        first_forward,
        [SMEM] + [HBM] * 8,
        [struct(*half)] * 4
        + [
            struct(TOK, 3 * CH),
            struct(STACK, TOK),
            struct(TOK, CH),
            struct(TOK, CH),
            struct(TOK, HID),
        ],
        [
            vmem(ROWS, COLS, LEVS, CH),
            vmem(ROWS, COLS, LEVS, CH),
            vmem(CH, 3 * CH),
            vmem(CH, CH),
            vmem(CH, HID),
            vmem(CH, HID),
            vmem(1, HEADS, 1, POS),
            pltpu.VMEM((UPLANES, UPLANES), BF16),
            vmem(3, TOK, 128),
        ]
        + wide_scratch
        + [
            vmem(STACK, TOK),
            vmem(TOK, 3 * CH),
            vmem(STACK, TOK),
            vmem(TOK, CH),
            vmem(TOK, CH),
            vmem(TOK, HID),
            pltpu.SemaphoreType.DMA((8,)),
            pltpu.SemaphoreType.DMA((5,)),
        ],
        cost=500_000_000,
        mib=60,
        far=5,
    )(lat_mask, x, cot, *weights, table, place)
    (bias_second,) = call(
        spread_bias,
        [table_spec(1), whole(UPLANES, UPLANES)],
        [struct(STACK, TOK)],
        wide_scratch,
        cost=200_000_000,
    )(table, place)
    held = exchange(pieces, -1, 0)
    around = (4, WIDE, 128)
    back_half = (2, THIN, 128)
    back_around = (4, THIN, 128)
    factors = [
        struct(STACK, TOK),
        struct(TOK, CH),
        struct(TOK, CH),
        struct(TOK, CH),
        struct(TOK, HID),
        struct(TOK, CH),
        struct(TOK, HID),
        struct(TOK, CH),
        struct(TOK, 3 * CH),
    ]
    second = call(
        second_pass,
        [SMEM] + [whole(*half)] * 4 + [whole(*around)] + weight_specs(1) + [whole(STACK, TOK)],
        [struct(*back_half)] * 4 + factors,
        [vmem(3, TOK, 128)],
        cost=1_000_000_000,
    )(lat_mask, *held, *weights, bias_second)
    back_pieces, saved = second[:4], second[4:]
    keep2, send2 = call(
        second_gradients,
        [whole(*f.shape) for f in factors] + [whole(UPLANES, UPLANES)],
        [struct(BUF, HID), struct(BUF, HID)],
        wide_scratch + [vmem(GROUPS, CH, HID)],
        cost=500_000_000,
    )(*saved, place)
    back_held = exchange(back_pieces, 1, 1)
    got2 = swap_cores(send2)
    dmid, dqkv, keep1, send1 = call(
        first_backward,
        [grid_spec]
        + [whole(*back_half)] * 4
        + [whole(*back_around)]
        + weight_specs(0)[1:]
        + [
            whole(TOK, 3 * CH),
            whole(STACK, TOK),
            whole(TOK, CH),
            whole(TOK, CH),
            whole(TOK, HID),
            whole(UPLANES, UPLANES),
        ],
        [struct(TOK, CH), struct(TOK, 3 * CH), struct(BUF, HID), struct(BUF, HID)],
        [vmem(3, TOK, 128)] + wide_scratch + [vmem(GROUPS, CH, HID), vmem(STACK, TOK)],
        cost=1_000_000_000,
    )(
        x, *back_held, *weights[1:],
        qkv, attention, attended, mid, pre, place,
    )
    (grad_input,) = call(
        input_gradient,
        [grid_spec, weight_specs(0)[0], whole(TOK, CH), whole(TOK, 3 * CH)],
        [struct(ROWS, COLS, LEVS, CH)],
        [vmem(3, TOK, 128)],
        cost=100_000_000,
    )(x, weights[0], dmid, dqkv)
    got1 = swap_cores(send1)
    for_plane, table_part = call(
        pair_sum,
        [whole(BUF, HID)] * 4,
        [struct(PLANE, NZ * UNIT, 128), struct(NZ, 24, 128)],
        [vmem(2, BUF, HID)],
    )(keep1, got1, keep2, got2)
    plane_got = lax.all_to_all(for_plane, ("lat", "lev"), 0, 0, tiled=True)
    (for_lon,) = call(
        plane_sum,
        [whole(PLANE, NZ * UNIT, 128), whole(NZ, 24, 128)],
        [struct(NZ, 56, 128)],
        [vmem(NZ * UNIT, 128)],
    )(plane_got, table_part)
    core_groups = [[z * 2 + c for z in range(NZ)] for c in range(2)]
    lon_got = lax.all_to_all(
        for_lon, "lon", 0, 0, axis_index_groups=core_groups, tiled=True
    )
    copies, grad_table = call(
        lon_sum,
        [whole(NZ, 56, 128)],
        [struct(PLANE, 32, 128), struct(2, 1, HEADS, 1, TSHARE)],
        [vmem(56, 128)],
    )(lon_got)
    shares = lax.all_to_all(copies, ("lat", "lev"), 0, 0, tiled=True)
    tokens = TOK * lax.axis_size("lon") * lax.axis_size("lat") * lax.axis_size("lev")
    grad_qkv, grad_proj, grad_up, grad_down = call(
        lambda *refs: unpack(float(tokens) ** (-0.5), *refs),
        [whole(PLANE, 32, 128)],
        [
            struct(SHARE, 2, 3 * CH),
            struct(SHARE, 2, CH),
            struct(SHARE, 2, HID),
            struct(2, 48, CH),
        ],
        [vmem(2, GROUPS, 16, HID)],
    )(shares)
    return (
        grad_input.transpose(2, 0, 1, 3),
        grad_qkv.transpose(1, 0, 2),
        grad_proj.transpose(1, 0, 2),
        grad_up.transpose(1, 0, 2),
        grad_down,
        grad_table.transpose(0, 1, 3, 2, 4),
    )


def solution(mesh):
    in_specs = (
        P("lev", "lat", "lon", None),
        P("lev", "lat", "lon", None),
        P(),
        P(),
        P(),
        P(),
        P(None, "lev", "lat", None, None),
        P(),
    )
    out_specs = (
        P("lev", "lat", "lon", None),
        P(None, "lon", None),
        P(None, "lon", None),
        P(None, "lon", None),
        P(None, "lon", None),
        P(None, "lev", "lat", None, "lon"),
    )
    return jax.shard_map(local, mesh=mesh, in_specs=in_specs, out_specs=out_specs, check_vma=False)
```

```python
import jax
import jax.numpy as jnp
import numpy as np
from jax import lax
from jax.experimental import pallas as pl
from jax.experimental.pallas import tpu as pltpu
from jax.sharding import PartitionSpec as P

F32 = jnp.float32
BF16 = jnp.bfloat16

HEADS = 6
HEAD = 32
CH = 192
HID = 768
LEVS = 2
ROWS = 6
COLS = 12
CELLS = LEVS * ROWS
TOK = CELLS * COLS
STACK = HEADS * TOK
SPAN = 2 * COLS - 1
POS = 3312
CHUNK = ROWS * SPAN
UPLANES = 384
NEGATIVE = -10000.0
SCALE = HEAD ** (-0.5)

NZ = 8
SHARE = 12
GROUPS = 3
GROWS = NZ * GROUPS * SHARE
TROWS = 24
BUF = GROWS + TROWS
TSHARE = POS // 16
PLANE = 16
UNIT = 27
TABLE_ROWS = 2 * HEADS
LON_ROWS = 56

NN = ((1,), (0,))
NT = ((1,), (1,))
TN = ((0,), (0,))


def params(mib=28):
    return pltpu.CompilerParams(vmem_limit_bytes=mib * 1024 * 1024)


def halves(v):
    top = v.astype(BF16)
    return top, (v - top.astype(F32)).astype(BF16)


def thirds(v):
    top = v.astype(BF16)
    rest = v - top.astype(F32)
    mid = rest.astype(BF16)
    return top, mid, (rest - mid.astype(F32)).astype(BF16)


def dot(a, b, dims):
    return lax.dot_general(a, b, (dims, ((), ())), preferred_element_type=F32)


def dot3(a, b, dims):
    return dot(a[0], b[0], dims) + (dot(a[0], b[1], dims) + dot(a[1], b[0], dims))


def exact_dot(v, one_hot, dims):
    a, b, c = thirds(v)
    return (dot(a, one_hot, dims) + dot(b, one_hot, dims)) + dot(c, one_hot, dims)


def norm(v):
    centered = v - jnp.mean(v, axis=-1, keepdims=True)
    inv = lax.rsqrt(jnp.mean(centered * centered, axis=-1, keepdims=True) + 1e-05)
    return centered * inv, inv


def norm_back(d, normed, inv):
    return inv * (
        d
        - jnp.mean(d, axis=-1, keepdims=True)
        - normed * jnp.mean(d * normed, axis=-1, keepdims=True)
    )


ERF_TOP = (
    0.00022905065861350646,
    0.0034082910107109506,
    0.050955695062380861,
    0.18520832239976145,
    1.128379143519084,
)
ERF_LOW = (
    -1.1791602954361697e-7,
    0.000023547966471313185,
    0.0010179625278914885,
    0.014070470171167667,
    0.11098505178285362,
    0.49746925110067538,
    1.0,
)


def erf(v):
    v = jnp.clip(v, -3.832506856900711, 3.832506856900711)
    sq = v * v
    top = jnp.full_like(v, ERF_TOP[0])
    for term in ERF_TOP[1:]:
        top = top * sq + term
    low = jnp.full_like(v, ERF_LOW[0])
    for term in ERF_LOW[1:]:
        low = low * sq + term
    return v * top / low


def half_cdf(pre):
    return 0.5 + 0.5 * erf(pre * (0.5**0.5))


def head_rows(dtype):
    lane = lax.broadcasted_iota(jnp.int32, (1, CH), 1)
    return [
        jnp.where((lane >= h * HEAD) & (lane < (h + 1) * HEAD), 1.0, 0.0).astype(dtype)
        for h in range(HEADS)
    ]


def stack_heads(pair):
    rows = head_rows(BF16)
    return tuple(jnp.concatenate([part * rows[h] for h in range(HEADS)], axis=0) for part in pair)


def turned(v, lanes):
    return jnp.concatenate([v[:, CH - lanes :], v[:, : CH - lanes]], axis=1)


def head_products(q, k):
    rows = head_rows(BF16)
    pairs = [rows[2 * r] + rows[2 * r + 1] for r in range(3)]
    q64, q128 = turned(q[1], 2 * HEAD), turned(q[0], 4 * HEAD)
    k64, k128 = turned(k[0], 2 * HEAD), turned(k[1], 4 * HEAD)
    out = []
    for r in range(3):
        right = k[0] * pairs[r] + k64 * pairs[(r + 1) % 3] + k128 * pairs[(r + 2) % 3]
        left = [
            q[0] * rows[h] + q64 * rows[(h + 2) % HEADS] + q128 * rows[(h + 4) % HEADS]
            for h in (2 * r, 2 * r + 1)
        ]
        out.append(dot(jnp.concatenate(left, axis=0), right, NT))
    return jnp.concatenate(out, axis=0)


def head_sums(p, v):
    half = CH // 2
    lane = lax.broadcasted_iota(jnp.int32, (1, CH), 1)
    lane = jnp.where(lane < half, lane, lane - half)
    out = []
    for group in range(2):
        lanes = slice(group * half, (group + 1) * half)
        rows = slice(group * STACK // 2, (group + 1) * STACK // 2)
        both = dot(p[0][rows], jnp.concatenate([v[0][:, lanes], v[1][:, lanes]], axis=1), NN)
        rest = dot(p[1][rows], v[0][:, lanes], NN)
        total, more = 0.0, 0.0
        for i in range(HEADS // 2):
            mine = jnp.where((lane >= i * HEAD) & (lane < (i + 1) * HEAD), 1.0, 0.0)
            total = total + both[i * TOK : (i + 1) * TOK] * mine
            more = more + rest[i * TOK : (i + 1) * TOK] * mine[:, 0:half]
        out.append(total[:, 0:half] + total[:, half:CH] + more)
    return jnp.concatenate(out, axis=1)


def place_matrix():
    mat = np.zeros((UPLANES, UPLANES), np.float32)
    for kl in range(LEVS):
        for kr in range(ROWS):
            for p in range(SPAN):
                mat[kl * CHUNK + kr * SPAN + p, p * CELLS + kr * LEVS + kl] = 1.0
    return jnp.asarray(mat, BF16)


def chunk_start(ql, kl, qr):
    return ((ql * LEVS + kl) * ROWS + qr) * CHUNK


def expand_bias(table_ref, place_ref, flat_ref, up_ref, bias_ref):
    flat_ref[...] = jnp.zeros_like(flat_ref)
    for h in range(HEADS):
        flat_ref[h : h + 1, 0:POS] = table_ref[0, h]
    lane = lax.broadcasted_iota(jnp.int32, (8, UPLANES), 1)
    for ql in range(LEVS):
        for qr in range(ROWS):
            g = qr * LEVS + ql
            row = jnp.zeros((8, UPLANES), F32)
            for kl in range(LEVS):
                start = chunk_start(ql, kl, qr)
                base = start // 128 * 128
                window = flat_ref[:, base : base + UPLANES]
                turn = (kl * CHUNK - (start - base)) % UPLANES
                if turn:
                    window = pltpu.roll(window, turn, 1)
                row = jnp.where((lane >= kl * CHUNK) & (lane < (kl + 1) * CHUNK), window, row)
            up_ref[g * 8 : (g + 1) * 8, :] = row
    ups = exact_dot(up_ref[...], place_ref[...], NN)
    for h in range(HEADS):
        rows = jnp.concatenate([ups[g * 8 + h : g * 8 + h + 1] for g in range(CELLS)], axis=0)
        for qc in range(COLS):
            turn = (-(COLS - 1 - qc) * CELLS) % UPLANES
            moved = pltpu.roll(rows, turn, 1) if turn else rows
            bias_ref[h * TOK + qc * CELLS : h * TOK + (qc + 1) * CELLS, :] = moved[:, 0:TOK]


def collect_table(dscore_ref, place_ref, up_ref, flat_ref):
    up_ref[...] = jnp.zeros_like(up_ref)
    for h in range(HEADS):
        total = jnp.zeros((CELLS, UPLANES), F32)
        for qc in range(COLS):
            block = dscore_ref[h * TOK + qc * CELLS : h * TOK + (qc + 1) * CELLS, :]
            block = jnp.concatenate([block, jnp.zeros((CELLS, UPLANES - TOK), F32)], axis=1)
            turn = (COLS - 1 - qc) * CELLS
            total = total + (pltpu.roll(block, turn, 1) if turn else block)
        for g in range(CELLS):
            up_ref[g * 8 + h : g * 8 + h + 1, :] = total[g : g + 1]
    raw = exact_dot(up_ref[...], place_ref[...], NT)
    flat_ref[...] = jnp.zeros_like(flat_ref)
    lane = lax.broadcasted_iota(jnp.int32, (8, UPLANES), 1)
    for ql in range(LEVS):
        for qr in range(ROWS):
            g = qr * LEVS + ql
            row = raw[g * 8 : (g + 1) * 8]
            for kl in range(LEVS):
                start = chunk_start(ql, kl, qr)
                base = start // 128 * 128
                shift = start - base
                turn = (shift - kl * CHUNK) % UPLANES
                moved = pltpu.roll(row, turn, 1) if turn else row
                keep = (lane >= shift) & (lane < shift + CHUNK)
                window = flat_ref[:, base : base + UPLANES]
                flat_ref[:, base : base + UPLANES] = jnp.where(keep, moved, window)


def window_masks(mask_ref, second):
    lev = lax.axis_index("lev")
    lat = lax.axis_index("lat")
    last_lev = lev == lax.axis_size("lev") - 1
    last_lat = lat == lax.axis_size("lat") - 1
    key_col = lax.broadcasted_iota(jnp.int32, (1, TOK), 1)
    key_row = lax.div(lax.rem(key_col, CELLS), LEVS)
    key_bias = jnp.zeros((1, TOK), F32)
    count = ROWS * lax.axis_size("lat")
    for r in range(ROWS):
        place = lat * ROWS + r
        if second:
            place = lax.rem(place + ROWS // 2, count)
        value = NEGATIVE * (1.0 - mask_ref[place].astype(F32))
        key_bias = jnp.where(key_row == r, value, key_bias)
    if not second:
        return key_bias, None

    def label(tokens):
        level = jnp.where(lax.rem(tokens, LEVS) >= LEVS // 2, 2, 0)
        row = jnp.where(lax.rem(tokens, CELLS) >= CELLS // 2, 1, 0)
        return level * last_lev.astype(jnp.int32) + row * last_lat.astype(jnp.int32)

    query = label(lax.broadcasted_iota(jnp.int32, (TOK, 1), 0))
    pair = jnp.where(query == label(key_col), 0.0, NEGATIVE).astype(F32)
    return key_bias, pair


def add_masks(scores, key_bias, pair):
    scores = scores + key_bias
    if pair is None:
        return scores
    return jnp.concatenate([scores[h * TOK : (h + 1) * TOK] + pair for h in range(HEADS)], axis=0)


def scaled_parts(qkv):
    return qkv[:, 0:CH] * SCALE, qkv[:, CH : 2 * CH], qkv[:, 2 * CH : 3 * CH]


def project(x, wq):
    normed, inv = norm(x)
    return normed, inv, dot3(halves(normed), wq, NN)


def attend(qkv, bias, key_bias, pair):
    q, k, v = scaled_parts(qkv)
    scores = add_masks(head_products(halves(q), halves(k)) + bias, key_bias, pair)
    grown = jnp.exp(scores - jnp.max(scores, axis=-1, keepdims=True))
    weights = grown * (1.0 / jnp.sum(grown, axis=-1, keepdims=True))
    return weights, head_sums(halves(weights), halves(v))


SIDE = COLS // 2
MAIN = ROWS // 2 * SIDE
WIDE = 56
THIN = 32
REST = CH - 128


MOVES = ((0, 0), (1, 0), (0, 1), (1, 1))


def six_rows(lev, j, k):
    for rr in range(ROWS // 2):
        yield rr, k * SIDE * CELLS + (j * (ROWS // 2) + rr) * LEVS + lev


def spread_pair(grid, out_refs):
    for (dlev, dj), out_ref in zip(MOVES, out_refs):
        for k in range(2):
            for rr, start in six_rows(1 - dlev, 1 - dj, k):
                rows = pl.ds(start, SIDE, stride=CELLS)
                for part, to in ((0, 0), (2, MAIN), (1, 2 * MAIN)):
                    out_ref[k, to + rr * SIDE : to + (rr + 1) * SIDE, :] = grid[part, rows, :]


def gather_pair(grid, own_refs, around_ref):
    for piece, (dlev, dj) in enumerate(MOVES):
        for k in range(2):
            ref, slot = (own_refs[piece], 1) if k == 0 else (around_ref, piece)
            for rr, start in six_rows(dlev, dj, k):
                rows = pl.ds(start, SIDE, stride=CELLS)
                for part, at in ((0, 0), (2, MAIN), (1, 2 * MAIN)):
                    grid[part, rows, :] = ref[slot, at + rr * SIDE : at + (rr + 1) * SIDE, :]


def spread_one(grid, out_refs):
    low = lax.broadcasted_iota(jnp.int32, (SIDE // 2, 128), 1) < REST
    for (dlev, dj), out_ref in zip(MOVES, out_refs):
        for k in range(2):
            for rr, start in six_rows(dlev, dj, k):
                rows = pl.ds(start, SIDE, stride=CELLS)
                out_ref[k, rr * SIDE : (rr + 1) * SIDE, :] = grid[0, rows, :]
                one = grid[1, pl.ds(start, SIDE // 2, stride=CELLS), :]
                two = grid[1, pl.ds(start + SIDE // 2 * CELLS, SIDE // 2, stride=CELLS), :]
                to = MAIN + rr * (SIDE // 2)
                out_ref[k, to : to + SIDE // 2, :] = jnp.where(low, one, pltpu.roll(two, REST, 1))


def gather_one(grid, own_refs, around_ref):
    for piece, (dlev, dj) in enumerate(MOVES):
        for k in range(2):
            ref, slot = (own_refs[piece], 0) if k == 1 else (around_ref, piece)
            for rr, start in six_rows(1 - dlev, 1 - dj, k):
                rows = pl.ds(start, SIDE, stride=CELLS)
                grid[0, rows, :] = ref[slot, rr * SIDE : (rr + 1) * SIDE, :]
                at = MAIN + rr * (SIDE // 2)
                both = ref[slot, at : at + SIDE // 2, :]
                grid[1, pl.ds(start, SIDE // 2, stride=CELLS), :] = both
                rows = pl.ds(start + SIDE // 2 * CELLS, SIDE // 2, stride=CELLS)
                grid[1, rows, :] = pltpu.roll(both, REST, 1)


def load_first(grid):
    return jnp.concatenate([grid[0], grid[1][:, 0:REST]], axis=1)


def load_second(grid):
    return jnp.concatenate([grid[2], grid[1][:, REST:128]], axis=1)


def store_first(grid, value):
    grid[0] = value[:, 0:128]
    grid[1, :, 0:REST] = value[:, 128:CH]


def load_window(x_ref, grid, second=False):
    head, at = (2, REST) if second else (0, 0)
    for r in range(ROWS):
        for c in range(COLS):
            rows = slice(c * CELLS + r * LEVS, c * CELLS + (r + 1) * LEVS)
            cell = x_ref[r, c]
            grid[head, rows, :] = cell[:, 0:128]
            grid[1, rows, at : at + REST] = cell[:, 128:CH]


def save_window(grid, out_ref):
    for r in range(ROWS):
        for c in range(COLS):
            rows = slice(c * CELLS + r * LEVS, c * CELLS + (r + 1) * LEVS)
            out_ref[r, c, :, 0:128] = grid[0, rows, :]
            out_ref[r, c, :, 128:CH] = grid[1, rows, 0:REST]


def first_forward(
    mask_hbm, x_hbm, cot_hbm, wq_hbm, wp_hbm, wu_hbm, wd_hbm, table_hbm, place_hbm,
    own_ref, lev_ref, lat_ref, both_ref, qkv_hbm, weights_hbm, attended_hbm, mid_hbm, pre_hbm,
    mask_ref, x_ref, cot_ref, wq_ref, wp_ref, wu_ref, wd_ref, table_ref, place_ref,
    grid_ref, flat_ref, up_ref, bias_ref, qkv_ref, weights_ref, attended_ref, mid_ref, pre_ref, sems,
    out_sems,
):
    pairs = (
        (x_hbm, x_ref),
        (wq_hbm.at[0], wq_ref),
        (table_hbm.at[0], table_ref),
        (place_hbm, place_ref),
        (mask_hbm, mask_ref),
        (wp_hbm.at[0], wp_ref),
        (wu_hbm.at[0], wu_ref),
        (wd_hbm.at[0], wd_ref),
        (cot_hbm, cot_ref),
    )
    copies = [pltpu.make_async_copy(*pair, sems.at[i]) for i, pair in enumerate(pairs)]
    for copy in copies:
        copy.start()
    copies[0].wait()
    load_window(x_ref, grid_ref)
    x = load_first(grid_ref)
    copies[1].wait()
    for copy in copies[2:5]:
        copy.wait()
    expand_bias(table_ref, place_ref, flat_ref, up_ref, bias_ref)
    key_bias, _ = window_masks(mask_ref, False)
    _, _, qkv = project(x, halves(wq_ref[...]))
    weights, attended = attend(qkv, bias_ref[...], key_bias, None)
    saved = []

    def save(value, ref, to):
        ref[...] = value
        saved.append(pltpu.make_async_copy(ref, to, out_sems.at[len(saved)]))
        saved[-1].start()

    save(qkv, qkv_ref, qkv_hbm)
    save(weights, weights_ref, weights_hbm)
    save(attended, attended_ref, attended_hbm)
    for copy in copies[5:]:
        copy.wait()
    mid = x + dot3(halves(attended), halves(wp_ref[...]), NN)
    save(mid, mid_ref, mid_hbm)
    normed, _ = norm(mid)
    pre = dot3(halves(normed), halves(wu_ref[...]), NN)
    save(pre, pre_ref, pre_hbm)
    hidden = pre * half_cdf(pre)
    load_window(cot_ref, grid_ref, True)
    store_first(grid_ref, mid + dot3(halves(hidden), halves(wd_ref[...]), NT))
    for copy in saved:
        copy.wait()
    spread_pair(grid_ref, (own_ref, lev_ref, lat_ref, both_ref))


def gelu_slope(pre, cdf):
    return cdf + pre * jnp.exp(-0.5 * pre * pre) * ((2.0 * np.pi) ** (-0.5))


def mlp_backward(g, slope, normed, inv, wu, wd):
    dpre = dot3(halves(g), wd, NN) * slope
    dnormed = dot3(halves(dpre), wu, NT)
    return dpre, g + norm_back(dnormed, normed, inv)


def attention_backward(dmid, qkv, weights, wp):
    q, k, v = scaled_parts(qkv)
    dattended = dot3(halves(dmid), wp, NT)
    dhalves = halves(dattended)
    dstack = stack_heads(dhalves)
    dweights = head_products(dhalves, halves(v))
    inner = jnp.sum(dweights * weights, axis=-1, keepdims=True)
    dscores = weights * (dweights - inner)
    ds = halves(dscores)
    dq = head_sums(ds, halves(k)) * SCALE
    dk = dot3(ds, stack_heads(halves(q)), TN)
    dv = dot3(halves(weights), dstack, TN)
    return dscores, jnp.concatenate([dq, dk, dv], axis=1)


def pack_gradients(keep_ref, send_ref, wide_ref, dqkv, dproj, dup, ddown, flat_ref):
    core = lax.rem(lax.axis_index("lon"), 2)
    wide_ref[0, :, 0 : 3 * CH] = dqkv
    wide_ref[0, :, 3 * CH : 4 * CH] = dproj
    wide_ref[1] = dup
    for share in range(2 * NZ):
        rows = [
            ddown[share * 48 + m * SHARE : share * 48 + (m + 1) * SHARE] for m in range(HID // CH)
        ]
        wide_ref[2, share * SHARE : (share + 1) * SHARE, :] = jnp.concatenate(rows, axis=1)
    even = core == 0
    for z in range(NZ):
        for group in range(GROUPS):
            first = wide_ref[group, 2 * SHARE * z : 2 * SHARE * z + SHARE, :]
            second = wide_ref[group, 2 * SHARE * z + SHARE : 2 * SHARE * (z + 1), :]
            rows = slice((z * GROUPS + group) * SHARE, (z * GROUPS + group + 1) * SHARE)
            keep_ref[rows, :] = jnp.where(even, first, second)
            send_ref[rows, :] = jnp.where(even, second, first)
    for ref in (keep_ref, send_ref):
        ref[GROWS:BUF, :] = jnp.zeros((TROWS, HID), F32)
    for z in range(NZ):
        first = table_share(flat_ref, 2 * z)
        second = table_share(flat_ref, 2 * z + 1)
        rows = slice(GROWS + z // 3 * 8, GROWS + z // 3 * 8 + 8)
        lanes = slice(z % 3 * 256, z % 3 * 256 + 256)
        keep_ref[rows, lanes] = jnp.where(even, first, second)
        send_ref[rows, lanes] = jnp.where(even, second, first)


def table_share(flat_ref, share):
    start = share * TSHARE
    base = start // 128 * 128
    window = flat_ref[:, base : base + UPLANES]
    if start - base:
        window = pltpu.roll(window, UPLANES - (start - base), 1)
    return window[:, 0:256]


def second_pass(
    own_ref, lev_ref, lat_ref, both_ref, around_ref, wq0_ref, wq1_ref, wp0_ref, wp1_ref, wu0_ref,
    wu1_ref, wd0_ref, wd1_ref, bias_ref, key_ref, pair_ref,
    back_own_ref, back_lev_ref, back_lat_ref, back_both_ref, dscores_ref, normed_ref, attended_ref, hnormed_ref, hidden_ref,
    g_ref, dpre_ref, dmid_ref, dqkv_ref,
    grid_ref,
):
    gather_pair(grid_ref, (own_ref, lev_ref, lat_ref, both_ref), around_ref)
    x = load_first(grid_ref)
    g = load_second(grid_ref)
    wq, wp = (wq0_ref[...], wq1_ref[...]), (wp0_ref[...], wp1_ref[...])
    wu, wd = (wu0_ref[...], wu1_ref[...]), (wd0_ref[...], wd1_ref[...])
    key_bias, pair = key_ref[0:1], pair_ref[...]
    normed, inv, qkv = project(x, wq)
    weights, attended = attend(qkv, bias_ref[...], key_bias, pair)
    normed_ref[...] = normed
    attended_ref[...] = attended
    mid = x + dot3(halves(attended), wp, NN)
    hnormed, hinv = norm(mid)
    hnormed_ref[...] = hnormed
    pre = dot3(halves(hnormed), wu, NN)
    cdf = half_cdf(pre)
    hidden_ref[...] = pre * cdf
    g_ref[...] = g
    dpre, dmid = mlp_backward(g, gelu_slope(pre, cdf), hnormed, hinv, wu, wd)
    dpre_ref[...] = dpre
    dmid_ref[...] = dmid
    dscores, dqkv = attention_backward(dmid, qkv, weights, wp)
    dscores_ref[...] = dscores
    dqkv_ref[...] = dqkv
    dx = dmid + norm_back(dot3(halves(dqkv), wq, NT), normed, inv)
    store_first(grid_ref, dx)
    spread_one(grid_ref, (back_own_ref, back_lev_ref, back_lat_ref, back_both_ref))


def second_gradients(
    dscores_ref, normed_ref, attended_ref, hnormed_ref, hidden_ref, g_ref, dpre_ref, dmid_ref,
    dqkv_ref, place_ref,
    keep_ref, send_ref,
    flat_ref, up_ref, wide_ref,
):
    collect_table(dscores_ref, place_ref, up_ref, flat_ref)
    pack_gradients(
        keep_ref, send_ref, wide_ref,
        dot3(halves(normed_ref[...]), halves(dqkv_ref[...]), TN),
        dot3(halves(attended_ref[...]), halves(dmid_ref[...]), TN),
        dot3(halves(hnormed_ref[...]), halves(dpre_ref[...]), TN),
        dot3(halves(hidden_ref[...]), halves(g_ref[...]), TN),
        flat_ref,
    )


def first_backward(
    own_ref, lev_ref, lat_ref, both_ref, around_ref, wp0_ref, wp1_ref, wu0_ref, wu1_ref, wd0_ref,
    wd1_ref, slope_ref, hidden_ref, hnormed_ref, hinv_ref, normed_ref, qkv_ref, weights_ref,
    attended_ref, place_ref,
    dmid_ref, dqkv_ref, gkeep_ref, gsend_ref,
    grid_ref, flat_ref, up_ref, wide_ref, dscores_ref,
):
    gather_one(grid_ref, (own_ref, lev_ref, lat_ref, both_ref), around_ref)
    g = load_first(grid_ref)
    wp = (wp0_ref[...], wp1_ref[...])
    wu, wd = (wu0_ref[...], wu1_ref[...]), (wd0_ref[...], wd1_ref[...])
    hnormed = hnormed_ref[...]
    dpre, dmid = mlp_backward(g, slope_ref[...], hnormed, hinv_ref[...], wu, wd)
    dup = dot3(halves(hnormed), halves(dpre), TN)
    ddown = dot3(halves(hidden_ref[...]), halves(g), TN)
    dproj = dot3(halves(attended_ref[...]), halves(dmid), TN)
    dscores, dqkv = attention_backward(dmid, qkv_ref[...], weights_ref[...], wp)
    dscores_ref[...] = dscores
    dmid_ref[...] = dmid
    dqkv_ref[...] = dqkv
    collect_table(dscores_ref, place_ref, up_ref, flat_ref)
    pack_gradients(
        gkeep_ref, gsend_ref, wide_ref,
        dot3(halves(normed_ref[...]), halves(dqkv), TN), dproj, dup, ddown, flat_ref,
    )


def first_prepare(
    x_ref, mid_ref, pre_ref, wp_ref, wu_ref, wd_ref,
    wp0_ref, wp1_ref, wu0_ref, wu1_ref, wd0_ref, wd1_ref, slope_ref, hidden_ref, hnormed_ref, hinv_ref,
    normed_ref,
    grid_ref,
):
    split_into(((wp_ref, wp0_ref, wp1_ref), (wu_ref, wu0_ref, wu1_ref), (wd_ref, wd0_ref, wd1_ref)))
    pre = pre_ref[...]
    cdf = half_cdf(pre)
    slope_ref[...] = gelu_slope(pre, cdf)
    hidden_ref[...] = pre * cdf
    hnormed_ref[...], hinv_ref[...] = norm(mid_ref[...])
    load_window(x_ref, grid_ref)
    normed_ref[...], _ = norm(load_first(grid_ref))


def split_into(triples):
    for ref, high_ref, low_ref in triples:
        high_ref[...], low_ref[...] = halves(ref[...])


def input_gradient(x_ref, wq_ref, dmid_ref, dqkv_ref, grad_ref, grid_ref):
    load_window(x_ref, grid_ref)
    normed, inv = norm(load_first(grid_ref))
    dnormed = dot3(halves(dqkv_ref[...]), halves(wq_ref[...]), NT)
    store_first(grid_ref, dmid_ref[...] + norm_back(dnormed, normed, inv))
    save_window(grid_ref, grad_ref)


def second_prepare(
    mask_ref, table_ref, place_ref, wq_ref, wp_ref, wu_ref, wd_ref,
    wq0_ref, wq1_ref, wp0_ref, wp1_ref, wu0_ref, wu1_ref, wd0_ref, wd1_ref, bias_ref, key_ref, pair_ref,
    flat_ref, up_ref,
):
    split_into(
        (
            (wq_ref, wq0_ref, wq1_ref),
            (wp_ref, wp0_ref, wp1_ref),
            (wu_ref, wu0_ref, wu1_ref),
            (wd_ref, wd0_ref, wd1_ref),
        )
    )
    expand_bias(table_ref, place_ref, flat_ref, up_ref, bias_ref)
    key_bias, pair = window_masks(mask_ref, True)
    key_ref[...] = jnp.broadcast_to(key_bias, (8, TOK))
    pair_ref[...] = pair


def unit_parts(block):
    for tile in range(18):
        number = block * 18 + tile
        if number < 32:
            yield number // 2, number % 2 * SHARE, SHARE, tile, 0
        else:
            for quarter in range(4):
                yield (number - 32) * 4 + quarter, 2 * SHARE, SHARE // 4, tile, quarter * (SHARE // 4)


def table_place(z):
    return slice(GROWS + z // 3 * 8, GROWS + z // 3 * 8 + 8), slice(z % 3 * 256, z % 3 * 256 + 256)


def join(mine0_ref, theirs0_ref, mine1_ref, theirs1_ref, plane_ref, table_ref, sum_ref):
    for block, (mine_ref, theirs_ref) in enumerate(((mine0_ref, theirs0_ref), (mine1_ref, theirs1_ref))):
        sum_ref[...] = mine_ref[...] + theirs_ref[...]
        for z in range(NZ):
            for p, at, count, tile, start in unit_parts(block):
                start = (z * GROUPS + tile // 6) * SHARE + start
                lanes = slice(tile % 6 * 128, tile % 6 * 128 + 128)
                at = z * UNIT + at
                plane_ref[p, at : at + count, :] = sum_ref[start : start + count, lanes]
            table = sum_ref[table_place(z)]
            for half in range(2):
                to = block * TABLE_ROWS + half * HEADS
                table_ref[z, to : to + HEADS, :] = table[0:HEADS, half * 128 : half * 128 + 128]


def plane_sum(got_ref, table_ref, out_ref, sum_ref):
    total = got_ref[0]
    for p in range(1, PLANE):
        total = total + got_ref[p]
    sum_ref[...] = total
    used = UNIT + 2 * TABLE_ROWS
    for z in range(NZ):
        out_ref[z, 0:UNIT, :] = sum_ref[z * UNIT : (z + 1) * UNIT, :]
        out_ref[z, UNIT:used, :] = table_ref[z]
        out_ref[z, used:LON_ROWS, :] = jnp.zeros((LON_ROWS - used, 128), F32)


def lon_sum(got_ref, out_ref, table_ref, sum_ref):
    total = got_ref[0]
    for z in range(1, NZ):
        total = total + got_ref[z]
    sum_ref[...] = total
    for p in range(PLANE):
        out_ref[p] = sum_ref[0:32, :]
    for block in range(2):
        for h in range(HEADS):
            row = UNIT + block * TABLE_ROWS + h
            table_ref[block, 0, h, :, 0:128] = sum_ref[row : row + 1, :]
            row = row + HEADS
            table_ref[block, 0, h, :, 128:TSHARE] = sum_ref[row : row + 1, 0 : TSHARE - 128]


def unpack(scale, got_ref, qkv_ref, proj_ref, up_ref, down_ref, wide_ref):
    for block in range(2):
        for p, at, count, tile, to in unit_parts(block):
            lanes = slice(tile % 6 * 128, tile % 6 * 128 + 128)
            wide_ref[block, tile // 6, to : to + count, lanes] = got_ref[p, at : at + count, :] * scale
        for row in range(SHARE):
            at = slice(row, row + 1)
            qkv_ref[row, block : block + 1, :] = wide_ref[block, 0, at, 0 : 3 * CH]
            proj_ref[row, block : block + 1, :] = wide_ref[block, 0, at, 3 * CH : 4 * CH]
            up_ref[row, block : block + 1, :] = wide_ref[block, 1, at, :]
        for m in range(HID // CH):
            down_ref[block, m * SHARE : (m + 1) * SHARE, :] = wide_ref[
                block, 2, 0:SHARE, m * CH : (m + 1) * CH
            ]


WEIGHTS = ((CH, 3 * CH), (CH, CH), (CH, HID), (CH, HID))


def struct(*shape, dtype=F32):
    return jax.ShapeDtypeStruct(shape, dtype)


def vmem(*shape):
    return pltpu.VMEM(shape, F32)


def whole(*shape):
    return pl.BlockSpec(shape, lambda i: (0,) * len(shape))


def part_of(block, *shape):
    return pl.BlockSpec((None,) + shape, lambda i: (block,) + (0,) * len(shape))


def weight_specs(block):
    return [
        part_of(block, CH, 3 * CH),
        part_of(block, CH, CH),
        part_of(block, CH, HID),
        part_of(block, CH, HID),
    ]


def table_spec(block):
    return part_of(block, 1, HEADS, 1, POS)


def call(body, in_specs, outs, scratch, cost=0, mib=28, far=0):
    near = [whole(*o.shape) for o in outs[: len(outs) - far]]
    return pl.pallas_call(
        body,
        grid=(1,),
        in_specs=in_specs,
        out_specs=near + [HBM] * far,
        out_shape=outs,
        scratch_shapes=scratch,
        compiler_params=params(mib),
        cost_estimate=pl.CostEstimate(flops=cost, bytes_accessed=4 * 2**20, transcendentals=0),
    )


SMEM = pl.BlockSpec(memory_space=pltpu.SMEM)
HBM = pl.BlockSpec(memory_space=pltpu.HBM)
FLAT = 3456


def shifted(block, axis, distance):
    devices = range(lax.axis_size(axis))
    route = [((i - distance) % len(devices), i) for i in devices]
    return lax.ppermute(block, axis, route)


def shifted_plane(block, levels, rows):
    size = lax.axis_size("lev")
    count = lax.axis_size("lat")
    route = [
        (lat * size + lev, (lat + rows) % count * size + (lev + levels) % size)
        for lat in range(count)
        for lev in range(size)
    ]
    return lax.ppermute(block, ("lat", "lev"), route)


def exchange(pieces, step, side, first=None):
    held = [pieces[0]] + [
        shifted_plane(piece, step * dlev, step * dlat)
        for piece, (dlev, dlat) in zip(pieces[1:], MOVES[1:])
    ]
    edge = jnp.stack([piece[side] for piece in held])
    if first is not None:
        edge, first = lax.optimization_barrier((edge, first))
    return held + [shifted(edge, "lon", step)], first


def swap_cores(v):
    return lax.ppermute(v, "lon", [(i, i ^ 1) for i in range(lax.axis_size("lon"))])


def local(inputs, cotangent, qkv_weight, proj_weight, up_weight, down_weight, bias_table, lat_mask):
    place = place_matrix()
    x = inputs.transpose(1, 2, 0, 3)
    cot = cotangent.transpose(1, 2, 0, 3)
    table = bias_table.transpose(0, 1, 3, 2, 4)
    weights = (qkv_weight, proj_weight, up_weight, down_weight.transpose(0, 2, 1))
    grid_spec = whole(ROWS, COLS, LEVS, CH)
    wide_scratch = [vmem(8, FLAT), vmem(8 * CELLS, UPLANES)]
    half = (2, WIDE, 128)
    *pieces, qkv, attention, attended, mid, pre = call(
        first_forward,
        [HBM] * 9,
        [struct(*half)] * 4
        + [
            struct(TOK, 3 * CH),
            struct(STACK, TOK),
            struct(TOK, CH),
            struct(TOK, CH),
            struct(TOK, HID),
        ],
        [
            pltpu.SMEM((8 * ROWS,), jnp.int32),
            vmem(ROWS, COLS, LEVS, CH),
            vmem(ROWS, COLS, LEVS, CH),
            vmem(CH, 3 * CH),
            vmem(CH, CH),
            vmem(CH, HID),
            vmem(CH, HID),
            vmem(1, HEADS, 1, POS),
            pltpu.VMEM((UPLANES, UPLANES), BF16),
            vmem(3, TOK, 128),
        ]
        + wide_scratch
        + [
            vmem(STACK, TOK),
            vmem(TOK, 3 * CH),
            vmem(STACK, TOK),
            vmem(TOK, CH),
            vmem(TOK, CH),
            vmem(TOK, HID),
            pltpu.SemaphoreType.DMA((9,)),
            pltpu.SemaphoreType.DMA((5,)),
        ],
        cost=500_000_000,
        mib=60,
        far=5,
    )(lat_mask, x, cot, *weights, table, place)
    prepared = call(
        second_prepare,
        [SMEM, table_spec(1), whole(UPLANES, UPLANES)] + weight_specs(1),
        [struct(*shape, dtype=BF16) for shape in WEIGHTS for _ in range(2)]
        + [struct(STACK, TOK), struct(8, TOK), struct(TOK, TOK)],
        wide_scratch,
        cost=200_000_000,
    )(lat_mask, table, place, *weights)
    held, _ = exchange(pieces, -1, 0)
    around = (4, WIDE, 128)
    back_half = (2, THIN, 128)
    back_around = (4, THIN, 128)
    factors = [
        struct(STACK, TOK),
        struct(TOK, CH),
        struct(TOK, CH),
        struct(TOK, CH),
        struct(TOK, HID),
        struct(TOK, CH),
        struct(TOK, HID),
        struct(TOK, CH),
        struct(TOK, 3 * CH),
    ]
    second = call(
        second_pass,
        [whole(*half)] * 4
        + [whole(*around)]
        + [whole(*shape) for shape in WEIGHTS for _ in range(2)]
        + [whole(STACK, TOK), whole(8, TOK), whole(TOK, TOK)],
        [struct(*back_half)] * 4 + factors,
        [vmem(3, TOK, 128)],
        cost=1_000_000_000,
    )(*held, *prepared)
    back_pieces, saved = second[:4], second[4:]
    keep2, send2 = call(
        second_gradients,
        [whole(*f.shape) for f in factors] + [whole(UPLANES, UPLANES)],
        [struct(BUF, HID), struct(BUF, HID)],
        wide_scratch + [vmem(GROUPS, CH, HID)],
        cost=500_000_000,
    )(*saved, place)
    back_held, send2 = exchange(back_pieces, 1, 1, send2)
    pre, _ = lax.optimization_barrier((pre, back_pieces[0]))
    ready = [struct(*shape, dtype=BF16) for shape in WEIGHTS[1:] for _ in range(2)] + [
        struct(TOK, HID),
        struct(TOK, HID),
        struct(TOK, CH),
        struct(TOK, 1),
        struct(TOK, CH),
    ]
    first_ready = call(
        first_prepare,
        [grid_spec, whole(TOK, CH), whole(TOK, HID)] + weight_specs(0)[1:],
        ready,
        [vmem(3, TOK, 128)],
        cost=200_000_000,
    )(x, mid, pre, *weights[1:])
    send2, slope = lax.optimization_barrier((send2, first_ready[6]))
    first_ready = list(first_ready[:6]) + [slope] + list(first_ready[7:])
    got2 = swap_cores(send2)
    dmid, dqkv, keep1, send1 = call(
        first_backward,
        [whole(*back_half)] * 4
        + [whole(*back_around)]
        + [whole(*r.shape) for r in ready]
        + [
            whole(TOK, 3 * CH),
            whole(STACK, TOK),
            whole(TOK, CH),
            whole(UPLANES, UPLANES),
        ],
        [struct(TOK, CH), struct(TOK, 3 * CH), struct(BUF, HID), struct(BUF, HID)],
        [vmem(3, TOK, 128)] + wide_scratch + [vmem(GROUPS, CH, HID), vmem(STACK, TOK)],
        cost=1_000_000_000,
    )(
        *back_held, *first_ready, qkv, attention, attended, place,
    )
    (grad_input,) = call(
        input_gradient,
        [grid_spec, weight_specs(0)[0], whole(TOK, CH), whole(TOK, 3 * CH)],
        [struct(ROWS, COLS, LEVS, CH)],
        [vmem(3, TOK, 128)],
        cost=100_000_000,
    )(x, weights[0], dmid, dqkv)
    got1 = swap_cores(send1)
    for_plane, table_part = call(
        join,
        [whole(BUF, HID)] * 4,
        [struct(PLANE, NZ * UNIT, 128), struct(NZ, 2 * TABLE_ROWS, 128)],
        [vmem(BUF, HID)],
    )(keep1, got1, keep2, got2)
    plane_got = lax.all_to_all(for_plane, ("lat", "lev"), 0, 0, tiled=True)
    (for_lon,) = call(
        plane_sum,
        [whole(PLANE, NZ * UNIT, 128), whole(NZ, 2 * TABLE_ROWS, 128)],
        [struct(NZ, LON_ROWS, 128)],
        [vmem(NZ * UNIT, 128)],
    )(plane_got, table_part)
    core_groups = [[z * 2 + c for z in range(NZ)] for c in range(2)]
    lon_got = lax.all_to_all(
        for_lon, "lon", 0, 0, axis_index_groups=core_groups, tiled=True
    )
    copies, grad_table = call(
        lon_sum,
        [whole(NZ, LON_ROWS, 128)],
        [struct(PLANE, 32, 128), struct(2, 1, HEADS, 1, TSHARE)],
        [vmem(LON_ROWS, 128)],
    )(lon_got)
    shares = lax.all_to_all(copies, ("lat", "lev"), 0, 0, tiled=True)
    tokens = TOK * lax.axis_size("lon") * lax.axis_size("lat") * lax.axis_size("lev")
    grad_qkv, grad_proj, grad_up, grad_down = call(
        lambda *refs: unpack(float(tokens) ** (-0.5), *refs),
        [whole(PLANE, 32, 128)],
        [
            struct(SHARE, 2, 3 * CH),
            struct(SHARE, 2, CH),
            struct(SHARE, 2, HID),
            struct(2, 48, CH),
        ],
        [vmem(2, GROUPS, 16, HID)],
    )(shares)
    return (
        grad_input.transpose(2, 0, 1, 3),
        grad_qkv.transpose(1, 0, 2),
        grad_proj.transpose(1, 0, 2),
        grad_up.transpose(1, 0, 2),
        grad_down,
        grad_table.transpose(0, 1, 3, 2, 4),
    )


def solution(mesh):
    in_specs = (
        P("lev", "lat", "lon", None),
        P("lev", "lat", "lon", None),
        P(),
        P(),
        P(),
        P(),
        P(None, "lev", "lat", None, None),
        P(),
    )
    out_specs = (
        P("lev", "lat", "lon", None),
        P(None, "lon", None),
        P(None, "lon", None),
        P(None, "lon", None),
        P(None, "lon", None),
        P(None, "lev", "lat", None, "lon"),
    )
    return jax.shard_map(local, mesh=mesh, in_specs=in_specs, out_specs=out_specs, check_vma=False)
```

```python
import jax
import jax.numpy as jnp
import numpy as np
from jax import lax
from jax.experimental import pallas as pl
from jax.experimental.pallas import tpu as pltpu
from jax.sharding import PartitionSpec as P

F32 = jnp.float32
BF16 = jnp.bfloat16

HEADS = 6
HEAD = 32
CH = 192
HID = 768
LEVS = 2
ROWS = 6
COLS = 12
CELLS = LEVS * ROWS
TOK = CELLS * COLS
STACK = HEADS * TOK
SPAN = 2 * COLS - 1
POS = 3312
CHUNK = ROWS * SPAN
UPLANES = 384
NEGATIVE = -10000.0
SCALE = HEAD ** (-0.5)

NZ = 8
SHARE = 12
GROUPS = 3
GROWS = NZ * GROUPS * SHARE
TROWS = 24
BUF = GROWS + TROWS
TSHARE = POS // 16
PLANE = 16
UNIT = 27
TABLE_ROWS = 2 * HEADS
LON_ROWS = 56

NN = ((1,), (0,))
NT = ((1,), (1,))
TN = ((0,), (0,))


def params(mib=28):
    return pltpu.CompilerParams(vmem_limit_bytes=mib * 1024 * 1024)


def halves(v):
    top = v.astype(BF16)
    return top, (v - top.astype(F32)).astype(BF16)


def thirds(v):
    top = v.astype(BF16)
    rest = v - top.astype(F32)
    mid = rest.astype(BF16)
    return top, mid, (rest - mid.astype(F32)).astype(BF16)


def dot(a, b, dims):
    return lax.dot_general(a, b, (dims, ((), ())), preferred_element_type=F32)


def dot3(a, b, dims):
    return dot(a[0], b[0], dims) + (dot(a[0], b[1], dims) + dot(a[1], b[0], dims))


def weight_gradient(a, b):
    a, b = halves(a), halves(b)
    left = jnp.concatenate([a[0], a[0], a[1]], axis=0)
    return dot(left, jnp.concatenate([b[0], b[1], b[0]], axis=0), TN)


def exact_dot(v, one_hot, dims):
    a, b, c = thirds(v)
    return (dot(a, one_hot, dims) + dot(b, one_hot, dims)) + dot(c, one_hot, dims)


def norm(v):
    centered = v - jnp.mean(v, axis=-1, keepdims=True)
    inv = lax.rsqrt(jnp.mean(centered * centered, axis=-1, keepdims=True) + 1e-05)
    return centered * inv, inv


def norm_back(d, normed, inv):
    return inv * (
        d
        - jnp.mean(d, axis=-1, keepdims=True)
        - normed * jnp.mean(d * normed, axis=-1, keepdims=True)
    )


ERF_TOP = (
    0.00022905065861350646,
    0.0034082910107109506,
    0.050955695062380861,
    0.18520832239976145,
    1.128379143519084,
)
ERF_LOW = (
    -1.1791602954361697e-7,
    0.000023547966471313185,
    0.0010179625278914885,
    0.014070470171167667,
    0.11098505178285362,
    0.49746925110067538,
    1.0,
)


def erf(v):
    v = jnp.clip(v, -3.832506856900711, 3.832506856900711)
    sq = v * v
    top = jnp.full_like(v, ERF_TOP[0])
    for term in ERF_TOP[1:]:
        top = top * sq + term
    low = jnp.full_like(v, ERF_LOW[0])
    for term in ERF_LOW[1:]:
        low = low * sq + term
    return v * top / low


def half_cdf(pre):
    return 0.5 + 0.5 * erf(pre * (0.5**0.5))


def head_rows(dtype):
    lane = lax.broadcasted_iota(jnp.int32, (1, CH), 1)
    return [
        jnp.where((lane >= h * HEAD) & (lane < (h + 1) * HEAD), 1.0, 0.0).astype(dtype)
        for h in range(HEADS)
    ]


def stack_heads(pair):
    rows = head_rows(BF16)
    return tuple(jnp.concatenate([part * rows[h] for h in range(HEADS)], axis=0) for part in pair)


def turned(v, lanes):
    return jnp.concatenate([v[:, CH - lanes :], v[:, : CH - lanes]], axis=1)


def head_products(q, k):
    rows = head_rows(BF16)
    pairs = [rows[2 * r] + rows[2 * r + 1] for r in range(3)]
    q64, q128 = turned(q[1], 2 * HEAD), turned(q[0], 4 * HEAD)
    k64, k128 = turned(k[0], 2 * HEAD), turned(k[1], 4 * HEAD)
    out = []
    for r in range(3):
        right = k[0] * pairs[r] + k64 * pairs[(r + 1) % 3] + k128 * pairs[(r + 2) % 3]
        left = [
            q[0] * rows[h] + q64 * rows[(h + 2) % HEADS] + q128 * rows[(h + 4) % HEADS]
            for h in (2 * r, 2 * r + 1)
        ]
        out.append(dot(jnp.concatenate(left, axis=0), right, NT))
    return jnp.concatenate(out, axis=0)


def head_sums(p, v):
    half = CH // 2
    lane = lax.broadcasted_iota(jnp.int32, (1, CH), 1)
    lane = jnp.where(lane < half, lane, lane - half)
    out = []
    for group in range(2):
        lanes = slice(group * half, (group + 1) * half)
        rows = slice(group * STACK // 2, (group + 1) * STACK // 2)
        both = dot(p[0][rows], jnp.concatenate([v[0][:, lanes], v[1][:, lanes]], axis=1), NN)
        rest = dot(p[1][rows], v[0][:, lanes], NN)
        total, more = 0.0, 0.0
        for i in range(HEADS // 2):
            mine = jnp.where((lane >= i * HEAD) & (lane < (i + 1) * HEAD), 1.0, 0.0)
            total = total + both[i * TOK : (i + 1) * TOK] * mine
            more = more + rest[i * TOK : (i + 1) * TOK] * mine[:, 0:half]
        out.append(total[:, 0:half] + total[:, half:CH] + more)
    return jnp.concatenate(out, axis=1)


def place_matrix():
    mat = np.zeros((UPLANES, UPLANES), np.float32)
    for kl in range(LEVS):
        for kr in range(ROWS):
            for p in range(SPAN):
                mat[kl * CHUNK + kr * SPAN + p, p * CELLS + kr * LEVS + kl] = 1.0
    return jnp.asarray(mat, BF16)


def chunk_start(ql, kl, qr):
    return ((ql * LEVS + kl) * ROWS + qr) * CHUNK


def expand_bias(table_ref, place_ref, flat_ref, up_ref, bias_ref):
    flat_ref[...] = jnp.zeros_like(flat_ref)
    for h in range(HEADS):
        flat_ref[h : h + 1, 0:POS] = table_ref[0, h]
    lane = lax.broadcasted_iota(jnp.int32, (8, UPLANES), 1)
    for ql in range(LEVS):
        for qr in range(ROWS):
            g = qr * LEVS + ql
            row = jnp.zeros((8, UPLANES), F32)
            for kl in range(LEVS):
                start = chunk_start(ql, kl, qr)
                base = start // 128 * 128
                window = flat_ref[:, base : base + UPLANES]
                turn = (kl * CHUNK - (start - base)) % UPLANES
                if turn:
                    window = pltpu.roll(window, turn, 1)
                row = jnp.where((lane >= kl * CHUNK) & (lane < (kl + 1) * CHUNK), window, row)
            up_ref[g * 8 : (g + 1) * 8, :] = row
    ups = exact_dot(up_ref[...], place_ref[...], NN)
    for h in range(HEADS):
        rows = jnp.concatenate([ups[g * 8 + h : g * 8 + h + 1] for g in range(CELLS)], axis=0)
        for qc in range(COLS):
            turn = (-(COLS - 1 - qc) * CELLS) % UPLANES
            moved = pltpu.roll(rows, turn, 1) if turn else rows
            bias_ref[h * TOK + qc * CELLS : h * TOK + (qc + 1) * CELLS, :] = moved[:, 0:TOK]


def collect_table(dscore_ref, place_ref, up_ref, flat_ref):
    up_ref[...] = jnp.zeros_like(up_ref)
    for h in range(HEADS):
        total = jnp.zeros((CELLS, UPLANES), F32)
        for qc in range(COLS):
            block = dscore_ref[h * TOK + qc * CELLS : h * TOK + (qc + 1) * CELLS, :]
            block = jnp.concatenate([block, jnp.zeros((CELLS, UPLANES - TOK), F32)], axis=1)
            turn = (COLS - 1 - qc) * CELLS
            total = total + (pltpu.roll(block, turn, 1) if turn else block)
        for g in range(CELLS):
            up_ref[g * 8 + h : g * 8 + h + 1, :] = total[g : g + 1]
    raw = exact_dot(up_ref[...], place_ref[...], NT)
    flat_ref[...] = jnp.zeros_like(flat_ref)
    lane = lax.broadcasted_iota(jnp.int32, (8, UPLANES), 1)
    for ql in range(LEVS):
        for qr in range(ROWS):
            g = qr * LEVS + ql
            row = raw[g * 8 : (g + 1) * 8]
            for kl in range(LEVS):
                start = chunk_start(ql, kl, qr)
                base = start // 128 * 128
                shift = start - base
                turn = (shift - kl * CHUNK) % UPLANES
                moved = pltpu.roll(row, turn, 1) if turn else row
                keep = (lane >= shift) & (lane < shift + CHUNK)
                window = flat_ref[:, base : base + UPLANES]
                flat_ref[:, base : base + UPLANES] = jnp.where(keep, moved, window)


def window_masks(mask_ref, second):
    lev = lax.axis_index("lev")
    lat = lax.axis_index("lat")
    last_lev = lev == lax.axis_size("lev") - 1
    last_lat = lat == lax.axis_size("lat") - 1
    key_col = lax.broadcasted_iota(jnp.int32, (1, TOK), 1)
    key_row = lax.div(lax.rem(key_col, CELLS), LEVS)
    key_bias = jnp.zeros((1, TOK), F32)
    count = ROWS * lax.axis_size("lat")
    for r in range(ROWS):
        place = lat * ROWS + r
        if second:
            place = lax.rem(place + ROWS // 2, count)
        value = NEGATIVE * (1.0 - mask_ref[place].astype(F32))
        key_bias = jnp.where(key_row == r, value, key_bias)
    if not second:
        return key_bias, None

    def label(tokens):
        level = jnp.where(lax.rem(tokens, LEVS) >= LEVS // 2, 2, 0)
        row = jnp.where(lax.rem(tokens, CELLS) >= CELLS // 2, 1, 0)
        return level * last_lev.astype(jnp.int32) + row * last_lat.astype(jnp.int32)

    query = label(lax.broadcasted_iota(jnp.int32, (TOK, 1), 0))
    pair = jnp.where(query == label(key_col), 0.0, NEGATIVE).astype(F32)
    return key_bias, pair


def add_masks(scores, key_bias, pair):
    scores = scores + key_bias
    if pair is None:
        return scores
    return jnp.concatenate([scores[h * TOK : (h + 1) * TOK] + pair for h in range(HEADS)], axis=0)


def scaled_parts(qkv):
    return qkv[:, 0:CH] * SCALE, qkv[:, CH : 2 * CH], qkv[:, 2 * CH : 3 * CH]


def project(x, wq):
    normed, inv = norm(x)
    return normed, inv, dot3(halves(normed), wq, NN)


def attend(qkv, bias, key_bias, pair):
    q, k, v = scaled_parts(qkv)
    scores = add_masks(head_products(halves(q), halves(k)) + bias, key_bias, pair)
    grown = jnp.exp(scores - jnp.max(scores, axis=-1, keepdims=True))
    weights = grown * (1.0 / jnp.sum(grown, axis=-1, keepdims=True))
    return weights, head_sums(halves(weights), halves(v))


SIDE = COLS // 2
MAIN = ROWS // 2 * SIDE
WIDE = 56
THIN = 32
REST = CH - 128


MOVES = ((0, 0), (1, 0), (0, 1), (1, 1))


def six_rows(lev, j, k):
    for rr in range(ROWS // 2):
        yield rr, k * SIDE * CELLS + (j * (ROWS // 2) + rr) * LEVS + lev


def spread_pair(grid, out_refs):
    for (dlev, dj), out_ref in zip(MOVES, out_refs):
        for k in range(2):
            for rr, start in six_rows(1 - dlev, 1 - dj, k):
                rows = pl.ds(start, SIDE, stride=CELLS)
                for part, to in ((0, 0), (2, MAIN), (1, 2 * MAIN)):
                    out_ref[k, to + rr * SIDE : to + (rr + 1) * SIDE, :] = grid[part, rows, :]


def gather_pair(grid, own_refs, around_ref):
    for piece, (dlev, dj) in enumerate(MOVES):
        for k in range(2):
            ref, slot = (own_refs[piece], 1) if k == 0 else (around_ref, piece)
            for rr, start in six_rows(dlev, dj, k):
                rows = pl.ds(start, SIDE, stride=CELLS)
                for part, at in ((0, 0), (2, MAIN), (1, 2 * MAIN)):
                    grid[part, rows, :] = ref[slot, at + rr * SIDE : at + (rr + 1) * SIDE, :]


def spread_one(grid, out_refs):
    low = lax.broadcasted_iota(jnp.int32, (SIDE // 2, 128), 1) < REST
    for (dlev, dj), out_ref in zip(MOVES, out_refs):
        for k in range(2):
            for rr, start in six_rows(dlev, dj, k):
                rows = pl.ds(start, SIDE, stride=CELLS)
                out_ref[k, rr * SIDE : (rr + 1) * SIDE, :] = grid[0, rows, :]
                one = grid[1, pl.ds(start, SIDE // 2, stride=CELLS), :]
                two = grid[1, pl.ds(start + SIDE // 2 * CELLS, SIDE // 2, stride=CELLS), :]
                to = MAIN + rr * (SIDE // 2)
                out_ref[k, to : to + SIDE // 2, :] = jnp.where(low, one, pltpu.roll(two, REST, 1))


def gather_one(grid, own_refs, around_ref):
    for piece, (dlev, dj) in enumerate(MOVES):
        for k in range(2):
            ref, slot = (own_refs[piece], 0) if k == 1 else (around_ref, piece)
            for rr, start in six_rows(1 - dlev, 1 - dj, k):
                rows = pl.ds(start, SIDE, stride=CELLS)
                grid[0, rows, :] = ref[slot, rr * SIDE : (rr + 1) * SIDE, :]
                at = MAIN + rr * (SIDE // 2)
                both = ref[slot, at : at + SIDE // 2, :]
                grid[1, pl.ds(start, SIDE // 2, stride=CELLS), :] = both
                rows = pl.ds(start + SIDE // 2 * CELLS, SIDE // 2, stride=CELLS)
                grid[1, rows, :] = pltpu.roll(both, REST, 1)


def load_first(grid):
    return jnp.concatenate([grid[0], grid[1][:, 0:REST]], axis=1)


def load_second(grid):
    return jnp.concatenate([grid[2], grid[1][:, REST:128]], axis=1)


def store_first(grid, value):
    grid[0] = value[:, 0:128]
    grid[1, :, 0:REST] = value[:, 128:CH]


def load_window(x_ref, grid, second=False):
    head, at = (2, REST) if second else (0, 0)
    for r in range(ROWS):
        for c in range(COLS):
            rows = slice(c * CELLS + r * LEVS, c * CELLS + (r + 1) * LEVS)
            cell = x_ref[r, c]
            grid[head, rows, :] = cell[:, 0:128]
            grid[1, rows, at : at + REST] = cell[:, 128:CH]


def save_window(grid, out_ref):
    for r in range(ROWS):
        for c in range(COLS):
            rows = slice(c * CELLS + r * LEVS, c * CELLS + (r + 1) * LEVS)
            out_ref[r, c, :, 0:128] = grid[0, rows, :]
            out_ref[r, c, :, 128:CH] = grid[1, rows, 0:REST]


def first_forward(
    mask_hbm, x_hbm, cot_hbm, wq_hbm, wp_hbm, wu_hbm, wd_hbm, table_hbm, place_hbm,
    own_ref, lev_ref, lat_ref, both_ref, qkv_hbm, weights_hbm, attended_hbm, mid_hbm, pre_hbm,
    mask_ref, x_ref, cot_ref, wq_ref, wp_ref, wu_ref, wd_ref, table_ref, place_ref,
    grid_ref, flat_ref, up_ref, bias_ref, qkv_ref, weights_ref, attended_ref, mid_ref, pre_ref, sems,
    out_sems,
):
    pairs = (
        (x_hbm, x_ref),
        (wq_hbm.at[0], wq_ref),
        (table_hbm.at[0], table_ref),
        (place_hbm, place_ref),
        (mask_hbm, mask_ref),
        (wp_hbm.at[0], wp_ref),
        (wu_hbm.at[0], wu_ref),
        (wd_hbm.at[0], wd_ref),
        (cot_hbm, cot_ref),
    )
    copies = [pltpu.make_async_copy(*pair, sems.at[i]) for i, pair in enumerate(pairs)]
    for copy in copies:
        copy.start()
    copies[0].wait()
    load_window(x_ref, grid_ref)
    x = load_first(grid_ref)
    copies[1].wait()
    for copy in copies[2:5]:
        copy.wait()
    expand_bias(table_ref, place_ref, flat_ref, up_ref, bias_ref)
    key_bias, _ = window_masks(mask_ref, False)
    _, _, qkv = project(x, halves(wq_ref[...]))
    weights, attended = attend(qkv, bias_ref[...], key_bias, None)
    saved = []

    def save(value, ref, to):
        ref[...] = value
        saved.append(pltpu.make_async_copy(ref, to, out_sems.at[len(saved)]))
        saved[-1].start()

    save(qkv, qkv_ref, qkv_hbm)
    save(weights, weights_ref, weights_hbm)
    save(attended, attended_ref, attended_hbm)
    for copy in copies[5:]:
        copy.wait()
    mid = x + dot3(halves(attended), halves(wp_ref[...]), NN)
    save(mid, mid_ref, mid_hbm)
    normed, _ = norm(mid)
    pre = dot3(halves(normed), halves(wu_ref[...]), NN)
    save(pre, pre_ref, pre_hbm)
    hidden = pre * half_cdf(pre)
    load_window(cot_ref, grid_ref, True)
    store_first(grid_ref, mid + dot3(halves(hidden), halves(wd_ref[...]), NT))
    for copy in saved:
        copy.wait()
    spread_pair(grid_ref, (own_ref, lev_ref, lat_ref, both_ref))


def gelu_slope(pre, cdf):
    return cdf + pre * jnp.exp(-0.5 * pre * pre) * ((2.0 * np.pi) ** (-0.5))


def mlp_backward(g, slope, normed, inv, wu, wd):
    dpre = dot3(halves(g), wd, NN) * slope
    dnormed = dot3(halves(dpre), wu, NT)
    return dpre, g + norm_back(dnormed, normed, inv)


def attention_backward(dmid, qkv, weights, wp):
    q, k, v = scaled_parts(qkv)
    dattended = dot3(halves(dmid), wp, NT)
    dhalves = halves(dattended)
    dstack = stack_heads(dhalves)
    dweights = head_products(dhalves, halves(v))
    inner = jnp.sum(dweights * weights, axis=-1, keepdims=True)
    dscores = weights * (dweights - inner)
    ds = halves(dscores)
    dq = head_sums(ds, halves(k)) * SCALE
    dk = dot3(ds, stack_heads(halves(q)), TN)
    dv = dot3(halves(weights), dstack, TN)
    return dscores, jnp.concatenate([dq, dk, dv], axis=1)


def pack_gradients(keep_ref, send_ref, wide_ref, dqkv, dproj, dup, ddown, flat_ref):
    core = lax.rem(lax.axis_index("lon"), 2)
    wide_ref[0, :, 0 : 3 * CH] = dqkv
    wide_ref[0, :, 3 * CH : 4 * CH] = dproj
    wide_ref[1] = dup
    for share in range(2 * NZ):
        rows = [
            ddown[share * 48 + m * SHARE : share * 48 + (m + 1) * SHARE] for m in range(HID // CH)
        ]
        wide_ref[2, share * SHARE : (share + 1) * SHARE, :] = jnp.concatenate(rows, axis=1)
    even = core == 0
    for z in range(NZ):
        for group in range(GROUPS):
            first = wide_ref[group, 2 * SHARE * z : 2 * SHARE * z + SHARE, :]
            second = wide_ref[group, 2 * SHARE * z + SHARE : 2 * SHARE * (z + 1), :]
            rows = slice((z * GROUPS + group) * SHARE, (z * GROUPS + group + 1) * SHARE)
            keep_ref[rows, :] = jnp.where(even, first, second)
            send_ref[rows, :] = jnp.where(even, second, first)
    for ref in (keep_ref, send_ref):
        ref[GROWS:BUF, :] = jnp.zeros((TROWS, HID), F32)
    for z in range(NZ):
        first = table_share(flat_ref, 2 * z)
        second = table_share(flat_ref, 2 * z + 1)
        rows = slice(GROWS + z // 3 * 8, GROWS + z // 3 * 8 + 8)
        lanes = slice(z % 3 * 256, z % 3 * 256 + 256)
        keep_ref[rows, lanes] = jnp.where(even, first, second)
        send_ref[rows, lanes] = jnp.where(even, second, first)


def table_share(flat_ref, share):
    start = share * TSHARE
    base = start // 128 * 128
    window = flat_ref[:, base : base + UPLANES]
    if start - base:
        window = pltpu.roll(window, UPLANES - (start - base), 1)
    return window[:, 0:256]


def second_pass(
    own_ref, lev_ref, lat_ref, both_ref, around_ref, wq0_ref, wq1_ref, wp0_ref, wp1_ref, wu0_ref,
    wu1_ref, wd0_ref, wd1_ref, bias_ref, key_ref, pair_ref,
    back_own_ref, back_lev_ref, back_lat_ref, back_both_ref, dscores_ref, normed_ref, attended_ref, hnormed_ref, hidden_ref,
    g_ref, dpre_ref, dmid_ref, dqkv_ref,
    grid_ref,
):
    gather_pair(grid_ref, (own_ref, lev_ref, lat_ref, both_ref), around_ref)
    x = load_first(grid_ref)
    g = load_second(grid_ref)
    wq, wp = (wq0_ref[...], wq1_ref[...]), (wp0_ref[...], wp1_ref[...])
    wu, wd = (wu0_ref[...], wu1_ref[...]), (wd0_ref[...], wd1_ref[...])
    key_bias, pair = key_ref[0:1], pair_ref[...]
    normed, inv, qkv = project(x, wq)
    weights, attended = attend(qkv, bias_ref[...], key_bias, pair)
    normed_ref[...] = normed
    attended_ref[...] = attended
    mid = x + dot3(halves(attended), wp, NN)
    hnormed, hinv = norm(mid)
    hnormed_ref[...] = hnormed
    pre = dot3(halves(hnormed), wu, NN)
    cdf = half_cdf(pre)
    hidden_ref[...] = pre * cdf
    g_ref[...] = g
    dpre, dmid = mlp_backward(g, gelu_slope(pre, cdf), hnormed, hinv, wu, wd)
    dpre_ref[...] = dpre
    dmid_ref[...] = dmid
    dscores, dqkv = attention_backward(dmid, qkv, weights, wp)
    dscores_ref[...] = dscores
    dqkv_ref[...] = dqkv
    dx = dmid + norm_back(dot3(halves(dqkv), wq, NT), normed, inv)
    store_first(grid_ref, dx)
    spread_one(grid_ref, (back_own_ref, back_lev_ref, back_lat_ref, back_both_ref))


def second_gradients(
    dscores_ref, normed_ref, attended_ref, hnormed_ref, hidden_ref, g_ref, dpre_ref, dmid_ref,
    dqkv_ref, place_ref,
    keep_ref, send_ref,
    flat_ref, up_ref, wide_ref,
):
    collect_table(dscores_ref, place_ref, up_ref, flat_ref)
    pack_gradients(
        keep_ref, send_ref, wide_ref,
        weight_gradient(normed_ref[...], dqkv_ref[...]),
        weight_gradient(attended_ref[...], dmid_ref[...]),
        weight_gradient(hnormed_ref[...], dpre_ref[...]),
        weight_gradient(hidden_ref[...], g_ref[...]),
        flat_ref,
    )


def first_backward(
    own_ref, lev_ref, lat_ref, both_ref, around_ref, wp0_ref, wp1_ref, wu0_ref, wu1_ref, wd0_ref,
    wd1_ref, slope_ref, hidden_ref, hnormed_ref, hinv_ref, normed_ref, qkv_ref, weights_ref,
    attended_ref, place_ref,
    dmid_ref, dqkv_ref, gkeep_ref, gsend_ref,
    grid_ref, flat_ref, up_ref, wide_ref, dscores_ref,
):
    gather_one(grid_ref, (own_ref, lev_ref, lat_ref, both_ref), around_ref)
    g = load_first(grid_ref)
    wp = (wp0_ref[...], wp1_ref[...])
    wu, wd = (wu0_ref[...], wu1_ref[...]), (wd0_ref[...], wd1_ref[...])
    hnormed = hnormed_ref[...]
    dpre, dmid = mlp_backward(g, slope_ref[...], hnormed, hinv_ref[...], wu, wd)
    dup = weight_gradient(hnormed, dpre)
    ddown = weight_gradient(hidden_ref[...], g)
    dproj = weight_gradient(attended_ref[...], dmid)
    dscores, dqkv = attention_backward(dmid, qkv_ref[...], weights_ref[...], wp)
    dscores_ref[...] = dscores
    dmid_ref[...] = dmid
    dqkv_ref[...] = dqkv
    collect_table(dscores_ref, place_ref, up_ref, flat_ref)
    pack_gradients(
        gkeep_ref, gsend_ref, wide_ref,
        weight_gradient(normed_ref[...], dqkv), dproj, dup, ddown, flat_ref,
    )


def first_prepare(
    x_ref, mid_ref, pre_ref, wp_ref, wu_ref, wd_ref,
    wp0_ref, wp1_ref, wu0_ref, wu1_ref, wd0_ref, wd1_ref, slope_ref, hidden_ref, hnormed_ref, hinv_ref,
    normed_ref,
    grid_ref,
):
    split_into(((wp_ref, wp0_ref, wp1_ref), (wu_ref, wu0_ref, wu1_ref), (wd_ref, wd0_ref, wd1_ref)))
    pre = pre_ref[...]
    cdf = half_cdf(pre)
    slope_ref[...] = gelu_slope(pre, cdf)
    hidden_ref[...] = pre * cdf
    hnormed_ref[...], hinv_ref[...] = norm(mid_ref[...])
    load_window(x_ref, grid_ref)
    normed_ref[...], _ = norm(load_first(grid_ref))


def split_into(triples):
    for ref, high_ref, low_ref in triples:
        high_ref[...], low_ref[...] = halves(ref[...])


def input_gradient(x_ref, wq_ref, dmid_ref, dqkv_ref, grad_ref, grid_ref):
    load_window(x_ref, grid_ref)
    normed, inv = norm(load_first(grid_ref))
    dnormed = dot3(halves(dqkv_ref[...]), halves(wq_ref[...]), NT)
    store_first(grid_ref, dmid_ref[...] + norm_back(dnormed, normed, inv))
    save_window(grid_ref, grad_ref)


def second_prepare(
    mask_ref, table_ref, place_ref, wq_ref, wp_ref, wu_ref, wd_ref,
    wq0_ref, wq1_ref, wp0_ref, wp1_ref, wu0_ref, wu1_ref, wd0_ref, wd1_ref, bias_ref, key_ref, pair_ref,
    flat_ref, up_ref,
):
    split_into(
        (
            (wq_ref, wq0_ref, wq1_ref),
            (wp_ref, wp0_ref, wp1_ref),
            (wu_ref, wu0_ref, wu1_ref),
            (wd_ref, wd0_ref, wd1_ref),
        )
    )
    expand_bias(table_ref, place_ref, flat_ref, up_ref, bias_ref)
    key_bias, pair = window_masks(mask_ref, True)
    key_ref[...] = jnp.broadcast_to(key_bias, (8, TOK))
    pair_ref[...] = pair


def unit_parts(block):
    for tile in range(18):
        number = block * 18 + tile
        if number < 32:
            yield number // 2, number % 2 * SHARE, SHARE, tile, 0
        else:
            for quarter in range(4):
                yield (number - 32) * 4 + quarter, 2 * SHARE, SHARE // 4, tile, quarter * (SHARE // 4)


def table_place(z):
    return slice(GROWS + z // 3 * 8, GROWS + z // 3 * 8 + 8), slice(z % 3 * 256, z % 3 * 256 + 256)


def join(mine0_ref, theirs0_ref, mine1_ref, theirs1_ref, plane_ref, table_ref, sum_ref):
    for block, (mine_ref, theirs_ref) in enumerate(((mine0_ref, theirs0_ref), (mine1_ref, theirs1_ref))):
        sum_ref[...] = mine_ref[...] + theirs_ref[...]
        for z in range(NZ):
            for p, at, count, tile, start in unit_parts(block):
                start = (z * GROUPS + tile // 6) * SHARE + start
                lanes = slice(tile % 6 * 128, tile % 6 * 128 + 128)
                at = z * UNIT + at
                plane_ref[p, at : at + count, :] = sum_ref[start : start + count, lanes]
            table = sum_ref[table_place(z)]
            for half in range(2):
                to = block * TABLE_ROWS + half * HEADS
                table_ref[z, to : to + HEADS, :] = table[0:HEADS, half * 128 : half * 128 + 128]


def plane_sum(got_ref, table_ref, out_ref, sum_ref):
    total = got_ref[0]
    for p in range(1, PLANE):
        total = total + got_ref[p]
    sum_ref[...] = total
    used = UNIT + 2 * TABLE_ROWS
    for z in range(NZ):
        out_ref[z, 0:UNIT, :] = sum_ref[z * UNIT : (z + 1) * UNIT, :]
        out_ref[z, UNIT:used, :] = table_ref[z]
        out_ref[z, used:LON_ROWS, :] = jnp.zeros((LON_ROWS - used, 128), F32)


def lon_sum(got_ref, out_ref):
    total = got_ref[0, 0:32, :]
    for z in range(1, NZ):
        total = total + got_ref[z, 0:32, :]
    for p in range(PLANE):
        out_ref[p] = total


def table_sum(got_ref, table_ref, sum_ref):
    total = got_ref[0]
    for z in range(1, NZ):
        total = total + got_ref[z]
    sum_ref[...] = total
    for block in range(2):
        for h in range(HEADS):
            row = UNIT + block * TABLE_ROWS + h
            table_ref[block, 0, h, :, 0:128] = sum_ref[row : row + 1, :]
            row = row + HEADS
            table_ref[block, 0, h, :, 128:TSHARE] = sum_ref[row : row + 1, 0 : TSHARE - 128]


def unpack(scale, got_ref, qkv_ref, proj_ref, up_ref, down_ref, wide_ref):
    for block in range(2):
        for p, at, count, tile, to in unit_parts(block):
            lanes = slice(tile % 6 * 128, tile % 6 * 128 + 128)
            wide_ref[block, tile // 6, to : to + count, lanes] = got_ref[p, at : at + count, :] * scale
        for row in range(SHARE):
            at = slice(row, row + 1)
            qkv_ref[row, block : block + 1, :] = wide_ref[block, 0, at, 0 : 3 * CH]
            proj_ref[row, block : block + 1, :] = wide_ref[block, 0, at, 3 * CH : 4 * CH]
            up_ref[row, block : block + 1, :] = wide_ref[block, 1, at, :]
        for m in range(HID // CH):
            down_ref[block, m * SHARE : (m + 1) * SHARE, :] = wide_ref[
                block, 2, 0:SHARE, m * CH : (m + 1) * CH
            ]


WEIGHTS = ((CH, 3 * CH), (CH, CH), (CH, HID), (CH, HID))


def struct(*shape, dtype=F32):
    return jax.ShapeDtypeStruct(shape, dtype)


def vmem(*shape):
    return pltpu.VMEM(shape, F32)


def whole(*shape):
    return pl.BlockSpec(shape, lambda i: (0,) * len(shape))


def part_of(block, *shape):
    return pl.BlockSpec((None,) + shape, lambda i: (block,) + (0,) * len(shape))


def weight_specs(block):
    return [
        part_of(block, CH, 3 * CH),
        part_of(block, CH, CH),
        part_of(block, CH, HID),
        part_of(block, CH, HID),
    ]


def table_spec(block):
    return part_of(block, 1, HEADS, 1, POS)


def call(body, in_specs, outs, scratch, cost=0, mib=28, far=0):
    near = [whole(*o.shape) for o in outs[: len(outs) - far]]
    return pl.pallas_call(
        body,
        grid=(1,),
        in_specs=in_specs,
        out_specs=near + [HBM] * far,
        out_shape=outs,
        scratch_shapes=scratch,
        compiler_params=params(mib),
        cost_estimate=pl.CostEstimate(flops=cost, bytes_accessed=4 * 2**20, transcendentals=0),
    )


SMEM = pl.BlockSpec(memory_space=pltpu.SMEM)
HBM = pl.BlockSpec(memory_space=pltpu.HBM)
FLAT = 3456


def shifted(block, axis, distance):
    devices = range(lax.axis_size(axis))
    route = [((i - distance) % len(devices), i) for i in devices]
    return lax.ppermute(block, axis, route)


def shifted_plane(block, levels, rows):
    size = lax.axis_size("lev")
    count = lax.axis_size("lat")
    route = [
        (lat * size + lev, (lat + rows) % count * size + (lev + levels) % size)
        for lat in range(count)
        for lev in range(size)
    ]
    return lax.ppermute(block, ("lat", "lev"), route)


def exchange(pieces, step, side, first=None):
    held = [pieces[0]] + [
        shifted_plane(piece, step * dlev, step * dlat)
        for piece, (dlev, dlat) in zip(pieces[1:], MOVES[1:])
    ]
    edge = jnp.stack([piece[side] for piece in held])
    if first is not None:
        edge, first = lax.optimization_barrier((edge, first))
    return held + [shifted(edge, "lon", step)], first


def swap_cores(v):
    return lax.ppermute(v, "lon", [(i, i ^ 1) for i in range(lax.axis_size("lon"))])


def local(inputs, cotangent, qkv_weight, proj_weight, up_weight, down_weight, bias_table, lat_mask):
    place = place_matrix()
    x = inputs.transpose(1, 2, 0, 3)
    cot = cotangent.transpose(1, 2, 0, 3)
    table = bias_table.transpose(0, 1, 3, 2, 4)
    weights = (qkv_weight, proj_weight, up_weight, down_weight.transpose(0, 2, 1))
    grid_spec = whole(ROWS, COLS, LEVS, CH)
    wide_scratch = [vmem(8, FLAT), vmem(8 * CELLS, UPLANES)]
    half = (2, WIDE, 128)
    *pieces, qkv, attention, attended, mid, pre = call(
        first_forward,
        [HBM] * 9,
        [struct(*half)] * 4
        + [
            struct(TOK, 3 * CH),
            struct(STACK, TOK),
            struct(TOK, CH),
            struct(TOK, CH),
            struct(TOK, HID),
        ],
        [
            pltpu.SMEM((8 * ROWS,), jnp.int32),
            vmem(ROWS, COLS, LEVS, CH),
            vmem(ROWS, COLS, LEVS, CH),
            vmem(CH, 3 * CH),
            vmem(CH, CH),
            vmem(CH, HID),
            vmem(CH, HID),
            vmem(1, HEADS, 1, POS),
            pltpu.VMEM((UPLANES, UPLANES), BF16),
            vmem(3, TOK, 128),
        ]
        + wide_scratch
        + [
            vmem(STACK, TOK),
            vmem(TOK, 3 * CH),
            vmem(STACK, TOK),
            vmem(TOK, CH),
            vmem(TOK, CH),
            vmem(TOK, HID),
            pltpu.SemaphoreType.DMA((9,)),
            pltpu.SemaphoreType.DMA((5,)),
        ],
        cost=500_000_000,
        mib=60,
        far=5,
    )(lat_mask, x, cot, *weights, table, place)
    prepared = call(
        second_prepare,
        [SMEM, table_spec(1), whole(UPLANES, UPLANES)] + weight_specs(1),
        [struct(*shape, dtype=BF16) for shape in WEIGHTS for _ in range(2)]
        + [struct(STACK, TOK), struct(8, TOK), struct(TOK, TOK)],
        wide_scratch,
        cost=200_000_000,
    )(lat_mask, table, place, *weights)
    held, prepared = exchange(pieces, -1, 0, prepared)
    around = (4, WIDE, 128)
    back_half = (2, THIN, 128)
    back_around = (4, THIN, 128)
    factors = [
        struct(STACK, TOK),
        struct(TOK, CH),
        struct(TOK, CH),
        struct(TOK, CH),
        struct(TOK, HID),
        struct(TOK, CH),
        struct(TOK, HID),
        struct(TOK, CH),
        struct(TOK, 3 * CH),
    ]
    second = call(
        second_pass,
        [whole(*half)] * 4
        + [whole(*around)]
        + [whole(*shape) for shape in WEIGHTS for _ in range(2)]
        + [whole(STACK, TOK), whole(8, TOK), whole(TOK, TOK)],
        [struct(*back_half)] * 4 + factors,
        [vmem(3, TOK, 128)],
        cost=1_000_000_000,
    )(*held, *prepared)
    back_pieces, saved = second[:4], second[4:]
    keep2, send2 = call(
        second_gradients,
        [whole(*f.shape) for f in factors] + [whole(UPLANES, UPLANES)],
        [struct(BUF, HID), struct(BUF, HID)],
        wide_scratch + [vmem(GROUPS, CH, HID)],
        cost=500_000_000,
    )(*saved, place)
    back_held, send2 = exchange(back_pieces, 1, 1, send2)
    pre, _ = lax.optimization_barrier((pre, back_pieces[0]))
    ready = [struct(*shape, dtype=BF16) for shape in WEIGHTS[1:] for _ in range(2)] + [
        struct(TOK, HID),
        struct(TOK, HID),
        struct(TOK, CH),
        struct(TOK, 1),
        struct(TOK, CH),
    ]
    first_ready = call(
        first_prepare,
        [grid_spec, whole(TOK, CH), whole(TOK, HID)] + weight_specs(0)[1:],
        ready,
        [vmem(3, TOK, 128)],
        cost=200_000_000,
    )(x, mid, pre, *weights[1:])
    send2, slope = lax.optimization_barrier((send2, first_ready[6]))
    first_ready = list(first_ready[:6]) + [slope] + list(first_ready[7:])
    got2 = swap_cores(send2)
    dmid, dqkv, keep1, send1 = call(
        first_backward,
        [whole(*back_half)] * 4
        + [whole(*back_around)]
        + [whole(*r.shape) for r in ready]
        + [
            whole(TOK, 3 * CH),
            whole(STACK, TOK),
            whole(TOK, CH),
            whole(UPLANES, UPLANES),
        ],
        [struct(TOK, CH), struct(TOK, 3 * CH), struct(BUF, HID), struct(BUF, HID)],
        [vmem(3, TOK, 128)] + wide_scratch + [vmem(GROUPS, CH, HID), vmem(STACK, TOK)],
        cost=1_000_000_000,
    )(
        *back_held, *first_ready, qkv, attention, attended, place,
    )
    (grad_input,) = call(
        input_gradient,
        [grid_spec, weight_specs(0)[0], whole(TOK, CH), whole(TOK, 3 * CH)],
        [struct(ROWS, COLS, LEVS, CH)],
        [vmem(3, TOK, 128)],
        cost=100_000_000,
    )(x, weights[0], dmid, dqkv)
    got1 = swap_cores(send1)
    keep1, grad_input = lax.optimization_barrier((keep1, grad_input))
    for_plane, table_part = call(
        join,
        [whole(BUF, HID)] * 4,
        [struct(PLANE, NZ * UNIT, 128), struct(NZ, 2 * TABLE_ROWS, 128)],
        [vmem(BUF, HID)],
    )(keep1, got1, keep2, got2)
    plane_got = lax.all_to_all(for_plane, ("lat", "lev"), 0, 0, tiled=True)
    (for_lon,) = call(
        plane_sum,
        [whole(PLANE, NZ * UNIT, 128), whole(NZ, 2 * TABLE_ROWS, 128)],
        [struct(NZ, LON_ROWS, 128)],
        [vmem(NZ * UNIT, 128)],
    )(plane_got, table_part)
    core_groups = [[z * 2 + c for z in range(NZ)] for c in range(2)]
    lon_got = lax.all_to_all(
        for_lon, "lon", 0, 0, axis_index_groups=core_groups, tiled=True
    )
    (copies,) = call(lon_sum, [whole(NZ, LON_ROWS, 128)], [struct(PLANE, 32, 128)], [])(lon_got)
    (grad_table,) = call(
        table_sum,
        [whole(NZ, LON_ROWS, 128)],
        [struct(2, 1, HEADS, 1, TSHARE)],
        [vmem(LON_ROWS, 128)],
    )(lon_got)
    shares = lax.all_to_all(copies, ("lat", "lev"), 0, 0, tiled=True)
    tokens = TOK * lax.axis_size("lon") * lax.axis_size("lat") * lax.axis_size("lev")
    grad_qkv, grad_proj, grad_up, grad_down = call(
        lambda *refs: unpack(float(tokens) ** (-0.5), *refs),
        [whole(PLANE, 32, 128)],
        [
            struct(SHARE, 2, 3 * CH),
            struct(SHARE, 2, CH),
            struct(SHARE, 2, HID),
            struct(2, 48, CH),
        ],
        [vmem(2, GROUPS, 16, HID)],
    )(shares)
    return (
        grad_input.transpose(2, 0, 1, 3),
        grad_qkv.transpose(1, 0, 2),
        grad_proj.transpose(1, 0, 2),
        grad_up.transpose(1, 0, 2),
        grad_down,
        grad_table.transpose(0, 1, 3, 2, 4),
    )


def solution(mesh):
    in_specs = (
        P("lev", "lat", "lon", None),
        P("lev", "lat", "lon", None),
        P(),
        P(),
        P(),
        P(),
        P(None, "lev", "lat", None, None),
        P(),
    )
    out_specs = (
        P("lev", "lat", "lon", None),
        P(None, "lon", None),
        P(None, "lon", None),
        P(None, "lon", None),
        P(None, "lon", None),
        P(None, "lev", "lat", None, "lon"),
    )
    return jax.shard_map(local, mesh=mesh, in_specs=in_specs, out_specs=out_specs, check_vma=False)
```

```python
import jax
import jax.numpy as jnp
import numpy as np
from jax import lax
from jax.experimental import pallas as pl
from jax.experimental.pallas import tpu as pltpu
from jax.sharding import PartitionSpec as P

F32 = jnp.float32
BF16 = jnp.bfloat16

HEADS = 6
HEAD = 32
CH = 192
HID = 768
LEVS = 2
ROWS = 6
COLS = 12
CELLS = LEVS * ROWS
TOK = CELLS * COLS
STACK = HEADS * TOK
SPAN = 2 * COLS - 1
POS = 3312
CHUNK = ROWS * SPAN
UPLANES = 384
NEGATIVE = -10000.0
SCALE = HEAD ** (-0.5)

NZ = 8
SHARE = 12
GROUPS = 3
GROWS = NZ * GROUPS * SHARE
TROWS = 24
BUF = GROWS + TROWS
TSHARE = POS // 16
PLANE = 16
UNIT = 27
TABLE_ROWS = 2 * HEADS
LON_ROWS = 56

NN = ((1,), (0,))
NT = ((1,), (1,))
TN = ((0,), (0,))


def params(mib=28):
    return pltpu.CompilerParams(vmem_limit_bytes=mib * 1024 * 1024)


def halves(v):
    top = v.astype(BF16)
    return top, (v - top.astype(F32)).astype(BF16)


def thirds(v):
    top = v.astype(BF16)
    rest = v - top.astype(F32)
    mid = rest.astype(BF16)
    return top, mid, (rest - mid.astype(F32)).astype(BF16)


def dot(a, b, dims):
    return lax.dot_general(a, b, (dims, ((), ())), preferred_element_type=F32)


def dot3(a, b, dims):
    return dot(a[0], b[0], dims) + (dot(a[0], b[1], dims) + dot(a[1], b[0], dims))


def weight_gradient(a, b):
    a, b = halves(a), halves(b)
    left = jnp.concatenate([a[0], a[0], a[1]], axis=0)
    return dot(left, jnp.concatenate([b[0], b[1], b[0]], axis=0), TN)


def exact_dot(v, one_hot, dims):
    a, b, c = thirds(v)
    return (dot(a, one_hot, dims) + dot(b, one_hot, dims)) + dot(c, one_hot, dims)


def norm(v):
    centered = v - jnp.mean(v, axis=-1, keepdims=True)
    inv = lax.rsqrt(jnp.mean(centered * centered, axis=-1, keepdims=True) + 1e-05)
    return centered * inv, inv


def norm_back(d, normed, inv):
    return inv * (
        d
        - jnp.mean(d, axis=-1, keepdims=True)
        - normed * jnp.mean(d * normed, axis=-1, keepdims=True)
    )


ERF_TOP = (
    0.00022905065861350646,
    0.0034082910107109506,
    0.050955695062380861,
    0.18520832239976145,
    1.128379143519084,
)
ERF_LOW = (
    -1.1791602954361697e-7,
    0.000023547966471313185,
    0.0010179625278914885,
    0.014070470171167667,
    0.11098505178285362,
    0.49746925110067538,
    1.0,
)


def erf(v):
    v = jnp.clip(v, -3.832506856900711, 3.832506856900711)
    sq = v * v
    top = jnp.full_like(v, ERF_TOP[0])
    for term in ERF_TOP[1:]:
        top = top * sq + term
    low = jnp.full_like(v, ERF_LOW[0])
    for term in ERF_LOW[1:]:
        low = low * sq + term
    return v * top / low


def half_cdf(pre):
    return 0.5 + 0.5 * erf(pre * (0.5**0.5))


def head_rows(dtype):
    lane = lax.broadcasted_iota(jnp.int32, (1, CH), 1)
    return [
        jnp.where((lane >= h * HEAD) & (lane < (h + 1) * HEAD), 1.0, 0.0).astype(dtype)
        for h in range(HEADS)
    ]


def stack_heads(pair):
    rows = head_rows(BF16)
    return tuple(jnp.concatenate([part * rows[h] for h in range(HEADS)], axis=0) for part in pair)


def turned(v, lanes):
    return jnp.concatenate([v[:, CH - lanes :], v[:, : CH - lanes]], axis=1)


def head_products(q, k):
    rows = head_rows(BF16)
    pairs = [rows[2 * r] + rows[2 * r + 1] for r in range(3)]
    q64, q128 = turned(q[1], 2 * HEAD), turned(q[0], 4 * HEAD)
    k64, k128 = turned(k[0], 2 * HEAD), turned(k[1], 4 * HEAD)
    out = []
    for r in range(3):
        right = k[0] * pairs[r] + k64 * pairs[(r + 1) % 3] + k128 * pairs[(r + 2) % 3]
        left = [
            q[0] * rows[h] + q64 * rows[(h + 2) % HEADS] + q128 * rows[(h + 4) % HEADS]
            for h in (2 * r, 2 * r + 1)
        ]
        out.append(dot(jnp.concatenate(left, axis=0), right, NT))
    return jnp.concatenate(out, axis=0)


def head_sums(p, v):
    half = CH // 2
    lane = lax.broadcasted_iota(jnp.int32, (1, CH), 1)
    lane = jnp.where(lane < half, lane, lane - half)
    out = []
    for group in range(2):
        lanes = slice(group * half, (group + 1) * half)
        rows = slice(group * STACK // 2, (group + 1) * STACK // 2)
        both = dot(p[0][rows], jnp.concatenate([v[0][:, lanes], v[1][:, lanes]], axis=1), NN)
        rest = dot(p[1][rows], v[0][:, lanes], NN)
        total, more = 0.0, 0.0
        for i in range(HEADS // 2):
            mine = jnp.where((lane >= i * HEAD) & (lane < (i + 1) * HEAD), 1.0, 0.0)
            total = total + both[i * TOK : (i + 1) * TOK] * mine
            more = more + rest[i * TOK : (i + 1) * TOK] * mine[:, 0:half]
        out.append(total[:, 0:half] + total[:, half:CH] + more)
    return jnp.concatenate(out, axis=1)


def place_matrix():
    mat = np.zeros((UPLANES, UPLANES), np.float32)
    for kl in range(LEVS):
        for kr in range(ROWS):
            for p in range(SPAN):
                mat[kl * CHUNK + kr * SPAN + p, p * CELLS + kr * LEVS + kl] = 1.0
    return jnp.asarray(mat, BF16)


def chunk_start(ql, kl, qr):
    return ((ql * LEVS + kl) * ROWS + qr) * CHUNK


def expand_bias(table_ref, place_ref, flat_ref, up_ref, bias_ref):
    flat_ref[...] = jnp.zeros_like(flat_ref)
    for h in range(HEADS):
        flat_ref[h : h + 1, 0:POS] = table_ref[0, h]
    lane = lax.broadcasted_iota(jnp.int32, (8, UPLANES), 1)
    for ql in range(LEVS):
        for qr in range(ROWS):
            g = qr * LEVS + ql
            row = jnp.zeros((8, UPLANES), F32)
            for kl in range(LEVS):
                start = chunk_start(ql, kl, qr)
                base = start // 128 * 128
                window = flat_ref[:, base : base + UPLANES]
                turn = (kl * CHUNK - (start - base)) % UPLANES
                if turn:
                    window = pltpu.roll(window, turn, 1)
                row = jnp.where((lane >= kl * CHUNK) & (lane < (kl + 1) * CHUNK), window, row)
            up_ref[g * 8 : (g + 1) * 8, :] = row
    ups = exact_dot(up_ref[...], place_ref[...], NN)
    for h in range(HEADS):
        rows = jnp.concatenate([ups[g * 8 + h : g * 8 + h + 1] for g in range(CELLS)], axis=0)
        for qc in range(COLS):
            turn = (-(COLS - 1 - qc) * CELLS) % UPLANES
            moved = pltpu.roll(rows, turn, 1) if turn else rows
            bias_ref[h * TOK + qc * CELLS : h * TOK + (qc + 1) * CELLS, :] = moved[:, 0:TOK]


def collect_table(dscore_ref, place_ref, up_ref, flat_ref):
    up_ref[...] = jnp.zeros_like(up_ref)
    for h in range(HEADS):
        total = jnp.zeros((CELLS, UPLANES), F32)
        for qc in range(COLS):
            block = dscore_ref[h * TOK + qc * CELLS : h * TOK + (qc + 1) * CELLS, :]
            block = jnp.concatenate([block, jnp.zeros((CELLS, UPLANES - TOK), F32)], axis=1)
            turn = (COLS - 1 - qc) * CELLS
            total = total + (pltpu.roll(block, turn, 1) if turn else block)
        for g in range(CELLS):
            up_ref[g * 8 + h : g * 8 + h + 1, :] = total[g : g + 1]
    raw = exact_dot(up_ref[...], place_ref[...], NT)
    flat_ref[...] = jnp.zeros_like(flat_ref)
    lane = lax.broadcasted_iota(jnp.int32, (8, UPLANES), 1)
    for ql in range(LEVS):
        for qr in range(ROWS):
            g = qr * LEVS + ql
            row = raw[g * 8 : (g + 1) * 8]
            for kl in range(LEVS):
                start = chunk_start(ql, kl, qr)
                base = start // 128 * 128
                shift = start - base
                turn = (shift - kl * CHUNK) % UPLANES
                moved = pltpu.roll(row, turn, 1) if turn else row
                keep = (lane >= shift) & (lane < shift + CHUNK)
                window = flat_ref[:, base : base + UPLANES]
                flat_ref[:, base : base + UPLANES] = jnp.where(keep, moved, window)


def window_masks(mask_ref, second):
    lev = lax.axis_index("lev")
    lat = lax.axis_index("lat")
    last_lev = lev == lax.axis_size("lev") - 1
    last_lat = lat == lax.axis_size("lat") - 1
    key_col = lax.broadcasted_iota(jnp.int32, (1, TOK), 1)
    key_row = lax.div(lax.rem(key_col, CELLS), LEVS)
    key_bias = jnp.zeros((1, TOK), F32)
    count = ROWS * lax.axis_size("lat")
    for r in range(ROWS):
        place = lat * ROWS + r
        if second:
            place = lax.rem(place + ROWS // 2, count)
        value = NEGATIVE * (1.0 - mask_ref[place].astype(F32))
        key_bias = jnp.where(key_row == r, value, key_bias)
    if not second:
        return key_bias, None

    def label(tokens):
        level = jnp.where(lax.rem(tokens, LEVS) >= LEVS // 2, 2, 0)
        row = jnp.where(lax.rem(tokens, CELLS) >= CELLS // 2, 1, 0)
        return level * last_lev.astype(jnp.int32) + row * last_lat.astype(jnp.int32)

    query = label(lax.broadcasted_iota(jnp.int32, (TOK, 1), 0))
    pair = jnp.where(query == label(key_col), 0.0, NEGATIVE).astype(F32)
    return key_bias, pair


def add_masks(scores, key_bias, pair):
    scores = scores + key_bias
    if pair is None:
        return scores
    return jnp.concatenate([scores[h * TOK : (h + 1) * TOK] + pair for h in range(HEADS)], axis=0)


def scaled_parts(qkv):
    return qkv[:, 0:CH] * SCALE, qkv[:, CH : 2 * CH], qkv[:, 2 * CH : 3 * CH]


def project(x, wq):
    normed, inv = norm(x)
    return normed, inv, dot3(halves(normed), wq, NN)


def attend(qkv, bias, key_bias, pair):
    q, k, v = scaled_parts(qkv)
    scores = add_masks(head_products(halves(q), halves(k)) + bias, key_bias, pair)
    grown = jnp.exp(scores - jnp.max(scores, axis=-1, keepdims=True))
    weights = grown * (1.0 / jnp.sum(grown, axis=-1, keepdims=True))
    return weights, head_sums(halves(weights), halves(v))


SIDE = COLS // 2
MAIN = ROWS // 2 * SIDE
WIDE = 56
THIN = 32
REST = CH - 128


MOVES = ((0, 0), (1, 0), (0, 1), (1, 1))


def six_rows(lev, j, k):
    for rr in range(ROWS // 2):
        yield rr, k * SIDE * CELLS + (j * (ROWS // 2) + rr) * LEVS + lev


def spread_pair(grid, out_refs):
    for (dlev, dj), out_ref in zip(MOVES, out_refs):
        for k in range(2):
            for rr, start in six_rows(1 - dlev, 1 - dj, k):
                rows = pl.ds(start, SIDE, stride=CELLS)
                for part, to in ((0, 0), (2, MAIN), (1, 2 * MAIN)):
                    out_ref[k, to + rr * SIDE : to + (rr + 1) * SIDE, :] = grid[part, rows, :]


def gather_pair(grid, own_refs, around_ref):
    for piece, (dlev, dj) in enumerate(MOVES):
        for k in range(2):
            ref, slot = (own_refs[piece], 1) if k == 0 else (around_ref, piece)
            for rr, start in six_rows(dlev, dj, k):
                rows = pl.ds(start, SIDE, stride=CELLS)
                for part, at in ((0, 0), (2, MAIN), (1, 2 * MAIN)):
                    grid[part, rows, :] = ref[slot, at + rr * SIDE : at + (rr + 1) * SIDE, :]


def spread_one(grid, out_refs):
    low = lax.broadcasted_iota(jnp.int32, (SIDE // 2, 128), 1) < REST
    for (dlev, dj), out_ref in zip(MOVES, out_refs):
        for k in range(2):
            for rr, start in six_rows(dlev, dj, k):
                rows = pl.ds(start, SIDE, stride=CELLS)
                out_ref[k, rr * SIDE : (rr + 1) * SIDE, :] = grid[0, rows, :]
                one = grid[1, pl.ds(start, SIDE // 2, stride=CELLS), :]
                two = grid[1, pl.ds(start + SIDE // 2 * CELLS, SIDE // 2, stride=CELLS), :]
                to = MAIN + rr * (SIDE // 2)
                out_ref[k, to : to + SIDE // 2, :] = jnp.where(low, one, pltpu.roll(two, REST, 1))


def gather_one(grid, own_refs, around_ref):
    for piece, (dlev, dj) in enumerate(MOVES):
        for k in range(2):
            ref, slot = (own_refs[piece], 0) if k == 1 else (around_ref, piece)
            for rr, start in six_rows(1 - dlev, 1 - dj, k):
                rows = pl.ds(start, SIDE, stride=CELLS)
                grid[0, rows, :] = ref[slot, rr * SIDE : (rr + 1) * SIDE, :]
                at = MAIN + rr * (SIDE // 2)
                both = ref[slot, at : at + SIDE // 2, :]
                grid[1, pl.ds(start, SIDE // 2, stride=CELLS), :] = both
                rows = pl.ds(start + SIDE // 2 * CELLS, SIDE // 2, stride=CELLS)
                grid[1, rows, :] = pltpu.roll(both, REST, 1)


def load_first(grid):
    return jnp.concatenate([grid[0], grid[1][:, 0:REST]], axis=1)


def load_second(grid):
    return jnp.concatenate([grid[2], grid[1][:, REST:128]], axis=1)


def store_first(grid, value):
    grid[0] = value[:, 0:128]
    grid[1, :, 0:REST] = value[:, 128:CH]


def load_window(x_ref, grid, second=False):
    head, at = (2, REST) if second else (0, 0)
    for r in range(ROWS):
        for c in range(COLS):
            rows = slice(c * CELLS + r * LEVS, c * CELLS + (r + 1) * LEVS)
            cell = x_ref[r, c]
            grid[head, rows, :] = cell[:, 0:128]
            grid[1, rows, at : at + REST] = cell[:, 128:CH]


def save_window(grid, out_ref):
    for r in range(ROWS):
        for c in range(COLS):
            rows = slice(c * CELLS + r * LEVS, c * CELLS + (r + 1) * LEVS)
            out_ref[r, c, :, 0:128] = grid[0, rows, :]
            out_ref[r, c, :, 128:CH] = grid[1, rows, 0:REST]


def first_forward(
    mask_hbm, x_hbm, cot_hbm, wq_hbm, wp_hbm, wu_hbm, wd_hbm, table_hbm, place_hbm,
    own_ref, lev_ref, lat_ref, both_ref, qkv_hbm, weights_hbm, attended_hbm, mid_hbm, pre_hbm,
    mask_ref, x_ref, cot_ref, wq_ref, wp_ref, wu_ref, wd_ref, table_ref, place_ref,
    grid_ref, flat_ref, up_ref, bias_ref, qkv_ref, weights_ref, attended_ref, mid_ref, pre_ref, sems,
    out_sems,
):
    pairs = (
        (x_hbm, x_ref),
        (wq_hbm.at[0], wq_ref),
        (table_hbm.at[0], table_ref),
        (place_hbm, place_ref),
        (mask_hbm, mask_ref),
        (wp_hbm.at[0], wp_ref),
        (wu_hbm.at[0], wu_ref),
        (wd_hbm.at[0], wd_ref),
        (cot_hbm, cot_ref),
    )
    copies = [pltpu.make_async_copy(*pair, sems.at[i]) for i, pair in enumerate(pairs)]
    for copy in copies:
        copy.start()
    copies[0].wait()
    load_window(x_ref, grid_ref)
    x = load_first(grid_ref)
    copies[1].wait()
    for copy in copies[2:5]:
        copy.wait()
    expand_bias(table_ref, place_ref, flat_ref, up_ref, bias_ref)
    key_bias, _ = window_masks(mask_ref, False)
    _, _, qkv = project(x, halves(wq_ref[...]))
    weights, attended = attend(qkv, bias_ref[...], key_bias, None)
    saved = []

    def save(value, ref, to):
        ref[...] = value
        saved.append(pltpu.make_async_copy(ref, to, out_sems.at[len(saved)]))
        saved[-1].start()

    save(qkv, qkv_ref, qkv_hbm)
    save(weights, weights_ref, weights_hbm)
    save(attended, attended_ref, attended_hbm)
    for copy in copies[5:]:
        copy.wait()
    mid = x + dot3(halves(attended), halves(wp_ref[...]), NN)
    save(mid, mid_ref, mid_hbm)
    normed, _ = norm(mid)
    pre = dot3(halves(normed), halves(wu_ref[...]), NN)
    save(pre, pre_ref, pre_hbm)
    hidden = pre * half_cdf(pre)
    load_window(cot_ref, grid_ref, True)
    store_first(grid_ref, mid + dot3(halves(hidden), halves(wd_ref[...]), NT))
    for copy in saved:
        copy.wait()
    spread_pair(grid_ref, (own_ref, lev_ref, lat_ref, both_ref))


def gelu_slope(pre, cdf):
    return cdf + pre * jnp.exp(-0.5 * pre * pre) * ((2.0 * np.pi) ** (-0.5))


def mlp_backward(g, slope, normed, inv, wu, wd):
    dpre = dot3(halves(g), wd, NN) * slope
    dnormed = dot3(halves(dpre), wu, NT)
    return dpre, g + norm_back(dnormed, normed, inv)


def attention_backward(dmid, qkv, weights, wp):
    q, k, v = scaled_parts(qkv)
    dattended = dot3(halves(dmid), wp, NT)
    dhalves = halves(dattended)
    dstack = stack_heads(dhalves)
    dweights = head_products(dhalves, halves(v))
    inner = jnp.sum(dweights * weights, axis=-1, keepdims=True)
    dscores = weights * (dweights - inner)
    ds = halves(dscores)
    dq = head_sums(ds, halves(k)) * SCALE
    dk = dot3(ds, stack_heads(halves(q)), TN)
    dv = dot3(halves(weights), dstack, TN)
    return dscores, jnp.concatenate([dq, dk, dv], axis=1)


def pack_gradients(keep_ref, send_ref, wide_ref, dqkv, dproj, dup, ddown, flat_ref):
    core = lax.rem(lax.axis_index("lon"), 2)
    wide_ref[0, :, 0 : 3 * CH] = dqkv
    wide_ref[0, :, 3 * CH : 4 * CH] = dproj
    wide_ref[1] = dup
    for share in range(2 * NZ):
        rows = [
            ddown[share * 48 + m * SHARE : share * 48 + (m + 1) * SHARE] for m in range(HID // CH)
        ]
        wide_ref[2, share * SHARE : (share + 1) * SHARE, :] = jnp.concatenate(rows, axis=1)
    even = core == 0
    for z in range(NZ):
        for group in range(GROUPS):
            first = wide_ref[group, 2 * SHARE * z : 2 * SHARE * z + SHARE, :]
            second = wide_ref[group, 2 * SHARE * z + SHARE : 2 * SHARE * (z + 1), :]
            rows = slice((z * GROUPS + group) * SHARE, (z * GROUPS + group + 1) * SHARE)
            keep_ref[rows, :] = jnp.where(even, first, second)
            send_ref[rows, :] = jnp.where(even, second, first)
    for ref in (keep_ref, send_ref):
        ref[GROWS:BUF, :] = jnp.zeros((TROWS, HID), F32)
    for z in range(NZ):
        first = table_share(flat_ref, 2 * z)
        second = table_share(flat_ref, 2 * z + 1)
        rows = slice(GROWS + z // 3 * 8, GROWS + z // 3 * 8 + 8)
        lanes = slice(z % 3 * 256, z % 3 * 256 + 256)
        keep_ref[rows, lanes] = jnp.where(even, first, second)
        send_ref[rows, lanes] = jnp.where(even, second, first)


def table_share(flat_ref, share):
    start = share * TSHARE
    base = start // 128 * 128
    window = flat_ref[:, base : base + UPLANES]
    if start - base:
        window = pltpu.roll(window, UPLANES - (start - base), 1)
    return window[:, 0:256]


def second_pass(
    own_ref, lev_ref, lat_ref, both_ref, around_ref, wq0_ref, wq1_ref, wp0_ref, wp1_ref, wu0_ref,
    wu1_ref, wd0_ref, wd1_ref, bias_ref, key_ref, pair_ref,
    back_own_ref, back_lev_ref, back_lat_ref, back_both_ref, dscores_ref, normed_ref, attended_ref, hnormed_ref, hidden_ref,
    g_ref, dpre_ref, dmid_ref, dqkv_ref,
    grid_ref,
):
    gather_pair(grid_ref, (own_ref, lev_ref, lat_ref, both_ref), around_ref)
    x = load_first(grid_ref)
    g = load_second(grid_ref)
    wq, wp = (wq0_ref[...], wq1_ref[...]), (wp0_ref[...], wp1_ref[...])
    wu, wd = (wu0_ref[...], wu1_ref[...]), (wd0_ref[...], wd1_ref[...])
    key_bias, pair = key_ref[0:1], pair_ref[...]
    normed, inv, qkv = project(x, wq)
    weights, attended = attend(qkv, bias_ref[...], key_bias, pair)
    normed_ref[...] = normed
    attended_ref[...] = attended
    mid = x + dot3(halves(attended), wp, NN)
    hnormed, hinv = norm(mid)
    hnormed_ref[...] = hnormed
    pre = dot3(halves(hnormed), wu, NN)
    cdf = half_cdf(pre)
    hidden_ref[...] = pre * cdf
    g_ref[...] = g
    dpre, dmid = mlp_backward(g, gelu_slope(pre, cdf), hnormed, hinv, wu, wd)
    dpre_ref[...] = dpre
    dmid_ref[...] = dmid
    dscores, dqkv = attention_backward(dmid, qkv, weights, wp)
    dscores_ref[...] = dscores
    dqkv_ref[...] = dqkv
    dx = dmid + norm_back(dot3(halves(dqkv), wq, NT), normed, inv)
    store_first(grid_ref, dx)
    spread_one(grid_ref, (back_own_ref, back_lev_ref, back_lat_ref, back_both_ref))


def second_gradients(
    dscores_ref, normed_ref, attended_ref, hnormed_ref, hidden_ref, g_ref, dpre_ref, dmid_ref,
    dqkv_ref, place_ref,
    keep_ref, send_ref,
    flat_ref, up_ref, wide_ref,
):
    collect_table(dscores_ref, place_ref, up_ref, flat_ref)
    pack_gradients(
        keep_ref, send_ref, wide_ref,
        weight_gradient(normed_ref[...], dqkv_ref[...]),
        weight_gradient(attended_ref[...], dmid_ref[...]),
        weight_gradient(hnormed_ref[...], dpre_ref[...]),
        weight_gradient(hidden_ref[...], g_ref[...]),
        flat_ref,
    )


def first_backward(
    own_ref, lev_ref, lat_ref, both_ref, around_ref, wp0_ref, wp1_ref, wu0_ref, wu1_ref, wd0_ref,
    wd1_ref, slope_ref, hidden_ref, hnormed_ref, hinv_ref, normed_ref, qkv_ref, weights_ref,
    attended_ref, place_ref,
    dmid_ref, dqkv_ref, gkeep_ref, gsend_ref,
    grid_ref, flat_ref, up_ref, wide_ref, dscores_ref,
):
    gather_one(grid_ref, (own_ref, lev_ref, lat_ref, both_ref), around_ref)
    g = load_first(grid_ref)
    wp = (wp0_ref[...], wp1_ref[...])
    wu, wd = (wu0_ref[...], wu1_ref[...]), (wd0_ref[...], wd1_ref[...])
    hnormed = hnormed_ref[...]
    dpre, dmid = mlp_backward(g, slope_ref[...], hnormed, hinv_ref[...], wu, wd)
    dup = weight_gradient(hnormed, dpre)
    ddown = weight_gradient(hidden_ref[...], g)
    dproj = weight_gradient(attended_ref[...], dmid)
    dscores, dqkv = attention_backward(dmid, qkv_ref[...], weights_ref[...], wp)
    dscores_ref[...] = dscores
    dmid_ref[...] = dmid
    dqkv_ref[...] = dqkv
    collect_table(dscores_ref, place_ref, up_ref, flat_ref)
    pack_gradients(
        gkeep_ref, gsend_ref, wide_ref,
        weight_gradient(normed_ref[...], dqkv), dproj, dup, ddown, flat_ref,
    )


def first_prepare(
    x_ref, mid_ref, pre_ref, wp_ref, wu_ref, wd_ref,
    wp0_ref, wp1_ref, wu0_ref, wu1_ref, wd0_ref, wd1_ref, slope_ref, hidden_ref, hnormed_ref, hinv_ref,
    normed_ref,
    grid_ref,
):
    split_into(((wp_ref, wp0_ref, wp1_ref), (wu_ref, wu0_ref, wu1_ref), (wd_ref, wd0_ref, wd1_ref)))
    pre = pre_ref[...]
    cdf = half_cdf(pre)
    slope_ref[...] = gelu_slope(pre, cdf)
    hidden_ref[...] = pre * cdf
    hnormed_ref[...], hinv_ref[...] = norm(mid_ref[...])
    load_window(x_ref, grid_ref)
    normed_ref[...], _ = norm(load_first(grid_ref))


def split_into(triples):
    for ref, high_ref, low_ref in triples:
        high_ref[...], low_ref[...] = halves(ref[...])


def input_gradient(x_ref, wq_ref, dmid_ref, dqkv_ref, grad_ref, grid_ref):
    load_window(x_ref, grid_ref)
    normed, inv = norm(load_first(grid_ref))
    dnormed = dot3(halves(dqkv_ref[...]), halves(wq_ref[...]), NT)
    store_first(grid_ref, dmid_ref[...] + norm_back(dnormed, normed, inv))
    save_window(grid_ref, grad_ref)


def split_weights(
    wq_ref, wp_ref, wu_ref, wd_ref,
    wq0_ref, wq1_ref, wp0_ref, wp1_ref, wu0_ref, wu1_ref, wd0_ref, wd1_ref,
):
    split_into(
        (
            (wq_ref, wq0_ref, wq1_ref),
            (wp_ref, wp0_ref, wp1_ref),
            (wu_ref, wu0_ref, wu1_ref),
            (wd_ref, wd0_ref, wd1_ref),
        )
    )


def second_prepare(
    mask_ref, table_ref, place_ref, bias_ref, key_ref, pair_ref, flat_ref, up_ref
):
    expand_bias(table_ref, place_ref, flat_ref, up_ref, bias_ref)
    key_bias, pair = window_masks(mask_ref, True)
    key_ref[...] = jnp.broadcast_to(key_bias, (8, TOK))
    pair_ref[...] = pair


def unit_parts(block):
    for tile in range(18):
        number = block * 18 + tile
        if number < 32:
            yield number // 2, number % 2 * SHARE, SHARE, tile, 0
        else:
            for quarter in range(4):
                yield (number - 32) * 4 + quarter, 2 * SHARE, SHARE // 4, tile, quarter * (SHARE // 4)


def table_place(z):
    return slice(GROWS + z // 3 * 8, GROWS + z // 3 * 8 + 8), slice(z % 3 * 256, z % 3 * 256 + 256)


def join(mine0_ref, theirs0_ref, mine1_ref, theirs1_ref, plane_ref, table_ref, sum_ref):
    for block, (mine_ref, theirs_ref) in enumerate(((mine0_ref, theirs0_ref), (mine1_ref, theirs1_ref))):
        sum_ref[...] = mine_ref[...] + theirs_ref[...]
        for z in range(NZ):
            for p, at, count, tile, start in unit_parts(block):
                start = (z * GROUPS + tile // 6) * SHARE + start
                lanes = slice(tile % 6 * 128, tile % 6 * 128 + 128)
                at = z * UNIT + at
                plane_ref[p, at : at + count, :] = sum_ref[start : start + count, lanes]
            table = sum_ref[table_place(z)]
            for half in range(2):
                to = block * TABLE_ROWS + half * HEADS
                table_ref[z, to : to + HEADS, :] = table[0:HEADS, half * 128 : half * 128 + 128]


def plane_sum(got_ref, table_ref, out_ref, sum_ref):
    total = got_ref[0]
    for p in range(1, PLANE):
        total = total + got_ref[p]
    sum_ref[...] = total
    used = UNIT + 2 * TABLE_ROWS
    for z in range(NZ):
        out_ref[z, 0:UNIT, :] = sum_ref[z * UNIT : (z + 1) * UNIT, :]
        out_ref[z, UNIT:used, :] = table_ref[z]
        out_ref[z, used:LON_ROWS, :] = jnp.zeros((LON_ROWS - used, 128), F32)


def lon_sum(got_ref, out_ref):
    total = got_ref[0, 0:32, :]
    for z in range(1, NZ):
        total = total + got_ref[z, 0:32, :]
    for p in range(PLANE):
        out_ref[p] = total


def table_sum(got_ref, table_ref, sum_ref):
    total = got_ref[0]
    for z in range(1, NZ):
        total = total + got_ref[z]
    sum_ref[...] = total
    for block in range(2):
        for h in range(HEADS):
            row = UNIT + block * TABLE_ROWS + h
            table_ref[block, 0, h, :, 0:128] = sum_ref[row : row + 1, :]
            row = row + HEADS
            table_ref[block, 0, h, :, 128:TSHARE] = sum_ref[row : row + 1, 0 : TSHARE - 128]


def unpack(scale, got_ref, qkv_ref, proj_ref, up_ref, down_ref, wide_ref):
    for block in range(2):
        for p, at, count, tile, to in unit_parts(block):
            lanes = slice(tile % 6 * 128, tile % 6 * 128 + 128)
            wide_ref[block, tile // 6, to : to + count, lanes] = got_ref[p, at : at + count, :] * scale
        for row in range(SHARE):
            at = slice(row, row + 1)
            qkv_ref[row, block : block + 1, :] = wide_ref[block, 0, at, 0 : 3 * CH]
            proj_ref[row, block : block + 1, :] = wide_ref[block, 0, at, 3 * CH : 4 * CH]
            up_ref[row, block : block + 1, :] = wide_ref[block, 1, at, :]
        for m in range(HID // CH):
            down_ref[block, m * SHARE : (m + 1) * SHARE, :] = wide_ref[
                block, 2, 0:SHARE, m * CH : (m + 1) * CH
            ]


WEIGHTS = ((CH, 3 * CH), (CH, CH), (CH, HID), (CH, HID))


def struct(*shape, dtype=F32):
    return jax.ShapeDtypeStruct(shape, dtype)


def vmem(*shape):
    return pltpu.VMEM(shape, F32)


def whole(*shape):
    return pl.BlockSpec(shape, lambda i: (0,) * len(shape))


def part_of(block, *shape):
    return pl.BlockSpec((None,) + shape, lambda i: (block,) + (0,) * len(shape))


def weight_specs(block):
    return [
        part_of(block, CH, 3 * CH),
        part_of(block, CH, CH),
        part_of(block, CH, HID),
        part_of(block, CH, HID),
    ]


def table_spec(block):
    return part_of(block, 1, HEADS, 1, POS)


def call(body, in_specs, outs, scratch, cost=0, mib=28, far=0):
    near = [whole(*o.shape) for o in outs[: len(outs) - far]]
    return pl.pallas_call(
        body,
        grid=(1,),
        in_specs=in_specs,
        out_specs=near + [HBM] * far,
        out_shape=outs,
        scratch_shapes=scratch,
        compiler_params=params(mib),
        cost_estimate=pl.CostEstimate(flops=cost, bytes_accessed=4 * 2**20, transcendentals=0),
    )


SMEM = pl.BlockSpec(memory_space=pltpu.SMEM)
HBM = pl.BlockSpec(memory_space=pltpu.HBM)
FLAT = 3456


def shifted(block, axis, distance):
    devices = range(lax.axis_size(axis))
    route = [((i - distance) % len(devices), i) for i in devices]
    return lax.ppermute(block, axis, route)


def shifted_plane(block, levels, rows):
    size = lax.axis_size("lev")
    count = lax.axis_size("lat")
    route = [
        (lat * size + lev, (lat + rows) % count * size + (lev + levels) % size)
        for lat in range(count)
        for lev in range(size)
    ]
    return lax.ppermute(block, ("lat", "lev"), route)


def exchange(pieces, step, side, first=None):
    held = [pieces[0]] + [
        shifted_plane(piece, step * dlev, step * dlat)
        for piece, (dlev, dlat) in zip(pieces[1:], MOVES[1:])
    ]
    edge = jnp.stack([piece[side] for piece in held])
    if first is not None:
        edge, first = lax.optimization_barrier((edge, first))
    return held + [shifted(edge, "lon", step)], first


def swap_cores(v):
    return lax.ppermute(v, "lon", [(i, i ^ 1) for i in range(lax.axis_size("lon"))])


def local(inputs, cotangent, qkv_weight, proj_weight, up_weight, down_weight, bias_table, lat_mask):
    place = place_matrix()
    x = inputs.transpose(1, 2, 0, 3)
    cot = cotangent.transpose(1, 2, 0, 3)
    table = bias_table.transpose(0, 1, 3, 2, 4)
    weights = (qkv_weight, proj_weight, up_weight, down_weight.transpose(0, 2, 1))
    grid_spec = whole(ROWS, COLS, LEVS, CH)
    wide_scratch = [vmem(8, FLAT), vmem(8 * CELLS, UPLANES)]
    half = (2, WIDE, 128)
    *pieces, qkv, attention, attended, mid, pre = call(
        first_forward,
        [HBM] * 9,
        [struct(*half)] * 4
        + [
            struct(TOK, 3 * CH),
            struct(STACK, TOK),
            struct(TOK, CH),
            struct(TOK, CH),
            struct(TOK, HID),
        ],
        [
            pltpu.SMEM((8 * ROWS,), jnp.int32),
            vmem(ROWS, COLS, LEVS, CH),
            vmem(ROWS, COLS, LEVS, CH),
            vmem(CH, 3 * CH),
            vmem(CH, CH),
            vmem(CH, HID),
            vmem(CH, HID),
            vmem(1, HEADS, 1, POS),
            pltpu.VMEM((UPLANES, UPLANES), BF16),
            vmem(3, TOK, 128),
        ]
        + wide_scratch
        + [
            vmem(STACK, TOK),
            vmem(TOK, 3 * CH),
            vmem(STACK, TOK),
            vmem(TOK, CH),
            vmem(TOK, CH),
            vmem(TOK, HID),
            pltpu.SemaphoreType.DMA((9,)),
            pltpu.SemaphoreType.DMA((5,)),
        ],
        cost=500_000_000,
        mib=60,
        far=5,
    )(lat_mask, x, cot, *weights, table, place)
    prepared = call(
        second_prepare,
        [SMEM, table_spec(1), whole(UPLANES, UPLANES)],
        [struct(STACK, TOK), struct(8, TOK), struct(TOK, TOK)],
        wide_scratch,
        cost=200_000_000,
    )(lat_mask, table, place)
    split = call(
        split_weights,
        weight_specs(1),
        [struct(*shape, dtype=BF16) for shape in WEIGHTS for _ in range(2)],
        [],
        cost=200_000_000,
    )(*weights)
    held, prepared = exchange(pieces, -1, 0, prepared)
    around = (4, WIDE, 128)
    back_half = (2, THIN, 128)
    back_around = (4, THIN, 128)
    factors = [
        struct(STACK, TOK),
        struct(TOK, CH),
        struct(TOK, CH),
        struct(TOK, CH),
        struct(TOK, HID),
        struct(TOK, CH),
        struct(TOK, HID),
        struct(TOK, CH),
        struct(TOK, 3 * CH),
    ]
    second = call(
        second_pass,
        [whole(*half)] * 4
        + [whole(*around)]
        + [whole(*shape) for shape in WEIGHTS for _ in range(2)]
        + [whole(STACK, TOK), whole(8, TOK), whole(TOK, TOK)],
        [struct(*back_half)] * 4 + factors,
        [vmem(3, TOK, 128)],
        cost=1_000_000_000,
    )(*held, *split, *prepared)
    back_pieces, saved = second[:4], second[4:]
    keep2, send2 = call(
        second_gradients,
        [whole(*f.shape) for f in factors] + [whole(UPLANES, UPLANES)],
        [struct(BUF, HID), struct(BUF, HID)],
        wide_scratch + [vmem(GROUPS, CH, HID)],
        cost=500_000_000,
    )(*saved, place)
    back_held, send2 = exchange(back_pieces, 1, 1, send2)
    pre, _ = lax.optimization_barrier((pre, back_pieces[0]))
    ready = [struct(*shape, dtype=BF16) for shape in WEIGHTS[1:] for _ in range(2)] + [
        struct(TOK, HID),
        struct(TOK, HID),
        struct(TOK, CH),
        struct(TOK, 1),
        struct(TOK, CH),
    ]
    first_ready = call(
        first_prepare,
        [grid_spec, whole(TOK, CH), whole(TOK, HID)] + weight_specs(0)[1:],
        ready,
        [vmem(3, TOK, 128)],
        cost=200_000_000,
    )(x, mid, pre, *weights[1:])
    send2, slope = lax.optimization_barrier((send2, first_ready[6]))
    first_ready = list(first_ready[:6]) + [slope] + list(first_ready[7:])
    got2 = swap_cores(send2)
    dmid, dqkv, keep1, send1 = call(
        first_backward,
        [whole(*back_half)] * 4
        + [whole(*back_around)]
        + [whole(*r.shape) for r in ready]
        + [
            whole(TOK, 3 * CH),
            whole(STACK, TOK),
            whole(TOK, CH),
            whole(UPLANES, UPLANES),
        ],
        [struct(TOK, CH), struct(TOK, 3 * CH), struct(BUF, HID), struct(BUF, HID)],
        [vmem(3, TOK, 128)] + wide_scratch + [vmem(GROUPS, CH, HID), vmem(STACK, TOK)],
        cost=1_000_000_000,
    )(
        *back_held, *first_ready, qkv, attention, attended, place,
    )
    (grad_input,) = call(
        input_gradient,
        [grid_spec, weight_specs(0)[0], whole(TOK, CH), whole(TOK, 3 * CH)],
        [struct(ROWS, COLS, LEVS, CH)],
        [vmem(3, TOK, 128)],
        cost=100_000_000,
    )(x, weights[0], dmid, dqkv)
    got1 = swap_cores(send1)
    keep1, grad_input = lax.optimization_barrier((keep1, grad_input))
    for_plane, table_part = call(
        join,
        [whole(BUF, HID)] * 4,
        [struct(PLANE, NZ * UNIT, 128), struct(NZ, 2 * TABLE_ROWS, 128)],
        [vmem(BUF, HID)],
    )(keep1, got1, keep2, got2)
    plane_got = lax.all_to_all(for_plane, ("lat", "lev"), 0, 0, tiled=True)
    (for_lon,) = call(
        plane_sum,
        [whole(PLANE, NZ * UNIT, 128), whole(NZ, 2 * TABLE_ROWS, 128)],
        [struct(NZ, LON_ROWS, 128)],
        [vmem(NZ * UNIT, 128)],
    )(plane_got, table_part)
    core_groups = [[z * 2 + c for z in range(NZ)] for c in range(2)]
    lon_got = lax.all_to_all(
        for_lon, "lon", 0, 0, axis_index_groups=core_groups, tiled=True
    )
    (copies,) = call(lon_sum, [whole(NZ, LON_ROWS, 128)], [struct(PLANE, 32, 128)], [])(lon_got)
    (grad_table,) = call(
        table_sum,
        [whole(NZ, LON_ROWS, 128)],
        [struct(2, 1, HEADS, 1, TSHARE)],
        [vmem(LON_ROWS, 128)],
    )(lon_got)
    shares = lax.all_to_all(copies, ("lat", "lev"), 0, 0, tiled=True)
    tokens = TOK * lax.axis_size("lon") * lax.axis_size("lat") * lax.axis_size("lev")
    grad_qkv, grad_proj, grad_up, grad_down = call(
        lambda *refs: unpack(float(tokens) ** (-0.5), *refs),
        [whole(PLANE, 32, 128)],
        [
            struct(SHARE, 2, 3 * CH),
            struct(SHARE, 2, CH),
            struct(SHARE, 2, HID),
            struct(2, 48, CH),
        ],
        [vmem(2, GROUPS, 16, HID)],
    )(shares)
    return (
        grad_input.transpose(2, 0, 1, 3),
        grad_qkv.transpose(1, 0, 2),
        grad_proj.transpose(1, 0, 2),
        grad_up.transpose(1, 0, 2),
        grad_down,
        grad_table.transpose(0, 1, 3, 2, 4),
    )


def solution(mesh):
    in_specs = (
        P("lev", "lat", "lon", None),
        P("lev", "lat", "lon", None),
        P(),
        P(),
        P(),
        P(),
        P(None, "lev", "lat", None, None),
        P(),
    )
    out_specs = (
        P("lev", "lat", "lon", None),
        P(None, "lon", None),
        P(None, "lon", None),
        P(None, "lon", None),
        P(None, "lon", None),
        P(None, "lev", "lat", None, "lon"),
    )
    return jax.shard_map(local, mesh=mesh, in_specs=in_specs, out_specs=out_specs, check_vma=False)
```

```python
import jax
import jax.numpy as jnp
import numpy as np
from jax import lax
from jax.experimental import pallas as pl
from jax.experimental.pallas import tpu as pltpu
from jax.sharding import PartitionSpec as P

F32 = jnp.float32
BF16 = jnp.bfloat16

HEADS = 6
HEAD = 32
CH = 192
HID = 768
LEVS = 2
ROWS = 6
COLS = 12
CELLS = LEVS * ROWS
TOK = CELLS * COLS
STACK = HEADS * TOK
SPAN = 2 * COLS - 1
POS = 3312
CHUNK = ROWS * SPAN
UPLANES = 384
NEGATIVE = -10000.0
SCALE = HEAD ** (-0.5)

NZ = 8
SHARE = 12
GROUPS = 3
GROWS = NZ * GROUPS * SHARE
TROWS = 24
BUF = GROWS + TROWS
TSHARE = POS // 16
PLANE = 16
UNIT = 27
TABLE_ROWS = 2 * HEADS
LON_ROWS = 56

NN = ((1,), (0,))
NT = ((1,), (1,))
TN = ((0,), (0,))


def params(mib=28):
    return pltpu.CompilerParams(vmem_limit_bytes=mib * 1024 * 1024)


def halves(v):
    top = v.astype(BF16)
    return top, (v - top.astype(F32)).astype(BF16)


def thirds(v):
    top = v.astype(BF16)
    rest = v - top.astype(F32)
    mid = rest.astype(BF16)
    return top, mid, (rest - mid.astype(F32)).astype(BF16)


def dot(a, b, dims):
    return lax.dot_general(a, b, (dims, ((), ())), preferred_element_type=F32)


def dot3(a, b, dims):
    return dot(a[0], b[0], dims) + (dot(a[0], b[1], dims) + dot(a[1], b[0], dims))


def weight_gradient(a, b):
    a, b = halves(a), halves(b)
    left = jnp.concatenate([a[0], a[0], a[1]], axis=0)
    return dot(left, jnp.concatenate([b[0], b[1], b[0]], axis=0), TN)


def exact_dot(v, one_hot, dims):
    a, b, c = thirds(v)
    return (dot(a, one_hot, dims) + dot(b, one_hot, dims)) + dot(c, one_hot, dims)


def norm(v):
    centered = v - jnp.mean(v, axis=-1, keepdims=True)
    inv = lax.rsqrt(jnp.mean(centered * centered, axis=-1, keepdims=True) + 1e-05)
    return centered * inv, inv


def norm_back(d, normed, inv):
    return inv * (
        d
        - jnp.mean(d, axis=-1, keepdims=True)
        - normed * jnp.mean(d * normed, axis=-1, keepdims=True)
    )


ERF_TOP = (
    0.00022905065861350646,
    0.0034082910107109506,
    0.050955695062380861,
    0.18520832239976145,
    1.128379143519084,
)
ERF_LOW = (
    -1.1791602954361697e-7,
    0.000023547966471313185,
    0.0010179625278914885,
    0.014070470171167667,
    0.11098505178285362,
    0.49746925110067538,
    1.0,
)


def erf(v):
    v = jnp.clip(v, -3.832506856900711, 3.832506856900711)
    sq = v * v
    top = jnp.full_like(v, ERF_TOP[0])
    for term in ERF_TOP[1:]:
        top = top * sq + term
    low = jnp.full_like(v, ERF_LOW[0])
    for term in ERF_LOW[1:]:
        low = low * sq + term
    return v * top / low


def half_cdf(pre):
    return 0.5 + 0.5 * erf(pre * (0.5**0.5))


def head_rows(dtype):
    lane = lax.broadcasted_iota(jnp.int32, (1, CH), 1)
    return [
        jnp.where((lane >= h * HEAD) & (lane < (h + 1) * HEAD), 1.0, 0.0).astype(dtype)
        for h in range(HEADS)
    ]


def stack_heads(pair):
    rows = head_rows(BF16)
    return tuple(jnp.concatenate([part * rows[h] for h in range(HEADS)], axis=0) for part in pair)


def turned(v, lanes):
    return jnp.concatenate([v[:, CH - lanes :], v[:, : CH - lanes]], axis=1)


def head_products(q, k):
    rows = head_rows(BF16)
    pairs = [rows[2 * r] + rows[2 * r + 1] for r in range(3)]
    q64, q128 = turned(q[1], 2 * HEAD), turned(q[0], 4 * HEAD)
    k64, k128 = turned(k[0], 2 * HEAD), turned(k[1], 4 * HEAD)
    out = []
    for r in range(3):
        right = k[0] * pairs[r] + k64 * pairs[(r + 1) % 3] + k128 * pairs[(r + 2) % 3]
        left = [
            q[0] * rows[h] + q64 * rows[(h + 2) % HEADS] + q128 * rows[(h + 4) % HEADS]
            for h in (2 * r, 2 * r + 1)
        ]
        out.append(dot(jnp.concatenate(left, axis=0), right, NT))
    return jnp.concatenate(out, axis=0)


def head_sums(p, v):
    half = CH // 2
    lane = lax.broadcasted_iota(jnp.int32, (1, CH), 1)
    lane = jnp.where(lane < half, lane, lane - half)
    out = []
    for group in range(2):
        lanes = slice(group * half, (group + 1) * half)
        rows = slice(group * STACK // 2, (group + 1) * STACK // 2)
        both = dot(p[0][rows], jnp.concatenate([v[0][:, lanes], v[1][:, lanes]], axis=1), NN)
        rest = dot(p[1][rows], v[0][:, lanes], NN)
        total, more = 0.0, 0.0
        for i in range(HEADS // 2):
            mine = jnp.where((lane >= i * HEAD) & (lane < (i + 1) * HEAD), 1.0, 0.0)
            total = total + both[i * TOK : (i + 1) * TOK] * mine
            more = more + rest[i * TOK : (i + 1) * TOK] * mine[:, 0:half]
        out.append(total[:, 0:half] + total[:, half:CH] + more)
    return jnp.concatenate(out, axis=1)


def place_matrix():
    mat = np.zeros((UPLANES, UPLANES), np.float32)
    for kl in range(LEVS):
        for kr in range(ROWS):
            for p in range(SPAN):
                mat[kl * CHUNK + kr * SPAN + p, p * CELLS + kr * LEVS + kl] = 1.0
    return jnp.asarray(mat, BF16)


def chunk_start(ql, kl, qr):
    return ((ql * LEVS + kl) * ROWS + qr) * CHUNK


def expand_bias(table_ref, place_ref, flat_ref, up_ref, bias_ref):
    flat_ref[...] = jnp.zeros_like(flat_ref)
    for h in range(HEADS):
        flat_ref[h : h + 1, 0:POS] = table_ref[0, h]
    lane = lax.broadcasted_iota(jnp.int32, (8, UPLANES), 1)
    for ql in range(LEVS):
        for qr in range(ROWS):
            g = qr * LEVS + ql
            row = jnp.zeros((8, UPLANES), F32)
            for kl in range(LEVS):
                start = chunk_start(ql, kl, qr)
                base = start // 128 * 128
                window = flat_ref[:, base : base + UPLANES]
                turn = (kl * CHUNK - (start - base)) % UPLANES
                if turn:
                    window = pltpu.roll(window, turn, 1)
                row = jnp.where((lane >= kl * CHUNK) & (lane < (kl + 1) * CHUNK), window, row)
            up_ref[g * 8 : (g + 1) * 8, :] = row
    ups = exact_dot(up_ref[...], place_ref[...], NN)
    for h in range(HEADS):
        rows = jnp.concatenate([ups[g * 8 + h : g * 8 + h + 1] for g in range(CELLS)], axis=0)
        for qc in range(COLS):
            turn = (-(COLS - 1 - qc) * CELLS) % UPLANES
            moved = pltpu.roll(rows, turn, 1) if turn else rows
            bias_ref[h * TOK + qc * CELLS : h * TOK + (qc + 1) * CELLS, :] = moved[:, 0:TOK]


def collect_table(dscore_ref, place_ref, up_ref, flat_ref):
    up_ref[...] = jnp.zeros_like(up_ref)
    for h in range(HEADS):
        total = jnp.zeros((CELLS, UPLANES), F32)
        for qc in range(COLS):
            block = dscore_ref[h * TOK + qc * CELLS : h * TOK + (qc + 1) * CELLS, :]
            block = jnp.concatenate([block, jnp.zeros((CELLS, UPLANES - TOK), F32)], axis=1)
            turn = (COLS - 1 - qc) * CELLS
            total = total + (pltpu.roll(block, turn, 1) if turn else block)
        for g in range(CELLS):
            up_ref[g * 8 + h : g * 8 + h + 1, :] = total[g : g + 1]
    raw = exact_dot(up_ref[...], place_ref[...], NT)
    flat_ref[...] = jnp.zeros_like(flat_ref)
    lane = lax.broadcasted_iota(jnp.int32, (8, UPLANES), 1)
    for ql in range(LEVS):
        for qr in range(ROWS):
            g = qr * LEVS + ql
            row = raw[g * 8 : (g + 1) * 8]
            for kl in range(LEVS):
                start = chunk_start(ql, kl, qr)
                base = start // 128 * 128
                shift = start - base
                turn = (shift - kl * CHUNK) % UPLANES
                moved = pltpu.roll(row, turn, 1) if turn else row
                keep = (lane >= shift) & (lane < shift + CHUNK)
                window = flat_ref[:, base : base + UPLANES]
                flat_ref[:, base : base + UPLANES] = jnp.where(keep, moved, window)


def window_masks(mask_ref, second):
    lev = lax.axis_index("lev")
    lat = lax.axis_index("lat")
    last_lev = lev == lax.axis_size("lev") - 1
    last_lat = lat == lax.axis_size("lat") - 1
    key_col = lax.broadcasted_iota(jnp.int32, (1, TOK), 1)
    key_row = lax.div(lax.rem(key_col, CELLS), LEVS)
    key_bias = jnp.zeros((1, TOK), F32)
    count = ROWS * lax.axis_size("lat")
    for r in range(ROWS):
        place = lat * ROWS + r
        if second:
            place = lax.rem(place + ROWS // 2, count)
        value = NEGATIVE * (1.0 - mask_ref[place].astype(F32))
        key_bias = jnp.where(key_row == r, value, key_bias)
    if not second:
        return key_bias, None

    def label(tokens):
        level = jnp.where(lax.rem(tokens, LEVS) >= LEVS // 2, 2, 0)
        row = jnp.where(lax.rem(tokens, CELLS) >= CELLS // 2, 1, 0)
        return level * last_lev.astype(jnp.int32) + row * last_lat.astype(jnp.int32)

    query = label(lax.broadcasted_iota(jnp.int32, (TOK, 1), 0))
    pair = jnp.where(query == label(key_col), 0.0, NEGATIVE).astype(F32)
    return key_bias, pair


def add_masks(scores, key_bias, pair):
    scores = scores + key_bias
    if pair is None:
        return scores
    return jnp.concatenate([scores[h * TOK : (h + 1) * TOK] + pair for h in range(HEADS)], axis=0)


def scaled_parts(qkv):
    return qkv[:, 0:CH] * SCALE, qkv[:, CH : 2 * CH], qkv[:, 2 * CH : 3 * CH]


def project(x, wq):
    normed, inv = norm(x)
    return normed, inv, dot3(halves(normed), wq, NN)


def attend(qkv, bias, key_bias, pair):
    q, k, v = scaled_parts(qkv)
    scores = add_masks(head_products(halves(q), halves(k)) + bias, key_bias, pair)
    grown = jnp.exp(scores - jnp.max(scores, axis=-1, keepdims=True))
    weights = grown * (1.0 / jnp.sum(grown, axis=-1, keepdims=True))
    return weights, head_sums(halves(weights), halves(v))


SIDE = COLS // 2
MAIN = ROWS // 2 * SIDE
WIDE = 56
THIN = 32
REST = CH - 128


MOVES = ((0, 0), (1, 0), (0, 1), (1, 1))


def six_rows(lev, j, k):
    for rr in range(ROWS // 2):
        yield rr, k * SIDE * CELLS + (j * (ROWS // 2) + rr) * LEVS + lev


def spread_pair(grid, out_refs):
    for (dlev, dj), out_ref in zip(MOVES, out_refs):
        for k in range(2):
            for rr, start in six_rows(1 - dlev, 1 - dj, k):
                rows = pl.ds(start, SIDE, stride=CELLS)
                for part, to in ((0, 0), (2, MAIN), (1, 2 * MAIN)):
                    out_ref[k, to + rr * SIDE : to + (rr + 1) * SIDE, :] = grid[part, rows, :]


def gather_pair(grid, own_refs, around_ref):
    for piece, (dlev, dj) in enumerate(MOVES):
        for k in range(2):
            ref, slot = (own_refs[piece], 1) if k == 0 else (around_ref, piece)
            for rr, start in six_rows(dlev, dj, k):
                rows = pl.ds(start, SIDE, stride=CELLS)
                for part, at in ((0, 0), (2, MAIN), (1, 2 * MAIN)):
                    grid[part, rows, :] = ref[slot, at + rr * SIDE : at + (rr + 1) * SIDE, :]


def spread_one(grid, out_refs):
    low = lax.broadcasted_iota(jnp.int32, (SIDE // 2, 128), 1) < REST
    for (dlev, dj), out_ref in zip(MOVES, out_refs):
        for k in range(2):
            for rr, start in six_rows(dlev, dj, k):
                rows = pl.ds(start, SIDE, stride=CELLS)
                out_ref[k, rr * SIDE : (rr + 1) * SIDE, :] = grid[0, rows, :]
                one = grid[1, pl.ds(start, SIDE // 2, stride=CELLS), :]
                two = grid[1, pl.ds(start + SIDE // 2 * CELLS, SIDE // 2, stride=CELLS), :]
                to = MAIN + rr * (SIDE // 2)
                out_ref[k, to : to + SIDE // 2, :] = jnp.where(low, one, pltpu.roll(two, REST, 1))


def gather_one(grid, own_refs, around_ref):
    for piece, (dlev, dj) in enumerate(MOVES):
        for k in range(2):
            ref, slot = (own_refs[piece], 0) if k == 1 else (around_ref, piece)
            for rr, start in six_rows(1 - dlev, 1 - dj, k):
                rows = pl.ds(start, SIDE, stride=CELLS)
                grid[0, rows, :] = ref[slot, rr * SIDE : (rr + 1) * SIDE, :]
                at = MAIN + rr * (SIDE // 2)
                both = ref[slot, at : at + SIDE // 2, :]
                grid[1, pl.ds(start, SIDE // 2, stride=CELLS), :] = both
                rows = pl.ds(start + SIDE // 2 * CELLS, SIDE // 2, stride=CELLS)
                grid[1, rows, :] = pltpu.roll(both, REST, 1)


def load_first(grid):
    return jnp.concatenate([grid[0], grid[1][:, 0:REST]], axis=1)


def load_second(grid):
    return jnp.concatenate([grid[2], grid[1][:, REST:128]], axis=1)


def store_first(grid, value):
    grid[0] = value[:, 0:128]
    grid[1, :, 0:REST] = value[:, 128:CH]


def load_window(x_ref, grid, second=False):
    head, at = (2, REST) if second else (0, 0)
    for r in range(ROWS):
        for c in range(COLS):
            rows = slice(c * CELLS + r * LEVS, c * CELLS + (r + 1) * LEVS)
            cell = x_ref[r, c]
            grid[head, rows, :] = cell[:, 0:128]
            grid[1, rows, at : at + REST] = cell[:, 128:CH]


def save_window(grid, out_ref):
    for r in range(ROWS):
        for c in range(COLS):
            rows = slice(c * CELLS + r * LEVS, c * CELLS + (r + 1) * LEVS)
            out_ref[r, c, :, 0:128] = grid[0, rows, :]
            out_ref[r, c, :, 128:CH] = grid[1, rows, 0:REST]


def first_forward(
    mask_hbm, x_hbm, cot_hbm, wq_hbm, wp_hbm, wu_hbm, wd_hbm, table_hbm, place_hbm,
    own_ref, lev_ref, lat_ref, both_ref, qkv_hbm, weights_hbm, attended_hbm, mid_hbm, pre_hbm,
    mask_ref, x_ref, cot_ref, wq_ref, wp_ref, wu_ref, wd_ref, table_ref, place_ref,
    grid_ref, flat_ref, up_ref, bias_ref, qkv_ref, weights_ref, attended_ref, mid_ref, pre_ref, sems,
    out_sems,
):
    pairs = (
        (x_hbm, x_ref),
        (wq_hbm.at[0], wq_ref),
        (table_hbm.at[0], table_ref),
        (place_hbm, place_ref),
        (mask_hbm, mask_ref),
        (wp_hbm.at[0], wp_ref),
        (wu_hbm.at[0], wu_ref),
        (wd_hbm.at[0], wd_ref),
        (cot_hbm, cot_ref),
    )
    copies = [pltpu.make_async_copy(*pair, sems.at[i]) for i, pair in enumerate(pairs)]
    for copy in copies:
        copy.start()
    copies[0].wait()
    load_window(x_ref, grid_ref)
    x = load_first(grid_ref)
    copies[1].wait()
    for copy in copies[2:5]:
        copy.wait()
    expand_bias(table_ref, place_ref, flat_ref, up_ref, bias_ref)
    key_bias, _ = window_masks(mask_ref, False)
    _, _, qkv = project(x, halves(wq_ref[...]))
    weights, attended = attend(qkv, bias_ref[...], key_bias, None)
    saved = []

    def save(value, ref, to):
        ref[...] = value
        saved.append(pltpu.make_async_copy(ref, to, out_sems.at[len(saved)]))
        saved[-1].start()

    save(qkv, qkv_ref, qkv_hbm)
    save(weights, weights_ref, weights_hbm)
    save(attended, attended_ref, attended_hbm)
    for copy in copies[5:]:
        copy.wait()
    mid = x + dot3(halves(attended), halves(wp_ref[...]), NN)
    save(mid, mid_ref, mid_hbm)
    normed, _ = norm(mid)
    pre = dot3(halves(normed), halves(wu_ref[...]), NN)
    save(pre, pre_ref, pre_hbm)
    hidden = pre * half_cdf(pre)
    load_window(cot_ref, grid_ref, True)
    store_first(grid_ref, mid + dot3(halves(hidden), halves(wd_ref[...]), NT))
    for copy in saved:
        copy.wait()
    spread_pair(grid_ref, (own_ref, lev_ref, lat_ref, both_ref))


def gelu_slope(pre, cdf):
    return cdf + pre * jnp.exp(-0.5 * pre * pre) * ((2.0 * np.pi) ** (-0.5))


def mlp_backward(g, slope, normed, inv, wu, wd):
    dpre = dot3(halves(g), wd, NN) * slope
    dnormed = dot3(halves(dpre), wu, NT)
    return dpre, g + norm_back(dnormed, normed, inv)


def attention_backward(dmid, qkv, weights, wp):
    q, k, v = scaled_parts(qkv)
    dattended = dot3(halves(dmid), wp, NT)
    dhalves = halves(dattended)
    dstack = stack_heads(dhalves)
    dweights = head_products(dhalves, halves(v))
    inner = jnp.sum(dweights * weights, axis=-1, keepdims=True)
    dscores = weights * (dweights - inner)
    ds = halves(dscores)
    dq = head_sums(ds, halves(k)) * SCALE
    dk = dot3(ds, stack_heads(halves(q)), TN)
    dv = dot3(halves(weights), dstack, TN)
    return dscores, jnp.concatenate([dq, dk, dv], axis=1)


def pack_gradients(keep_ref, send_ref, wide_ref, dqkv, dproj, dup, ddown, flat_ref):
    core = lax.rem(lax.axis_index("lon"), 2)
    wide_ref[0, :, 0 : 3 * CH] = dqkv
    wide_ref[0, :, 3 * CH : 4 * CH] = dproj
    wide_ref[1] = dup
    for share in range(2 * NZ):
        rows = [
            ddown[share * 48 + m * SHARE : share * 48 + (m + 1) * SHARE] for m in range(HID // CH)
        ]
        wide_ref[2, share * SHARE : (share + 1) * SHARE, :] = jnp.concatenate(rows, axis=1)
    even = core == 0
    for z in range(NZ):
        for group in range(GROUPS):
            first = wide_ref[group, 2 * SHARE * z : 2 * SHARE * z + SHARE, :]
            second = wide_ref[group, 2 * SHARE * z + SHARE : 2 * SHARE * (z + 1), :]
            rows = slice((z * GROUPS + group) * SHARE, (z * GROUPS + group + 1) * SHARE)
            keep_ref[rows, :] = jnp.where(even, first, second)
            send_ref[rows, :] = jnp.where(even, second, first)
    for ref in (keep_ref, send_ref):
        ref[GROWS:BUF, :] = jnp.zeros((TROWS, HID), F32)
    for z in range(NZ):
        first = table_share(flat_ref, 2 * z)
        second = table_share(flat_ref, 2 * z + 1)
        rows = slice(GROWS + z // 3 * 8, GROWS + z // 3 * 8 + 8)
        lanes = slice(z % 3 * 256, z % 3 * 256 + 256)
        keep_ref[rows, lanes] = jnp.where(even, first, second)
        send_ref[rows, lanes] = jnp.where(even, second, first)


def table_share(flat_ref, share):
    start = share * TSHARE
    base = start // 128 * 128
    window = flat_ref[:, base : base + UPLANES]
    if start - base:
        window = pltpu.roll(window, UPLANES - (start - base), 1)
    return window[:, 0:256]


def second_pass(
    own_ref, lev_ref, lat_ref, both_ref, around_ref, wq0_ref, wq1_ref, wp0_ref, wp1_ref, wu0_ref,
    wu1_ref, wd0_ref, wd1_ref, bias_ref, key_ref, pair_ref,
    back_own_ref, back_lev_ref, back_lat_ref, back_both_ref, dscores_ref, normed_ref, attended_ref, hnormed_ref, hidden_ref,
    g_ref, dpre_ref, dmid_ref, dqkv_ref,
    grid_ref,
):
    gather_pair(grid_ref, (own_ref, lev_ref, lat_ref, both_ref), around_ref)
    x = load_first(grid_ref)
    g = load_second(grid_ref)
    wq, wp = (wq0_ref[...], wq1_ref[...]), (wp0_ref[...], wp1_ref[...])
    wu, wd = (wu0_ref[...], wu1_ref[...]), (wd0_ref[...], wd1_ref[...])
    key_bias, pair = key_ref[0:1], pair_ref[...]
    normed, inv, qkv = project(x, wq)
    weights, attended = attend(qkv, bias_ref[...], key_bias, pair)
    normed_ref[...] = normed
    attended_ref[...] = attended
    mid = x + dot3(halves(attended), wp, NN)
    hnormed, hinv = norm(mid)
    hnormed_ref[...] = hnormed
    pre = dot3(halves(hnormed), wu, NN)
    cdf = half_cdf(pre)
    hidden_ref[...] = pre * cdf
    g_ref[...] = g
    dpre, dmid = mlp_backward(g, gelu_slope(pre, cdf), hnormed, hinv, wu, wd)
    dpre_ref[...] = dpre
    dmid_ref[...] = dmid
    dscores, dqkv = attention_backward(dmid, qkv, weights, wp)
    dscores_ref[...] = dscores
    dqkv_ref[...] = dqkv
    dx = dmid + norm_back(dot3(halves(dqkv), wq, NT), normed, inv)
    store_first(grid_ref, dx)
    spread_one(grid_ref, (back_own_ref, back_lev_ref, back_lat_ref, back_both_ref))


def second_gradients(
    dscores_ref, normed_ref, attended_ref, hnormed_ref, hidden_ref, g_ref, dpre_ref, dmid_ref,
    dqkv_ref, place_ref,
    keep_ref, send_ref,
    flat_ref, up_ref, wide_ref,
):
    collect_table(dscores_ref, place_ref, up_ref, flat_ref)
    pack_gradients(
        keep_ref, send_ref, wide_ref,
        weight_gradient(normed_ref[...], dqkv_ref[...]),
        weight_gradient(attended_ref[...], dmid_ref[...]),
        weight_gradient(hnormed_ref[...], dpre_ref[...]),
        weight_gradient(hidden_ref[...], g_ref[...]),
        flat_ref,
    )


def first_backward(
    own_ref, lev_ref, lat_ref, both_ref, around_ref, wp0_ref, wp1_ref, wu0_ref, wu1_ref, wd0_ref,
    wd1_ref, slope_ref, hidden_ref, hnormed_ref, hinv_ref, normed_ref, qkv_ref, weights_ref,
    attended_ref, place_ref,
    dmid_ref, dqkv_ref, gkeep_ref, gsend_ref,
    grid_ref, flat_ref, up_ref, wide_ref, dscores_ref,
):
    gather_one(grid_ref, (own_ref, lev_ref, lat_ref, both_ref), around_ref)
    g = load_first(grid_ref)
    wp = (wp0_ref[...], wp1_ref[...])
    wu, wd = (wu0_ref[...], wu1_ref[...]), (wd0_ref[...], wd1_ref[...])
    hnormed = hnormed_ref[...]
    dpre, dmid = mlp_backward(g, slope_ref[...], hnormed, hinv_ref[...], wu, wd)
    dup = weight_gradient(hnormed, dpre)
    ddown = weight_gradient(hidden_ref[...], g)
    dproj = weight_gradient(attended_ref[...], dmid)
    dscores, dqkv = attention_backward(dmid, qkv_ref[...], weights_ref[...], wp)
    dscores_ref[...] = dscores
    dmid_ref[...] = dmid
    dqkv_ref[...] = dqkv
    collect_table(dscores_ref, place_ref, up_ref, flat_ref)
    pack_gradients(
        gkeep_ref, gsend_ref, wide_ref,
        weight_gradient(normed_ref[...], dqkv), dproj, dup, ddown, flat_ref,
    )


def first_prepare(
    x_ref, mid_ref, pre_ref,
    slope_ref, hidden_ref, hnormed_ref, hinv_ref, normed_ref,
    grid_ref,
):
    pre = pre_ref[...]
    cdf = half_cdf(pre)
    slope_ref[...] = gelu_slope(pre, cdf)
    hidden_ref[...] = pre * cdf
    hnormed_ref[...], hinv_ref[...] = norm(mid_ref[...])
    load_window(x_ref, grid_ref)
    normed_ref[...], _ = norm(load_first(grid_ref))


def input_gradient(x_ref, wq_ref, dmid_ref, dqkv_ref, grad_ref, grid_ref):
    load_window(x_ref, grid_ref)
    normed, inv = norm(load_first(grid_ref))
    dnormed = dot3(halves(dqkv_ref[...]), halves(wq_ref[...]), NT)
    store_first(grid_ref, dmid_ref[...] + norm_back(dnormed, normed, inv))
    save_window(grid_ref, grad_ref)


def split_weights(*refs):
    count = len(refs) // 3
    for i, ref in enumerate(refs[:count]):
        high_ref, low_ref = refs[count + 2 * i : count + 2 * i + 2]
        high_ref[...], low_ref[...] = halves(ref[...])


def second_prepare(
    mask_ref, table_ref, place_ref, bias_ref, key_ref, pair_ref, flat_ref, up_ref
):
    expand_bias(table_ref, place_ref, flat_ref, up_ref, bias_ref)
    key_bias, pair = window_masks(mask_ref, True)
    key_ref[...] = jnp.broadcast_to(key_bias, (8, TOK))
    pair_ref[...] = pair


def unit_parts(block):
    for tile in range(18):
        number = block * 18 + tile
        if number < 32:
            yield number // 2, number % 2 * SHARE, SHARE, tile, 0
        else:
            for quarter in range(4):
                yield (number - 32) * 4 + quarter, 2 * SHARE, SHARE // 4, tile, quarter * (SHARE // 4)


def table_place(z):
    return slice(GROWS + z // 3 * 8, GROWS + z // 3 * 8 + 8), slice(z % 3 * 256, z % 3 * 256 + 256)


def join(mine0_ref, theirs0_ref, mine1_ref, theirs1_ref, plane_ref, table_ref, sum_ref):
    for block, (mine_ref, theirs_ref) in enumerate(((mine0_ref, theirs0_ref), (mine1_ref, theirs1_ref))):
        sum_ref[...] = mine_ref[...] + theirs_ref[...]
        for z in range(NZ):
            for p, at, count, tile, start in unit_parts(block):
                start = (z * GROUPS + tile // 6) * SHARE + start
                lanes = slice(tile % 6 * 128, tile % 6 * 128 + 128)
                at = z * UNIT + at
                plane_ref[p, at : at + count, :] = sum_ref[start : start + count, lanes]
            table = sum_ref[table_place(z)]
            for half in range(2):
                to = block * TABLE_ROWS + half * HEADS
                table_ref[z, to : to + HEADS, :] = table[0:HEADS, half * 128 : half * 128 + 128]


def plane_sum(got_ref, table_ref, out_ref, sum_ref):
    total = got_ref[0]
    for p in range(1, PLANE):
        total = total + got_ref[p]
    sum_ref[...] = total
    used = UNIT + 2 * TABLE_ROWS
    for z in range(NZ):
        out_ref[z, 0:UNIT, :] = sum_ref[z * UNIT : (z + 1) * UNIT, :]
        out_ref[z, UNIT:used, :] = table_ref[z]
        out_ref[z, used:LON_ROWS, :] = jnp.zeros((LON_ROWS - used, 128), F32)


def lon_sum(got_ref, out_ref):
    total = got_ref[0, 0:32, :]
    for z in range(1, NZ):
        total = total + got_ref[z, 0:32, :]
    for p in range(PLANE):
        out_ref[p] = total


def table_sum(got_ref, table_ref, sum_ref):
    total = got_ref[0]
    for z in range(1, NZ):
        total = total + got_ref[z]
    sum_ref[...] = total
    for block in range(2):
        for h in range(HEADS):
            row = UNIT + block * TABLE_ROWS + h
            table_ref[block, 0, h, :, 0:128] = sum_ref[row : row + 1, :]
            row = row + HEADS
            table_ref[block, 0, h, :, 128:TSHARE] = sum_ref[row : row + 1, 0 : TSHARE - 128]


def unpack(scale, got_ref, qkv_ref, proj_ref, up_ref, down_ref, wide_ref):
    for block in range(2):
        for p, at, count, tile, to in unit_parts(block):
            lanes = slice(tile % 6 * 128, tile % 6 * 128 + 128)
            wide_ref[block, tile // 6, to : to + count, lanes] = got_ref[p, at : at + count, :] * scale
        for row in range(SHARE):
            at = slice(row, row + 1)
            qkv_ref[row, block : block + 1, :] = wide_ref[block, 0, at, 0 : 3 * CH]
            proj_ref[row, block : block + 1, :] = wide_ref[block, 0, at, 3 * CH : 4 * CH]
            up_ref[row, block : block + 1, :] = wide_ref[block, 1, at, :]
        for m in range(HID // CH):
            down_ref[block, m * SHARE : (m + 1) * SHARE, :] = wide_ref[
                block, 2, 0:SHARE, m * CH : (m + 1) * CH
            ]


WEIGHTS = ((CH, 3 * CH), (CH, CH), (CH, HID), (CH, HID))


def struct(*shape, dtype=F32):
    return jax.ShapeDtypeStruct(shape, dtype)


def vmem(*shape):
    return pltpu.VMEM(shape, F32)


def whole(*shape):
    return pl.BlockSpec(shape, lambda i: (0,) * len(shape))


def part_of(block, *shape):
    return pl.BlockSpec((None,) + shape, lambda i: (block,) + (0,) * len(shape))


def weight_specs(block):
    return [
        part_of(block, CH, 3 * CH),
        part_of(block, CH, CH),
        part_of(block, CH, HID),
        part_of(block, CH, HID),
    ]


def table_spec(block):
    return part_of(block, 1, HEADS, 1, POS)


def call(body, in_specs, outs, scratch, cost=0, mib=28, far=0):
    near = [whole(*o.shape) for o in outs[: len(outs) - far]]
    return pl.pallas_call(
        body,
        grid=(1,),
        in_specs=in_specs,
        out_specs=near + [HBM] * far,
        out_shape=outs,
        scratch_shapes=scratch,
        compiler_params=params(mib),
        cost_estimate=pl.CostEstimate(flops=cost, bytes_accessed=4 * 2**20, transcendentals=0),
    )


SMEM = pl.BlockSpec(memory_space=pltpu.SMEM)
HBM = pl.BlockSpec(memory_space=pltpu.HBM)
FLAT = 3456


def shifted(block, axis, distance):
    devices = range(lax.axis_size(axis))
    route = [((i - distance) % len(devices), i) for i in devices]
    return lax.ppermute(block, axis, route)


def shifted_plane(block, levels, rows):
    size = lax.axis_size("lev")
    count = lax.axis_size("lat")
    route = [
        (lat * size + lev, (lat + rows) % count * size + (lev + levels) % size)
        for lat in range(count)
        for lev in range(size)
    ]
    return lax.ppermute(block, ("lat", "lev"), route)


def exchange(pieces, step, side, first=None):
    held = [pieces[0]] + [
        shifted_plane(piece, step * dlev, step * dlat)
        for piece, (dlev, dlat) in zip(pieces[1:], MOVES[1:])
    ]
    edge = jnp.stack([piece[side] for piece in held])
    if first is not None:
        edge, first = lax.optimization_barrier((edge, first))
    return held + [shifted(edge, "lon", step)], first


def swap_cores(v):
    return lax.ppermute(v, "lon", [(i, i ^ 1) for i in range(lax.axis_size("lon"))])


def local(inputs, cotangent, qkv_weight, proj_weight, up_weight, down_weight, bias_table, lat_mask):
    place = place_matrix()
    x = inputs.transpose(1, 2, 0, 3)
    cot = cotangent.transpose(1, 2, 0, 3)
    table = bias_table.transpose(0, 1, 3, 2, 4)
    weights = (qkv_weight, proj_weight, up_weight, down_weight.transpose(0, 2, 1))
    grid_spec = whole(ROWS, COLS, LEVS, CH)
    wide_scratch = [vmem(8, FLAT), vmem(8 * CELLS, UPLANES)]
    half = (2, WIDE, 128)
    *pieces, qkv, attention, attended, mid, pre = call(
        first_forward,
        [HBM] * 9,
        [struct(*half)] * 4
        + [
            struct(TOK, 3 * CH),
            struct(STACK, TOK),
            struct(TOK, CH),
            struct(TOK, CH),
            struct(TOK, HID),
        ],
        [
            pltpu.SMEM((8 * ROWS,), jnp.int32),
            vmem(ROWS, COLS, LEVS, CH),
            vmem(ROWS, COLS, LEVS, CH),
            vmem(CH, 3 * CH),
            vmem(CH, CH),
            vmem(CH, HID),
            vmem(CH, HID),
            vmem(1, HEADS, 1, POS),
            pltpu.VMEM((UPLANES, UPLANES), BF16),
            vmem(3, TOK, 128),
        ]
        + wide_scratch
        + [
            vmem(STACK, TOK),
            vmem(TOK, 3 * CH),
            vmem(STACK, TOK),
            vmem(TOK, CH),
            vmem(TOK, CH),
            vmem(TOK, HID),
            pltpu.SemaphoreType.DMA((9,)),
            pltpu.SemaphoreType.DMA((5,)),
        ],
        cost=500_000_000,
        mib=60,
        far=5,
    )(lat_mask, x, cot, *weights, table, place)
    prepared = call(
        second_prepare,
        [SMEM, table_spec(1), whole(UPLANES, UPLANES)],
        [struct(STACK, TOK), struct(8, TOK), struct(TOK, TOK)],
        wide_scratch,
        cost=200_000_000,
    )(lat_mask, table, place)
    split = call(
        split_weights,
        weight_specs(1),
        [struct(*shape, dtype=BF16) for shape in WEIGHTS for _ in range(2)],
        [],
        cost=200_000_000,
    )(*weights)
    first_split = call(
        split_weights,
        weight_specs(0)[1:],
        [struct(*shape, dtype=BF16) for shape in WEIGHTS[1:] for _ in range(2)],
        [],
        cost=200_000_000,
    )(*weights[1:])
    first_split = list(first_split)
    held, prepared = exchange(pieces, -1, 0, prepared)
    around = (4, WIDE, 128)
    back_half = (2, THIN, 128)
    held[-1], first_split[0] = lax.optimization_barrier((held[-1], first_split[0]))
    back_around = (4, THIN, 128)
    factors = [
        struct(STACK, TOK),
        struct(TOK, CH),
        struct(TOK, CH),
        struct(TOK, CH),
        struct(TOK, HID),
        struct(TOK, CH),
        struct(TOK, HID),
        struct(TOK, CH),
        struct(TOK, 3 * CH),
    ]
    second = call(
        second_pass,
        [whole(*half)] * 4
        + [whole(*around)]
        + [whole(*shape) for shape in WEIGHTS for _ in range(2)]
        + [whole(STACK, TOK), whole(8, TOK), whole(TOK, TOK)],
        [struct(*back_half)] * 4 + factors,
        [vmem(3, TOK, 128)],
        cost=1_000_000_000,
    )(*held, *split, *prepared)
    back_pieces, saved = second[:4], second[4:]
    keep2, send2 = call(
        second_gradients,
        [whole(*f.shape) for f in factors] + [whole(UPLANES, UPLANES)],
        [struct(BUF, HID), struct(BUF, HID)],
        wide_scratch + [vmem(GROUPS, CH, HID)],
        cost=500_000_000,
    )(*saved, place)
    back_held, send2 = exchange(back_pieces, 1, 1, send2)
    pre, _ = lax.optimization_barrier((pre, back_pieces[0]))
    ready = [
        struct(TOK, HID),
        struct(TOK, HID),
        struct(TOK, CH),
        struct(TOK, 1),
        struct(TOK, CH),
    ]
    first_ready = call(
        first_prepare,
        [grid_spec, whole(TOK, CH), whole(TOK, HID)],
        ready,
        [vmem(3, TOK, 128)],
        cost=200_000_000,
    )(x, mid, pre)
    send2, slope = lax.optimization_barrier((send2, first_ready[0]))
    first_ready = [slope] + list(first_ready[1:])
    got2 = swap_cores(send2)
    dmid, dqkv, keep1, send1 = call(
        first_backward,
        [whole(*back_half)] * 4
        + [whole(*back_around)]
        + [whole(*shape) for shape in WEIGHTS[1:] for _ in range(2)]
        + [whole(*r.shape) for r in ready]
        + [
            whole(TOK, 3 * CH),
            whole(STACK, TOK),
            whole(TOK, CH),
            whole(UPLANES, UPLANES),
        ],
        [struct(TOK, CH), struct(TOK, 3 * CH), struct(BUF, HID), struct(BUF, HID)],
        [vmem(3, TOK, 128)] + wide_scratch + [vmem(GROUPS, CH, HID), vmem(STACK, TOK)],
        cost=1_000_000_000,
    )(
        *back_held, *first_split, *first_ready, qkv, attention, attended, place,
    )
    (grad_input,) = call(
        input_gradient,
        [grid_spec, weight_specs(0)[0], whole(TOK, CH), whole(TOK, 3 * CH)],
        [struct(ROWS, COLS, LEVS, CH)],
        [vmem(3, TOK, 128)],
        cost=100_000_000,
    )(x, weights[0], dmid, dqkv)
    got1 = swap_cores(send1)
    keep1, grad_input = lax.optimization_barrier((keep1, grad_input))
    for_plane, table_part = call(
        join,
        [whole(BUF, HID)] * 4,
        [struct(PLANE, NZ * UNIT, 128), struct(NZ, 2 * TABLE_ROWS, 128)],
        [vmem(BUF, HID)],
    )(keep1, got1, keep2, got2)
    plane_got = lax.all_to_all(for_plane, ("lat", "lev"), 0, 0, tiled=True)
    (for_lon,) = call(
        plane_sum,
        [whole(PLANE, NZ * UNIT, 128), whole(NZ, 2 * TABLE_ROWS, 128)],
        [struct(NZ, LON_ROWS, 128)],
        [vmem(NZ * UNIT, 128)],
    )(plane_got, table_part)
    core_groups = [[z * 2 + c for z in range(NZ)] for c in range(2)]
    lon_got = lax.all_to_all(
        for_lon, "lon", 0, 0, axis_index_groups=core_groups, tiled=True
    )
    (copies,) = call(lon_sum, [whole(NZ, LON_ROWS, 128)], [struct(PLANE, 32, 128)], [])(lon_got)
    (grad_table,) = call(
        table_sum,
        [whole(NZ, LON_ROWS, 128)],
        [struct(2, 1, HEADS, 1, TSHARE)],
        [vmem(LON_ROWS, 128)],
    )(lon_got)
    shares = lax.all_to_all(copies, ("lat", "lev"), 0, 0, tiled=True)
    tokens = TOK * lax.axis_size("lon") * lax.axis_size("lat") * lax.axis_size("lev")
    grad_qkv, grad_proj, grad_up, grad_down = call(
        lambda *refs: unpack(float(tokens) ** (-0.5), *refs),
        [whole(PLANE, 32, 128)],
        [
            struct(SHARE, 2, 3 * CH),
            struct(SHARE, 2, CH),
            struct(SHARE, 2, HID),
            struct(2, 48, CH),
        ],
        [vmem(2, GROUPS, 16, HID)],
    )(shares)
    return (
        grad_input.transpose(2, 0, 1, 3),
        grad_qkv.transpose(1, 0, 2),
        grad_proj.transpose(1, 0, 2),
        grad_up.transpose(1, 0, 2),
        grad_down,
        grad_table.transpose(0, 1, 3, 2, 4),
    )


def solution(mesh):
    in_specs = (
        P("lev", "lat", "lon", None),
        P("lev", "lat", "lon", None),
        P(),
        P(),
        P(),
        P(),
        P(None, "lev", "lat", None, None),
        P(),
    )
    out_specs = (
        P("lev", "lat", "lon", None),
        P(None, "lon", None),
        P(None, "lon", None),
        P(None, "lon", None),
        P(None, "lon", None),
        P(None, "lev", "lat", None, "lon"),
    )
    return jax.shard_map(local, mesh=mesh, in_specs=in_specs, out_specs=out_specs, check_vma=False)
```
